32 devices in a mesh: wave: 8 (over z, y), lev: 4 (over x, core).
Axes of the slice: x: 2, y: 2, z: 4, core: 2. Of those that a mesh axis runs over, the one named last changes fastest.
Arguments:
- control: bfloat16 [32, 1281, 512], P(('wave', 'lev')), may hold values from -6 to 6
- covariance: float32 [1280, 128, 128], P(('wave', 'lev')), may hold values from -0.5 to 0.5
- legendre: bfloat16 [32, 1281, 2560], P(('wave', 'lev')), may hold values from -0.25 to 0.25
- pair_order: int32 [32], P(('wave', 'lev')), may hold values from 0 to 639, as said below
- band_rows: int32 [8], replicated, may hold values from 1 to 400, 2560 in all
Outputs:
- fourier: bfloat16 [64, 3200, 512], P(None, 'wave', 'lev')
The draws below stay inside these ranges and needn't reach their ends.
Inputs may be any that keep to these rules, and one draw needn't show every extreme that they name: `pair_order`: the pair holds zonal wavenumbers m and 1279 - m; values may repeat. `band_rows`: band sizes sum to 2560; bands follow one another from latitude 0.
All inputs are finite; a program needn't handle non-finite values.
Results may differ from the reference program's by a relative error of at most 0.0049.
Values may be sent and summed in bfloat16 or wider, within the bound.
No kernel may reach another device: no remote copies, remote signals or barrier semaphores. Data moves between devices by JAX's collectives and lax.ppermute only.
A program may use at most 128 MiB of HBM per device.

```python
import math
import jax
import jax.numpy as jnp
import numpy as np
from jax import lax

NT = 1280
LEV = 128
NLAT = 2560
SLOTS = 1281
PAIRS = 32
BAND_MOST = 400
N_WAVE = 8


def draw_pair_order(key, part):
    key = jax.random.fold_in(key, 7)
    key_values, key_first, key_step = jax.random.split(key, 3)
    values = jax.random.randint(key_values, (PAIRS,), 0, NT // 2)
    first_pos = jax.random.randint(key_first, (), 0, PAIRS)
    step_pos = jax.random.randint(key_step, (), 1, PAIRS)
    other_pos = (first_pos + step_pos) % PAIRS
    values = values.at[first_pos].set(0)
    values = values.at[other_pos].set(NT // 2 - 1)
    return values.astype(jnp.int32)


def levels(stream_key, shape, shards, least, top_value):
    gain = 1.0
    for axis_at, parts in shards:
        steps = jax.random.uniform(jax.random.fold_in(jax.random.fold_in(stream_key, 6), axis_at), (parts,), jnp.float32, least / len(shards), top_value / len(shards))
        gain = gain * jnp.repeat(jnp.exp(steps), shape[axis_at] // parts).reshape((-1,) + (1,) * (len(shape) - 1 - axis_at))
    return gain


def profile(number_of, total, limit, slope):
    portions = [(1 << 20) // math.isqrt(standing ** slope) + 1 for standing in range(2, number_of + 1)]
    surplus, holding = total - limit - (number_of - 1), [1] * (number_of - 1)
    while surplus > 0:
        candidates = [i for i in range(number_of - 1) if holding[i] < limit]
        pool, left = sum([portions[i] for i in candidates]), surplus
        for i in candidates:
            addition = min(limit - holding[i], max(1, left * portions[i] // pool), surplus)
            holding[i] = holding[i] + addition
            surplus = surplus - addition
    return np.array([limit] + holding)


def ragged(own_key, count, total, bound, skew):
    if count == 2:
        one = jax.random.randint(own_key, (), max(1, total - bound), min(bound, total - 1) + 1)
        return jnp.stack([one, total - one])
    lengths = jnp.asarray(profile(count, total, bound, skew), jnp.int32)
    pairs = (count - 1) // 2
    giver, sink = lengths[1:1 + 2 * pairs:2], lengths[2:2 + 2 * pairs:2]
    slack = jnp.minimum(giver - 1, bound - sink)
    passed = jax.random.randint(jax.random.fold_in(own_key, 1), (pairs,), 0, 1 << 20) % (slack + 1)
    lengths = lengths.at[1:1 + 2 * pairs:2].set(giver - passed).at[2:2 + 2 * pairs:2].set(sink + passed)
    return lengths[jax.random.permutation(jax.random.fold_in(own_key, 2), count)]


def centred(stream_key, dims, scale, bound, pieces=(), held_as=jnp.bfloat16):
    values = scale * jax.random.normal(stream_key, dims, jnp.float32)
    if pieces:
        values = values * levels(stream_key, dims, pieces, -0.22, 0.18)
    return jnp.clip(values, -bound, bound).astype(held_as)


def setup_inputs(seed: int = 0) -> dict:
    keys = jax.random.split(jax.random.key(seed), 6)
    control = centred(keys[0], (PAIRS, SLOTS, 4 * LEV), 1.0, 6.0, ((0, 32),))
    covariance = centred(keys[1], (NT, LEV, LEV), LEV ** -0.5, 0.5, ((0, 32),), jnp.float32)
    legendre = centred(keys[2], (PAIRS, SLOTS, NLAT), (SLOTS // 2) ** -0.5, 0.25, ((0, 32),))
    pair_order = draw_pair_order(jax.random.fold_in(keys[5], 71), 0)
    band_rows = ragged(keys[4], N_WAVE, NLAT, BAND_MOST, 2).astype(jnp.int32)
    return dict(control=control, covariance=covariance, legendre=legendre, pair_order=pair_order, band_rows=band_rows)


def reference(control, covariance, legendre, pair_order, band_rows):
    starts = jnp.cumsum(band_rows) - band_rows
    offsets = jnp.arange(BAND_MOST, dtype=jnp.int32)
    latitude_rows = (starts[:, None] + offsets[None, :]).reshape(-1)
    latitude_rows = jnp.minimum(latitude_rows, NLAT - 1).astype(jnp.int32)
    inside = (offsets[None, :] < band_rows[:, None]).reshape(-1)
    slot_index = jnp.arange(SLOTS, dtype=jnp.int32)

    def one_pair(index):
        coeffs = control[index]
        table = legendre[index]
        lowest = pair_order[index]
        leading = slot_index < NT - lowest
        degree = jnp.where(leading, lowest + slot_index, slot_index - 1).astype(jnp.int32)
        chosen = covariance[degree].astype(jnp.float32)
        columns = coeffs.astype(jnp.float32).reshape(SLOTS, 4, LEV)
        filtered = jnp.einsum("sij,scj->sci", chosen, columns, precision=lax.Precision.HIGHEST)
        filtered = filtered.astype(jnp.bfloat16).reshape(SLOTS, 4 * LEV)
        blank = jnp.zeros_like(filtered)
        upper_seg = jnp.where(leading[:, None], filtered, blank)
        lower_seg = jnp.where(leading[:, None], blank, filtered)
        grid_upper = jnp.dot(table.T, upper_seg, preferred_element_type=jnp.float32)
        grid_lower = jnp.dot(table.T, lower_seg, preferred_element_type=jnp.float32)
        gridded = jnp.stack([grid_upper, grid_lower], axis=0).astype(jnp.bfloat16)
        picked = jnp.take(gridded, latitude_rows, axis=1)
        return jnp.where(inside[None, :, None], picked, jnp.zeros_like(picked))

    def place(index, fourier):
        piece = one_pair(index)
        return lax.dynamic_update_slice(fourier, piece, ((2 * index).astype(jnp.int32), jnp.int32(0), jnp.int32(0)))

    fourier = jnp.zeros((2 * PAIRS, N_WAVE * BAND_MOST, 4 * LEV), jnp.bfloat16)
    return lax.fori_loop(0, PAIRS, place, fourier)
```

```python
import functools

import jax
import jax.numpy as jnp
import numpy as np
from jax import lax
from jax.experimental import pallas as pl
from jax.experimental.pallas import tpu as pltpu
from jax.sharding import PartitionSpec as P

BF = jnp.bfloat16
F32 = jnp.float32
VMEM_LIMIT = 56 * 1024 * 1024
SUB = 16


def ceil_to(value, step):
    return (value + step - 1) // step * step


class Plan:
    def __init__(self, devices, degrees):
        self.devices = devices
        self.group = devices // 2
        self.degrees = degrees
        self.block = degrees // devices
        self.chunks = []
        row, fold = 0, 0
        for count in self.fold_counts(self.block):
            self.chunks.append((row, fold, count))
            row += ceil_to(2 * count, SUB)
            fold += count
        self.rows = row

    @staticmethod
    def fold_counts(block):
        return (block,)

    def row_tables(self):
        fold = np.zeros(self.rows, np.int32)
        folded = np.zeros(self.rows, bool)
        used = np.zeros(self.rows, bool)
        for row, first, count in self.chunks:
            index = np.arange(count)
            fold[row:row + count] = first + index
            folded[row:row + count] = True
            fold[row + count:row + 2 * count] = first + index
            used[row:row + 2 * count] = True
        return fold, folded, used


def pack_kernel(plan, levels, info_ref, slot_ref, control_ref, out_ref):
    slots = control_ref.shape[0]
    messages = out_ref.shape[0]
    even = slots - 1
    rows = messages * plan.rows
    slot = slot_ref[...]
    pick = (slot == lax.broadcasted_iota(jnp.int32, (rows, even), 1)).astype(F32).astype(BF)
    got = jnp.dot(pick, control_ref[:even, :], preferred_element_type=F32)
    last = control_ref[even:slots, :].astype(F32)
    got = jnp.where(slot == even, last, got).astype(BF)
    extra_slot = plan.degrees - info_ref[0]
    lane = lax.broadcasted_iota(jnp.int32, (SUB, even), 1)
    first = lax.broadcasted_iota(jnp.int32, (SUB, even), 0) == 0
    choose = jnp.where(first & (lane == extra_slot), 1.0, 0.0).astype(BF)
    extra = jnp.dot(choose, control_ref[:even, :], preferred_element_type=F32)
    extra = jnp.where(extra_slot == even, last, extra)
    place = lax.broadcasted_iota(jnp.int32, (SUB, levels), 0)
    tail = jnp.zeros((SUB, levels), F32)
    for c in range(4):
        tail = jnp.where(place == c, extra[0:1, c * levels:(c + 1) * levels], tail)
    tail = tail.astype(BF)
    for k in range(messages):
        for c in range(4):
            out_ref[k, c * plan.rows:(c + 1) * plan.rows, :] = got[
                k * plan.rows:(k + 1) * plan.rows, c * levels:(c + 1) * levels
            ]
        out_ref[k, 4 * plan.rows:, :] = tail


def pack(plan, control, lowest, slots_of_rows):
    slots, columns = control.shape
    levels = columns // 4
    height = 4 * plan.rows + SUB
    per_step = max(1, min(plan.group, 320 // plan.rows))
    return pl.pallas_call(
        functools.partial(pack_kernel, plan, levels),
        grid=(plan.group // per_step,),
        out_shape=jax.ShapeDtypeStruct((plan.group, height, levels), BF),
        in_specs=[
            pl.BlockSpec(memory_space=pltpu.SMEM),
            pl.BlockSpec((per_step * plan.rows, 1), lambda k: (k, 0)),
            pl.BlockSpec((slots, columns), lambda k: (0, 0)),
        ],
        out_specs=pl.BlockSpec((per_step, height, levels), lambda k: (k, 0, 0)),
        compiler_params=pltpu.CompilerParams(vmem_limit_bytes=VMEM_LIMIT),
        cost_estimate=pl.CostEstimate(
            flops=2 * plan.group * plan.rows * slots * columns,
            bytes_accessed=slots * columns * 2 + plan.group * height * levels * 2,
            transcendentals=0,
        ),
        name="pack_rows",
    )(lowest, slots_of_rows, control)


def swap_matrix():
    i = lax.broadcasted_iota(jnp.int32, (SUB * SUB, SUB * SUB), 0)
    j = lax.broadcasted_iota(jnp.int32, (SUB * SUB, SUB * SUB), 1)
    return jnp.where((i // SUB == j % SUB) & (i % SUB == j // SUB), 1.0, 0.0).astype(BF)


def filter_kernel(plan, chunk, with_extra, levels, info_ref, lowest_ref, low_ref, rows_ref, own_ref, other_ref, out_ref, x_ref, y_ref):
    row0, fold0, count = chunk
    height = ceil_to(2 * count, SUB)
    is_high = info_ref[0] == 1
    first_fold = info_ref[1]
    block = plan.block
    swap = swap_matrix()

    def low_matrix(fold):
        return jnp.where(is_high, other_ref[fold], own_ref[fold])

    def high_matrix(fold):
        return jnp.where(is_high, own_ref[block - 1 - fold], other_ref[block - 1 - fold])

    def times(rows, matrix):
        return lax.dot_general(rows, matrix, (((1,), (1,)), ((), ())), preferred_element_type=F32)

    for g in range(plan.group // SUB):
        sources = range(g * SUB, (g + 1) * SUB)
        for r in range(0, height, SUB):
            parts = []
            for c in range(4):
                at = c * plan.rows + row0 + r
                parts.append(
                    rows_ref[g * SUB:(g + 1) * SUB, at:at + SUB, :].reshape(SUB * SUB, levels)
                )
            block_rows = jnp.concatenate(parts, axis=1)
            x_ref[r * SUB:(r + SUB) * SUB, :] = jnp.dot(
                swap, block_rows, preferred_element_type=F32
            ).astype(BF)
        low = low_ref[g * SUB:(g + 1) * SUB, :]
        low = jnp.concatenate([low] * 4, axis=0)
        for i in range(count):
            def stack(row):
                return jnp.concatenate(
                    [x_ref[row * SUB:(row + 1) * SUB, c * levels:(c + 1) * levels] for c in range(4)], axis=0
                )

            folded, high = stack(i), stack(count + i)
            from_low = times(folded, low_matrix(fold0 + i))
            from_high = times(jnp.concatenate([folded, high], axis=0), high_matrix(fold0 + i))
            mixed = jnp.where(low <= first_fold + fold0 + i, from_low, from_high[:4 * SUB])
            for row, value in ((i, mixed), (count + i, from_high[4 * SUB:])):
                value = value.astype(BF)
                for c in range(4):
                    y_ref[row * SUB:(row + 1) * SUB, c * levels:(c + 1) * levels] = value[c * SUB:(c + 1) * SUB]
        if height > 2 * count:
            y_ref[2 * count * SUB:height * SUB, :] = jnp.zeros(((height - 2 * count) * SUB, 4 * levels), BF)
        for r in range(0, height, SUB):
            back = jnp.dot(swap, y_ref[r * SUB:(r + SUB) * SUB, :], preferred_element_type=F32).astype(BF)
            for c in range(4):
                at = c * height + r
                out_ref[g * SUB:(g + 1) * SUB, at:at + SUB, :] = back[:, c * levels:(c + 1) * levels].reshape(
                    SUB, SUB, levels
                )
        if with_extra:
            for s in sources:
                fold = jnp.clip(lowest_ref[info_ref[2] + s] - first_fold, 0, block - 1)
                value = times(rows_ref[s, 4 * plan.rows:4 * plan.rows + SUB, :], high_matrix(fold))
                out_ref[s, 4 * height:4 * height + SUB, :] = value.astype(BF)


def filter_rows(plan, chunk, with_extra, info, lowest_all, low_rows, received, own, other):
    levels = received.shape[2]
    height = ceil_to(2 * chunk[2], SUB)
    out_height = 4 * height + (SUB if with_extra else 0)
    smem = pl.BlockSpec(memory_space=pltpu.SMEM)
    vmem = pl.BlockSpec(memory_space=pltpu.VMEM)
    return pl.pallas_call(
        functools.partial(filter_kernel, plan, chunk, with_extra, levels),
        out_shape=jax.ShapeDtypeStruct((plan.group, out_height, levels), BF),
        in_specs=[smem, smem, vmem, vmem, vmem, vmem],
        out_specs=vmem,
        scratch_shapes=[
            pltpu.VMEM((height * SUB, 4 * levels), BF),
            pltpu.VMEM((height * SUB, 4 * levels), BF),
        ],
        compiler_params=pltpu.CompilerParams(vmem_limit_bytes=VMEM_LIMIT),
        cost_estimate=pl.CostEstimate(
            flops=2 * plan.group * 12 * chunk[2] * levels * levels * 4,
            bytes_accessed=plan.group * out_height * levels * 4 + 4 * chunk[2] * levels * levels,
            transcendentals=0,
        ),
        name="filter_rows",
    )(info, lowest_all, low_rows, received, own, other)


def grid_kernel(plan, levels, latitudes, depth, level_cols, info_ref, starts_ref, bands_ref, *refs):
    count = len(plan.chunks)
    parts = refs[:count]
    table_ref, out_ref, rows_ref, grid_ref = refs[count:]
    half, step = pl.program_id(0), pl.program_id(1)
    tile = table_ref.shape[1]

    @pl.when((half == 0) & (step == 0))
    def _():
        for k in range(plan.group):
            for c in range(4):
                for (row, _, folds), part in zip(plan.chunks, parts):
                    height = ceil_to(2 * folds, SUB)
                    at = k * plan.rows + row
                    rows_ref[at:at + height, c * levels:(c + 1) * levels] = part[k, c * height:(c + 1) * height, :]

    @pl.when((half == 1) & (step == 0))
    def _():
        height = ceil_to(2 * plan.chunks[-1][2], SUB)
        extra = parts[-1][info_ref[0], 4 * height:4 * height + SUB, :]
        base = info_ref[1] // SUB * SUB
        at = pl.ds(pl.multiple_of(base, SUB), SUB)
        here = lax.broadcasted_iota(jnp.int32, (SUB, levels), 0) == info_ref[1] - base
        for c in range(4):
            cols = slice(c * levels, (c + 1) * levels)
            held = rows_ref[at, cols].astype(F32)
            rows_ref[at, cols] = jnp.where(here, extra[c:c + 1, :].astype(F32), held).astype(BF)

    @pl.when((half == 0) & (step == 0))
    def _():
        grid_ref[latitudes:, :] = jnp.zeros((grid_ref.shape[0] - latitudes, 4 * levels), BF)

    grid_ref[pl.ds(pl.multiple_of(step * tile, tile), tile), :] = jnp.dot(
        table_ref[0], rows_ref[...], preferred_element_type=F32
    ).astype(BF)

    @pl.when(step == pl.num_programs(1) - 1)
    def _():
        waves = bands_ref.shape[0]
        groups = 4 * levels // level_cols
        piece = 80 if depth % 80 == 0 else depth
        window = ceil_to(piece + SUB - 1, SUB)
        i = lax.broadcasted_iota(jnp.int32, (piece, window), 0)
        j = lax.broadcasted_iota(jnp.int32, (piece, window), 1)
        for w in range(waves):
            start = starts_ref[w]
            base = start // SUB * SUB
            moved = j - i == start - base
            for r in range(0, depth, piece):
                pick = jnp.where(moved & (i < bands_ref[w] - r), 1.0, 0.0).astype(BF)
                held = grid_ref[pl.ds(pl.multiple_of(base + r, SUB), window), :]
                got = jnp.dot(pick, held, preferred_element_type=F32).astype(BF)
                for g in range(groups):
                    out_ref[w * groups + g, 0, r:r + piece, :] = got[:, g * level_cols:(g + 1) * level_cols]


def to_bands(plan, info, starts, bands, parts, table, depth, level_cols):
    halves, latitudes, width = table.shape
    levels = parts[0].shape[2]
    columns = 4 * levels
    waves = bands.shape[0]
    tile = 512
    smem = pl.BlockSpec(memory_space=pltpu.SMEM)
    messages = waves * columns // level_cols
    return pl.pallas_call(
        functools.partial(grid_kernel, plan, levels, latitudes, depth, level_cols),
        grid=(halves, latitudes // tile),
        out_shape=jax.ShapeDtypeStruct((messages, halves, depth, level_cols), BF),
        in_specs=[smem, smem, smem]
        + [pl.BlockSpec(part.shape, lambda h, t: (0, 0, 0)) for part in parts]
        + [pl.BlockSpec((1, tile, width), lambda h, t: (h, t, 0))],
        out_specs=pl.BlockSpec((messages, 1, depth, level_cols), lambda h, t: (0, h, 0, 0)),
        scratch_shapes=[
            pltpu.VMEM((width, columns), BF),
            pltpu.VMEM((ceil_to(latitudes + depth, SUB) + SUB, columns), BF),
        ],
        compiler_params=pltpu.CompilerParams(vmem_limit_bytes=VMEM_LIMIT),
        cost_estimate=pl.CostEstimate(
            flops=2 * halves * latitudes * width * columns,
            bytes_accessed=2 * halves * latitudes * width + 2 * messages * halves * depth * level_cols,
            transcendentals=0,
        ),
        name="grid_bands",
    )(info, starts, bands, *parts, table)


def per_device(control, covariance, legendre, pair_order, band_rows):
    axes = ("wave", "lev")
    waves, lev_count = lax.axis_size("wave"), lax.axis_size("lev")
    _, slots, columns = control.shape
    degrees, levels = slots - 1, columns // 4
    latitudes = legendre.shape[2]
    depth = 5 * latitudes // (4 * waves)
    level_cols = columns // lev_count
    plan = Plan(waves * lev_count, degrees)
    group, block = plan.group, plan.block
    me = lax.axis_index("wave") * lev_count + lax.axis_index("lev")
    is_high = (me >= group).astype(jnp.int32)
    rank = me - group * is_high
    mine = jnp.where(is_high == 1, group - 1 - rank, rank)
    lowest = pair_order[0]
    halves = [list(range(group)), list(range(group, 2 * group))]

    own = covariance.astype(BF)
    other = lax.ppermute(own, axes, [(d, 2 * group - 1 - d) for d in range(2 * group)])
    lowest_all = lax.all_gather(pair_order, axes, tiled=True)

    fold, folded, used = plan.row_tables()
    message = jnp.arange(group, dtype=jnp.int32)
    message = jnp.where(is_high == 1, group - 1 - message, message)
    degree = (message[:, None] * block + fold[None, :]).reshape(-1)
    folded = jnp.asarray(np.tile(folded, group))
    used = jnp.asarray(np.tile(used, group))
    upper = jnp.where(folded, degree - lowest, degrees - 1 - degree - lowest)
    upper = jnp.where(used & (upper >= 0), upper, -1)
    lower = jnp.where(used & folded, degrees - degree, -1)
    sent = jnp.where(used & folded & (degree < lowest), lower, upper)
    lower = jnp.where(degree <= lowest, lower, -1)

    packed = pack(plan, control[0], pair_order, sent[:, None])
    received = lax.all_to_all(packed, axes, split_axis=0, concat_axis=0, tiled=True, axis_index_groups=halves)

    slot_index = jnp.arange(slots, dtype=jnp.int32)[:, None]
    pick = jnp.stack([upper, lower])[:, None, :] == slot_index[None]
    table = jnp.einsum("sl,hsr->hlr", legendre[0], pick.astype(BF), preferred_element_type=F32).astype(BF)

    info = jnp.stack([is_high, mine * block, is_high * group])
    low_group = lax.dynamic_slice_in_dim(lowest_all, is_high * group, group, 0)
    low_rows = jnp.broadcast_to(low_group[:, None], (group, levels))
    parts = []
    for at, chunk in enumerate(plan.chunks):
        result = filter_rows(
            plan, chunk, at == len(plan.chunks) - 1, info, lowest_all, low_rows, received, own, other
        )
        parts.append(
            lax.all_to_all(result, axes, split_axis=0, concat_axis=0, tiled=True, axis_index_groups=halves)
        )

    extra_block = lowest // block
    extra_message = jnp.where(is_high == 1, group - 1 - extra_block, extra_block)
    extra_fold = lowest - extra_block * block
    extra_row = jnp.int32(0)
    for row, first, count in plan.chunks:
        extra_row = jnp.where(extra_fold >= first, row + extra_fold - first, extra_row)
    where = jnp.stack([extra_message, extra_message * plan.rows + extra_row])
    starts = jnp.cumsum(band_rows) - band_rows
    outgoing = to_bands(plan, where, starts, band_rows, parts, table, depth, level_cols)
    outgoing = outgoing.reshape(-1, depth, level_cols)
    return lax.all_to_all(outgoing, axes, split_axis=0, concat_axis=0, tiled=True)


def solution(mesh):
    return jax.shard_map(
        per_device,
        mesh=mesh,
        in_specs=(
            P(("wave", "lev"), None, None),
            P(("wave", "lev"), None, None),
            P(("wave", "lev"), None, None),
            P(("wave", "lev")),
            P(),
        ),
        out_specs=P(None, "wave", "lev"),
        check_vma=False,
    )
```

```python
import functools

import jax
import jax.numpy as jnp
import numpy as np
from jax import lax
from jax.experimental import pallas as pl
from jax.experimental.pallas import tpu as pltpu
from jax.sharding import PartitionSpec as P

BF = jnp.bfloat16
F32 = jnp.float32
VMEM_LIMIT = 56 * 1024 * 1024
SUB = 16
DIGIT = 16


def ceil_to(value, step):
    return (value + step - 1) // step * step


class Plan:
    def __init__(self, devices, degrees):
        self.devices = devices
        self.group = devices // 2
        self.degrees = degrees
        self.block = degrees // devices
        self.chunks = []
        row, fold = 0, 0
        for count in self.fold_counts(self.block):
            self.chunks.append((row, fold, count))
            row += ceil_to(2 * count, SUB)
            fold += count
        self.rows = row
        whole = [(at, n) for at, (_, _, n) in enumerate(self.chunks) if n % SUB == 0]
        mixed = [(at, n) for at, (_, _, n) in enumerate(self.chunks) if n % SUB]
        lower = [(at, 0, n) for at, n in whole] + [(at, 0, ceil_to(2 * n, SUB)) for at, n in mixed]
        self.segments = lower + [(at, n, n) for at, n in whole]
        self.widths = [
            self.group * sum(n for _, _, n in self.segments),
            self.group * sum(n for _, _, n in lower),
        ]

    @staticmethod
    def fold_counts(block):
        return (block - 8, 8) if block % SUB == 8 and block > 8 else (block,)

    def chunk_rows(self, at):
        _, first, count = self.chunks[at]
        height = ceil_to(2 * count, SUB)
        fold = np.zeros(height, np.int32)
        fold[:2 * count] = first + np.tile(np.arange(count), 2)
        row = np.arange(height)
        return fold, row < count, row < 2 * count

    def message_rows(self):
        tables = [self.chunk_rows(at) for at in range(len(self.chunks))]
        one = [np.concatenate(column) for column in zip(*tables)]
        return [np.repeat(np.arange(self.group, dtype=np.int32), self.rows)] + [
            np.tile(column, self.group) for column in one
        ]

    def transform_rows(self):
        parts = []
        for at, first, count in self.segments:
            columns = [column[first:first + count] for column in self.chunk_rows(at)]
            parts.append(
                [np.repeat(np.arange(self.group, dtype=np.int32), count)]
                + [np.tile(column, self.group) for column in columns]
            )
        return [np.concatenate(column) for column in zip(*parts)]

    def extra_row(self, message, fold):
        base, result = 0, jnp.int32(0)
        for at, first, count in self.segments:
            if first == 0:
                start = self.chunks[at][1]
                here = (fold >= start) & (fold < start + self.chunks[at][2])
                result = jnp.where(here, base + message * count + fold - start, result)
            base += self.group * count
        return result


def pack_kernel(plan, levels, info_ref, slot_ref, control_ref, out_ref):
    slots = control_ref.shape[0]
    messages = out_ref.shape[0]
    even = slots - 1
    rows = messages * plan.rows
    slot = slot_ref[...]
    pick = (slot == lax.broadcasted_iota(jnp.int32, (rows, even), 1)).astype(F32).astype(BF)
    got = jnp.dot(pick, control_ref[:even, :], preferred_element_type=F32)
    last = control_ref[even:slots, :].astype(F32)
    got = jnp.where(slot == even, last, got).astype(BF)
    extra_slot = plan.degrees - info_ref[0]
    lane = lax.broadcasted_iota(jnp.int32, (SUB, even), 1)
    first = lax.broadcasted_iota(jnp.int32, (SUB, even), 0) == 0
    choose = jnp.where(first & (lane == extra_slot), 1.0, 0.0).astype(BF)
    extra = jnp.dot(choose, control_ref[:even, :], preferred_element_type=F32)
    extra = jnp.where(extra_slot == even, last, extra)
    place = lax.broadcasted_iota(jnp.int32, (SUB, levels), 0)
    tail = jnp.zeros((SUB, levels), F32)
    for c in range(4):
        tail = jnp.where(place == c, extra[0:1, c * levels:(c + 1) * levels], tail)
    high_digit = (info_ref[0] // DIGIT).astype(F32)
    low_digit = (info_ref[0] % DIGIT).astype(F32)
    tail = jnp.where(place == 4, high_digit, jnp.where(place == 5, low_digit, tail)).astype(BF)
    for k in range(messages):
        for c in range(4):
            out_ref[k, c * plan.rows:(c + 1) * plan.rows, :] = got[
                k * plan.rows:(k + 1) * plan.rows, c * levels:(c + 1) * levels
            ]
        out_ref[k, 4 * plan.rows:, :] = tail


def pack(plan, control, lowest, slots_of_rows):
    slots, columns = control.shape
    levels = columns // 4
    height = 4 * plan.rows + SUB
    per_step = max(1, min(plan.group, 320 // plan.rows))
    return pl.pallas_call(
        functools.partial(pack_kernel, plan, levels),
        grid=(plan.group // per_step,),
        out_shape=jax.ShapeDtypeStruct((plan.group, height, levels), BF),
        in_specs=[
            pl.BlockSpec(memory_space=pltpu.SMEM),
            pl.BlockSpec((per_step * plan.rows, 1), lambda k: (k, 0)),
            pl.BlockSpec((slots, columns), lambda k: (0, 0)),
        ],
        out_specs=pl.BlockSpec((per_step, height, levels), lambda k: (k, 0, 0)),
        compiler_params=pltpu.CompilerParams(vmem_limit_bytes=VMEM_LIMIT),
        cost_estimate=pl.CostEstimate(
            flops=2 * plan.group * plan.rows * slots * columns,
            bytes_accessed=slots * columns * 2 + plan.group * height * levels * 2,
            transcendentals=0,
        ),
        name="pack_rows",
    )(lowest, slots_of_rows, control)


def swap_matrix():
    i = lax.broadcasted_iota(jnp.int32, (SUB * SUB, SUB * SUB), 0)
    j = lax.broadcasted_iota(jnp.int32, (SUB * SUB, SUB * SUB), 1)
    return jnp.where((i // SUB == j % SUB) & (i % SUB == j // SUB), 1.0, 0.0).astype(BF)


def filter_kernel(plan, at, levels, info_ref, rows_ref, own_ref, other_ref, *refs):
    row0, fold0, count = plan.chunks[at]
    last = at == len(plan.chunks) - 1
    before_ref = None if at == 0 else refs[0]
    out_ref, *carry, x_ref, y_ref = refs[0 if at == 0 else 1:]
    height = ceil_to(2 * count, SUB)
    is_high = info_ref[0] == 1
    first_fold = (info_ref[1] + fold0).astype(F32)
    swap = swap_matrix()

    def low_matrix(i):
        return jnp.where(is_high, other_ref[i], own_ref[i])

    def high_matrix(i):
        return jnp.where(is_high, own_ref[count - 1 - i], other_ref[count - 1 - i])

    def times(rows, matrix):
        return lax.dot_general(rows, matrix, (((1,), (1,)), ((), ())), preferred_element_type=F32)

    def turn(rows):
        return jnp.dot(swap, rows, preferred_element_type=F32)

    for g in range(plan.group // SUB):
        sources = slice(g * SUB, (g + 1) * SUB)
        for r in range(0, height, SUB):
            parts = []
            for c in range(4):
                start = c * plan.rows + row0 + r
                parts.append(rows_ref[sources, start:start + SUB, :].reshape(SUB * SUB, levels))
            x_ref[r * SUB:(r + SUB) * SUB, :] = turn(jnp.concatenate(parts, axis=1)).astype(BF)
        tail = turn(rows_ref[sources, 4 * plan.rows:4 * plan.rows + SUB, :].reshape(SUB * SUB, levels))
        extra = tail[:4 * SUB].astype(BF)
        low = tail[4 * SUB:5 * SUB] * DIGIT + tail[5 * SUB:6 * SUB]
        low = jnp.concatenate([low] * 4, axis=0)
        if at == 0:
            kept = jnp.zeros((4 * SUB, levels), F32)
        else:
            kept = before_ref[4 * SUB * g:4 * SUB * (g + 1), :]
        for i in range(count):
            def stack(row):
                return jnp.concatenate(
                    [x_ref[row * SUB:(row + 1) * SUB, c * levels:(c + 1) * levels] for c in range(4)], axis=0
                )

            folded, high = stack(i), stack(count + i)
            from_low = times(folded, low_matrix(i))
            from_high = times(jnp.concatenate([folded, high, extra], axis=0), high_matrix(i))
            mixed = jnp.where(low <= first_fold + i, from_low, from_high[:4 * SUB])
            kept = jnp.where(low == first_fold + i, from_high[8 * SUB:], kept)
            for row, value in ((i, mixed), (count + i, from_high[4 * SUB:8 * SUB])):
                value = value.astype(BF)
                for c in range(4):
                    y_ref[row * SUB:(row + 1) * SUB, c * levels:(c + 1) * levels] = value[c * SUB:(c + 1) * SUB]
        if height > 2 * count:
            y_ref[2 * count * SUB:height * SUB, :] = jnp.zeros(((height - 2 * count) * SUB, 4 * levels), BF)
        for r in range(0, height, SUB):
            back = turn(y_ref[r * SUB:(r + SUB) * SUB, :]).astype(BF)
            for c in range(4):
                out_ref[sources, c * height + r:c * height + r + SUB, :] = back[
                    :, c * levels:(c + 1) * levels
                ].reshape(SUB, SUB, levels)
        if last:
            filled = jnp.concatenate([kept, jnp.zeros((12 * SUB, levels), F32)], axis=0).astype(BF)
            out_ref[sources, 4 * height:4 * height + SUB, :] = turn(filled).astype(BF).reshape(SUB, SUB, levels)
        else:
            carry[0][4 * SUB * g:4 * SUB * (g + 1), :] = kept


def filter_rows(plan, at, info, received, own, other, before):
    levels = received.shape[2]
    count = plan.chunks[at][2]
    last = at == len(plan.chunks) - 1
    height = ceil_to(2 * count, SUB)
    out_height = 4 * height + (SUB if last else 0)
    smem = pl.BlockSpec(memory_space=pltpu.SMEM)
    vmem = pl.BlockSpec(memory_space=pltpu.VMEM)
    out_shape = [jax.ShapeDtypeStruct((plan.group, out_height, levels), BF)]
    if not last:
        out_shape.append(jax.ShapeDtypeStruct((4 * plan.group, levels), F32))
    operands = [info, received, own, other] + ([] if at == 0 else [before])
    return pl.pallas_call(
        functools.partial(filter_kernel, plan, at, levels),
        out_shape=out_shape,
        in_specs=[smem] + [vmem] * (len(operands) - 1),
        out_specs=[vmem] * len(out_shape),
        scratch_shapes=[
            pltpu.VMEM((height * SUB, 4 * levels), BF),
            pltpu.VMEM((height * SUB, 4 * levels), BF),
        ],
        compiler_params=pltpu.CompilerParams(vmem_limit_bytes=VMEM_LIMIT),
        cost_estimate=pl.CostEstimate(
            flops=2 * plan.group * 16 * count * levels * levels * 4,
            bytes_accessed=plan.group * out_height * levels * 4 + 4 * count * levels * levels,
            transcendentals=0,
        ),
        name="filter_rows",
    )(*operands)


def grid_kernel(plan, half, levels, latitudes, depth, level_cols, info_ref, starts_ref, bands_ref, *refs):
    count = len(plan.chunks)
    parts = refs[:count]
    table_ref, out_ref, rows_ref, grid_ref = refs[count:]
    step = pl.program_id(0)
    tile, width = table_ref.shape

    @pl.when(step == 0)
    def _():
        grid_ref[latitudes:, :] = jnp.zeros((grid_ref.shape[0] - latitudes, 4 * levels), BF)
        base = 0
        for at, first, rows in plan.segments:
            if base < width:
                height = ceil_to(2 * plan.chunks[at][2], SUB)
                for k in range(plan.group):
                    for c in range(4):
                        rows_ref[base + k * rows:base + (k + 1) * rows, c * levels:(c + 1) * levels] = parts[at][
                            k, c * height + first:c * height + first + rows, :
                        ]
            base += plan.group * rows
        if half == 1:
            height = ceil_to(2 * plan.chunks[-1][2], SUB)
            extra = parts[-1][info_ref[0], 4 * height:4 * height + SUB, :]
            base = info_ref[1] // SUB * SUB
            place = pl.ds(pl.multiple_of(base, SUB), SUB)
            here = lax.broadcasted_iota(jnp.int32, (SUB, levels), 0) == info_ref[1] - base
            for c in range(4):
                cols = slice(c * levels, (c + 1) * levels)
                held = rows_ref[place, cols].astype(F32)
                rows_ref[place, cols] = jnp.where(here, extra[c:c + 1, :].astype(F32), held).astype(BF)

    grid_ref[pl.ds(pl.multiple_of(step * tile, tile), tile), :] = jnp.dot(
        table_ref[...], rows_ref[...], preferred_element_type=F32
    ).astype(BF)

    @pl.when(step == pl.num_programs(0) - 1)
    def _():
        waves = bands_ref.shape[0]
        groups = 4 * levels // level_cols
        piece = 80 if depth % 80 == 0 else depth
        window = ceil_to(piece + SUB - 1, SUB)
        i = lax.broadcasted_iota(jnp.int32, (piece, window), 0)
        j = lax.broadcasted_iota(jnp.int32, (piece, window), 1)
        for w in range(waves):
            start = starts_ref[w]
            base = start // SUB * SUB
            moved = j - i == start - base
            for r in range(0, depth, piece):
                pick = jnp.where(moved & (i < bands_ref[w] - r), 1.0, 0.0).astype(BF)
                held = grid_ref[pl.ds(pl.multiple_of(base + r, SUB), window), :]
                got = jnp.dot(pick, held, preferred_element_type=F32).astype(BF)
                for g in range(groups):
                    out_ref[w * groups + g, r:r + piece, :] = got[:, g * level_cols:(g + 1) * level_cols]


def to_bands(plan, half, info, starts, bands, parts, table, depth, level_cols):
    latitudes, width = table.shape
    levels = parts[0].shape[2]
    columns = 4 * levels
    tile = 512
    smem = pl.BlockSpec(memory_space=pltpu.SMEM)
    messages = bands.shape[0] * columns // level_cols
    return pl.pallas_call(
        functools.partial(grid_kernel, plan, half, levels, latitudes, depth, level_cols),
        grid=(latitudes // tile,),
        out_shape=jax.ShapeDtypeStruct((messages, depth, level_cols), BF),
        in_specs=[smem, smem, smem]
        + [pl.BlockSpec(part.shape, lambda t: (0, 0, 0)) for part in parts]
        + [pl.BlockSpec((tile, width), lambda t: (t, 0))],
        out_specs=pl.BlockSpec((messages, depth, level_cols), lambda t: (0, 0, 0)),
        scratch_shapes=[
            pltpu.VMEM((width, columns), BF),
            pltpu.VMEM((ceil_to(latitudes + depth, SUB) + SUB, columns), BF),
        ],
        compiler_params=pltpu.CompilerParams(vmem_limit_bytes=VMEM_LIMIT),
        cost_estimate=pl.CostEstimate(
            flops=2 * latitudes * width * columns,
            bytes_accessed=2 * latitudes * width + 2 * messages * depth * level_cols,
            transcendentals=0,
        ),
        name="grid_bands",
    )(info, starts, bands, *parts, table)


def per_device(control, covariance, legendre, pair_order, band_rows):
    axes = ("wave", "lev")
    waves, lev_count = lax.axis_size("wave"), lax.axis_size("lev")
    _, slots, columns = control.shape
    degrees, levels = slots - 1, columns // 4
    latitudes = legendre.shape[2]
    depth = 5 * latitudes // (4 * waves)
    level_cols = columns // lev_count
    plan = Plan(waves * lev_count, degrees)
    group, block = plan.group, plan.block
    me = lax.axis_index("wave") * lev_count + lax.axis_index("lev")
    is_high = (me >= group).astype(jnp.int32)
    rank = me - group * is_high
    mine = jnp.where(is_high == 1, group - 1 - rank, rank)
    lowest = pair_order[0]
    halves = [list(range(group)), list(range(group, 2 * group))]

    def exchange(rows):
        return lax.all_to_all(rows, axes, split_axis=0, concat_axis=0, tiled=True, axis_index_groups=halves)

    mirror = [(d, 2 * group - 1 - d) for d in range(2 * group)]
    own, other = [], []
    for _, first, count in plan.chunks:
        start = jnp.where(is_high == 1, block - first - count, first)
        own.append(lax.dynamic_slice_in_dim(covariance, start, count, 0).astype(BF))
        other.append(lax.ppermute(own[-1], axes, mirror))

    def slots_of(message, fold, folded, used):
        message = jnp.where(is_high == 1, group - 1 - message, message)
        degree = message * block + fold
        upper = jnp.where(folded, degree - lowest, degrees - 1 - degree - lowest)
        upper = jnp.where(used & (upper >= 0), upper, -1)
        lower = jnp.where(used & folded & (degree <= lowest), degrees - degree, -1)
        return upper, lower

    upper, lower = slots_of(*plan.message_rows())
    sent = jnp.where(upper >= 0, upper, lower)
    received = exchange(pack(plan, control[0], pair_order, sent[:, None]))

    slot_index = jnp.arange(slots, dtype=jnp.int32)[:, None]
    tables = [
        jnp.einsum(
            "sl,sr->lr", legendre[0], (index[None, :] == slot_index).astype(BF), preferred_element_type=F32
        ).astype(BF)
        for index in (
            index[:width] for index, width in zip(slots_of(*plan.transform_rows()), plan.widths)
        )
    ]

    info = jnp.stack([is_high, mine * block])
    parts, before = [], None
    for at in range(len(plan.chunks)):
        result, *rest = filter_rows(plan, at, info, received, own[at], other[at], before)
        before = rest[0] if rest else None
        parts.append(exchange(result))

    extra_block = lowest // block
    extra_message = jnp.where(is_high == 1, group - 1 - extra_block, extra_block)
    extra_row = plan.extra_row(extra_message, lowest - extra_block * block)
    where = jnp.stack([extra_message, extra_row])
    starts = jnp.cumsum(band_rows) - band_rows
    fourier = [None, None]
    for half in (1, 0):
        outgoing = to_bands(plan, half, where, starts, band_rows, parts, tables[half], depth, level_cols)
        fourier[half] = lax.all_to_all(outgoing, axes, split_axis=0, concat_axis=0, tiled=True)
    return jnp.stack(fourier, axis=1).reshape(-1, depth, level_cols)


def solution(mesh):
    return jax.shard_map(
        per_device,
        mesh=mesh,
        in_specs=(
            P(("wave", "lev"), None, None),
            P(("wave", "lev"), None, None),
            P(("wave", "lev"), None, None),
            P(("wave", "lev")),
            P(),
        ),
        out_specs=P(None, "wave", "lev"),
        check_vma=False,
    )
```

```python
import functools

import jax
import jax.numpy as jnp
import numpy as np
from jax import lax
from jax.experimental import pallas as pl
from jax.experimental.pallas import tpu as pltpu
from jax.sharding import PartitionSpec as P

BF = jnp.bfloat16
F32 = jnp.float32
VMEM_LIMIT = 56 * 1024 * 1024
SUB = 16
DIGIT = 16


def ceil_to(value, step):
    return (value + step - 1) // step * step


class Plan:
    def __init__(self, devices, degrees):
        self.devices = devices
        self.group = devices // 2
        self.degrees = degrees
        self.block = degrees // devices
        self.chunks = []
        row, fold = 0, 0
        for count in self.fold_counts(self.block):
            self.chunks.append((row, fold, count))
            row += ceil_to(2 * count, SUB)
            fold += count
        self.rows = row
        whole = [(at, n) for at, (_, _, n) in enumerate(self.chunks) if n % SUB == 0]
        mixed = [(at, n) for at, (_, _, n) in enumerate(self.chunks) if n % SUB]
        lower = [(at, 0, n) for at, n in whole] + [(at, 0, ceil_to(2 * n, SUB)) for at, n in mixed]
        self.segments = lower + [(at, n, n) for at, n in whole]
        self.widths = [
            self.group * sum(n for _, _, n in self.segments),
            self.group * sum(n for _, _, n in lower),
        ]

    @staticmethod
    def fold_counts(block):
        return (block - 8, 8) if block % SUB == 8 and block > 8 else (block,)

    def chunk_rows(self, at):
        _, first, count = self.chunks[at]
        height = ceil_to(2 * count, SUB)
        fold = np.zeros(height, np.int32)
        fold[:2 * count] = first + np.tile(np.arange(count), 2)
        row = np.arange(height)
        return fold, row < count, row < 2 * count

    def message_rows(self):
        tables = [self.chunk_rows(at) for at in range(len(self.chunks))]
        one = [np.concatenate(column) for column in zip(*tables)]
        return [np.repeat(np.arange(self.group, dtype=np.int32), self.rows)] + [
            np.tile(column, self.group) for column in one
        ]

    def transform_rows(self):
        parts = []
        for at, first, count in self.segments:
            columns = [column[first:first + count] for column in self.chunk_rows(at)]
            parts.append(
                [np.repeat(np.arange(self.group, dtype=np.int32), count)]
                + [np.tile(column, self.group) for column in columns]
            )
        return [np.concatenate(column) for column in zip(*parts)]

    def extra_row(self, message, fold):
        base, result = 0, jnp.int32(0)
        for at, first, count in self.segments:
            if first == 0:
                start = self.chunks[at][1]
                here = (fold >= start) & (fold < start + self.chunks[at][2])
                result = jnp.where(here, base + message * count + fold - start, result)
            base += self.group * count
        return result


def pack_kernel(plan, levels, info_ref, slot_ref, control_ref, out_ref):
    slots = control_ref.shape[0]
    messages = out_ref.shape[0]
    even = slots - 1
    rows = messages * plan.rows
    slot = slot_ref[...]
    pick = (slot == lax.broadcasted_iota(jnp.int32, (rows, even), 1)).astype(F32).astype(BF)
    got = jnp.dot(pick, control_ref[:even, :], preferred_element_type=F32)
    last = control_ref[even:slots, :].astype(F32)
    got = jnp.where(slot == even, last, got).astype(BF)
    extra_slot = plan.degrees - info_ref[0]
    lane = lax.broadcasted_iota(jnp.int32, (SUB, even), 1)
    first = lax.broadcasted_iota(jnp.int32, (SUB, even), 0) == 0
    choose = jnp.where(first & (lane == extra_slot), 1.0, 0.0).astype(BF)
    extra = jnp.dot(choose, control_ref[:even, :], preferred_element_type=F32)
    extra = jnp.where(extra_slot == even, last, extra)
    place = lax.broadcasted_iota(jnp.int32, (SUB, levels), 0)
    tail = jnp.zeros((SUB, levels), F32)
    for c in range(4):
        tail = jnp.where(place == c, extra[0:1, c * levels:(c + 1) * levels], tail)
    high_digit = (info_ref[0] // DIGIT).astype(F32)
    low_digit = (info_ref[0] % DIGIT).astype(F32)
    tail = jnp.where(place == 4, high_digit, jnp.where(place == 5, low_digit, tail)).astype(BF)
    for k in range(messages):
        for c in range(4):
            out_ref[k, c * plan.rows:(c + 1) * plan.rows, :] = got[
                k * plan.rows:(k + 1) * plan.rows, c * levels:(c + 1) * levels
            ]
        out_ref[k, 4 * plan.rows:, :] = tail


def pack(plan, control, lowest, slots_of_rows):
    slots, columns = control.shape
    levels = columns // 4
    height = 4 * plan.rows + SUB
    per_step = max(1, min(plan.group, 320 // plan.rows))
    return pl.pallas_call(
        functools.partial(pack_kernel, plan, levels),
        grid=(plan.group // per_step,),
        out_shape=jax.ShapeDtypeStruct((plan.group, height, levels), BF),
        in_specs=[
            pl.BlockSpec(memory_space=pltpu.SMEM),
            pl.BlockSpec((per_step * plan.rows, 1), lambda k: (k, 0)),
            pl.BlockSpec((slots, columns), lambda k: (0, 0)),
        ],
        out_specs=pl.BlockSpec((per_step, height, levels), lambda k: (k, 0, 0)),
        compiler_params=pltpu.CompilerParams(vmem_limit_bytes=VMEM_LIMIT),
        cost_estimate=pl.CostEstimate(
            flops=2 * plan.group * plan.rows * slots * columns,
            bytes_accessed=slots * columns * 2 + plan.group * height * levels * 2,
            transcendentals=0,
        ),
        name="pack_rows",
    )(lowest, slots_of_rows, control)


def swap_matrix():
    i = lax.broadcasted_iota(jnp.int32, (SUB * SUB, SUB * SUB), 0)
    j = lax.broadcasted_iota(jnp.int32, (SUB * SUB, SUB * SUB), 1)
    return jnp.where((i // SUB == j % SUB) & (i % SUB == j // SUB), 1.0, 0.0).astype(BF)


def filter_kernel(plan, at, levels, info_ref, rows_ref, own_ref, other_ref, *refs):
    row0, fold0, count = plan.chunks[at]
    last = at == len(plan.chunks) - 1
    before_ref = None if at == 0 else refs[0]
    out_ref, *carry, x_ref, y_ref = refs[0 if at == 0 else 1:]
    height = ceil_to(2 * count, SUB)
    is_high = info_ref[0] == 1
    first_fold = (info_ref[1] + fold0).astype(F32)
    swap = swap_matrix()

    def low_matrix(i):
        return jnp.where(is_high, other_ref[i], own_ref[i])

    def high_matrix(i):
        return jnp.where(is_high, own_ref[count - 1 - i], other_ref[count - 1 - i])

    def times(rows, matrix):
        return lax.dot_general(rows, matrix, (((1,), (1,)), ((), ())), preferred_element_type=F32)

    def turn(rows):
        return jnp.dot(swap, rows, preferred_element_type=F32)

    for g in range(plan.group // SUB):
        sources = slice(g * SUB, (g + 1) * SUB)
        for r in range(0, height, SUB):
            parts = []
            for c in range(4):
                start = c * plan.rows + row0 + r
                parts.append(rows_ref[sources, start:start + SUB, :].reshape(SUB * SUB, levels))
            x_ref[r * SUB:(r + SUB) * SUB, :] = turn(jnp.concatenate(parts, axis=1)).astype(BF)
        tail = turn(rows_ref[sources, 4 * plan.rows:4 * plan.rows + SUB, :].reshape(SUB * SUB, levels))
        extra = tail[:4 * SUB].astype(BF)
        low = tail[4 * SUB:5 * SUB] * DIGIT + tail[5 * SUB:6 * SUB]
        low = jnp.concatenate([low] * 4, axis=0)
        if at == 0:
            kept = jnp.zeros((4 * SUB, levels), F32)
        else:
            kept = before_ref[4 * SUB * g:4 * SUB * (g + 1), :]
        for i in range(count):
            def stack(row):
                return jnp.concatenate(
                    [x_ref[row * SUB:(row + 1) * SUB, c * levels:(c + 1) * levels] for c in range(4)], axis=0
                )

            folded, high = stack(i), stack(count + i)
            from_low = times(folded, low_matrix(i))
            from_high = times(jnp.concatenate([folded, high, extra], axis=0), high_matrix(i))
            mixed = jnp.where(low <= first_fold + i, from_low, from_high[:4 * SUB])
            kept = jnp.where(low == first_fold + i, from_high[8 * SUB:], kept)
            for row, value in ((i, mixed), (count + i, from_high[4 * SUB:8 * SUB])):
                value = value.astype(BF)
                for c in range(4):
                    y_ref[row * SUB:(row + 1) * SUB, c * levels:(c + 1) * levels] = value[c * SUB:(c + 1) * SUB]
        if height > 2 * count:
            y_ref[2 * count * SUB:height * SUB, :] = jnp.zeros(((height - 2 * count) * SUB, 4 * levels), BF)
        for r in range(0, height, SUB):
            back = turn(y_ref[r * SUB:(r + SUB) * SUB, :]).astype(BF)
            for c in range(4):
                out_ref[sources, c * height + r:c * height + r + SUB, :] = back[
                    :, c * levels:(c + 1) * levels
                ].reshape(SUB, SUB, levels)
        if last:
            filled = jnp.concatenate([kept, jnp.zeros((12 * SUB, levels), F32)], axis=0).astype(BF)
            out_ref[sources, 4 * height:4 * height + SUB, :] = turn(filled).astype(BF).reshape(SUB, SUB, levels)
        else:
            carry[0][4 * SUB * g:4 * SUB * (g + 1), :] = kept


def filter_rows(plan, at, info, received, own, other, before):
    levels = received.shape[2]
    count = plan.chunks[at][2]
    last = at == len(plan.chunks) - 1
    height = ceil_to(2 * count, SUB)
    out_height = 4 * height + (SUB if last else 0)
    smem = pl.BlockSpec(memory_space=pltpu.SMEM)
    vmem = pl.BlockSpec(memory_space=pltpu.VMEM)
    out_shape = [jax.ShapeDtypeStruct((plan.group, out_height, levels), BF)]
    if not last:
        out_shape.append(jax.ShapeDtypeStruct((4 * plan.group, levels), F32))
    operands = [info, received, own, other] + ([] if at == 0 else [before])
    return pl.pallas_call(
        functools.partial(filter_kernel, plan, at, levels),
        out_shape=out_shape,
        in_specs=[smem] + [vmem] * (len(operands) - 1),
        out_specs=[vmem] * len(out_shape),
        scratch_shapes=[
            pltpu.VMEM((height * SUB, 4 * levels), BF),
            pltpu.VMEM((height * SUB, 4 * levels), BF),
        ],
        compiler_params=pltpu.CompilerParams(vmem_limit_bytes=VMEM_LIMIT),
        cost_estimate=pl.CostEstimate(
            flops=2 * plan.group * 16 * count * levels * levels * 4,
            bytes_accessed=plan.group * out_height * levels * 4 + 4 * count * levels * levels,
            transcendentals=0,
        ),
        name="filter_rows",
    )(*operands)


def grid_kernel(plan, levels, latitudes, depth, level_cols, info_ref, starts_ref, bands_ref, *refs):
    count = len(plan.chunks)
    parts = refs[:count]
    tables, (out_ref, rows_ref, grid_ref) = refs[count:count + 2], refs[count + 2:]
    half, step = pl.program_id(0), pl.program_id(1)
    tile = tables[0].shape[0]

    @pl.when((half == 0) & (step == 0))
    def _():
        base = 0
        for at, first, rows in plan.segments:
            height = ceil_to(2 * plan.chunks[at][2], SUB)
            for k in range(plan.group):
                for c in range(4):
                    rows_ref[base + k * rows:base + (k + 1) * rows, c * levels:(c + 1) * levels] = parts[at][
                        k, c * height + first:c * height + first + rows, :
                    ]
            base += plan.group * rows

    @pl.when((half == 1) & (step == 0))
    def _():
        height = ceil_to(2 * plan.chunks[-1][2], SUB)
        extra = parts[-1][info_ref[0], 4 * height:4 * height + SUB, :]
        base = info_ref[1] // SUB * SUB
        place = pl.ds(pl.multiple_of(base, SUB), SUB)
        here = lax.broadcasted_iota(jnp.int32, (SUB, levels), 0) == info_ref[1] - base
        for c in range(4):
            cols = slice(c * levels, (c + 1) * levels)
            held = rows_ref[place, cols].astype(F32)
            rows_ref[place, cols] = jnp.where(here, extra[c:c + 1, :].astype(F32), held).astype(BF)

    for at in range(2):
        @pl.when(half == at)
        def _():
            grid_ref[pl.ds(pl.multiple_of(step * tile, tile), tile), :] = jnp.dot(
                tables[at][...], rows_ref[:plan.widths[at], :], preferred_element_type=F32
            )

    @pl.when(step == pl.num_programs(1) - 1)
    def _():
        waves = bands_ref.shape[0]
        groups = 4 * levels // level_cols
        piece = 80 if depth % 80 == 0 else depth
        i = lax.broadcasted_iota(jnp.int32, (piece, 4 * levels), 0)
        for w in range(waves):
            start = starts_ref[w]
            base = start // 8 * 8
            for r in range(0, depth, piece):
                held = grid_ref[pl.ds(pl.multiple_of(base + r, 8), piece + 8), :]
                held = pltpu.roll(held, (piece + 8 - (start - base)) % (piece + 8), axis=0)[:piece]
                got = jnp.where(i < bands_ref[w] - r, held, 0.0).astype(BF)
                for g in range(groups):
                    out_ref[w * groups + g, 0, r:r + piece, :] = got[:, g * level_cols:(g + 1) * level_cols]


def to_bands(plan, info, starts, bands, parts, tables, depth, level_cols):
    latitudes = tables[0].shape[0]
    levels = parts[0].shape[2]
    columns = 4 * levels
    tile = 512
    steps = latitudes // tile
    smem = pl.BlockSpec(memory_space=pltpu.SMEM)
    messages = bands.shape[0] * columns // level_cols
    return pl.pallas_call(
        functools.partial(grid_kernel, plan, levels, latitudes, depth, level_cols),
        grid=(2, steps),
        out_shape=jax.ShapeDtypeStruct((messages, 2, depth, level_cols), BF),
        in_specs=[smem, smem, smem]
        + [pl.BlockSpec(part.shape, lambda h, t: (0, 0, 0)) for part in parts]
        + [
            pl.BlockSpec((tile, plan.widths[0]), lambda h, t: (jnp.where(h == 0, t, steps - 1), 0)),
            pl.BlockSpec((tile, plan.widths[1]), lambda h, t: (jnp.where(h == 0, 0, t), 0)),
        ],
        out_specs=pl.BlockSpec((messages, 1, depth, level_cols), lambda h, t: (0, h, 0, 0)),
        scratch_shapes=[
            pltpu.VMEM((plan.widths[0], columns), BF),
            pltpu.VMEM((ceil_to(latitudes + depth, 8) + 8, columns), F32),
        ],
        compiler_params=pltpu.CompilerParams(vmem_limit_bytes=VMEM_LIMIT),
        cost_estimate=pl.CostEstimate(
            flops=2 * latitudes * sum(plan.widths) * columns,
            bytes_accessed=2 * latitudes * sum(plan.widths) + 4 * messages * depth * level_cols,
            transcendentals=0,
        ),
        name="grid_bands",
    )(info, starts, bands, *parts, *tables)


def per_device(control, covariance, legendre, pair_order, band_rows):
    axes = ("wave", "lev")
    waves, lev_count = lax.axis_size("wave"), lax.axis_size("lev")
    _, slots, columns = control.shape
    degrees, levels = slots - 1, columns // 4
    latitudes = legendre.shape[2]
    depth = 5 * latitudes // (4 * waves)
    level_cols = columns // lev_count
    plan = Plan(waves * lev_count, degrees)
    group, block = plan.group, plan.block
    me = lax.axis_index("wave") * lev_count + lax.axis_index("lev")
    is_high = (me >= group).astype(jnp.int32)
    rank = me - group * is_high
    mine = jnp.where(is_high == 1, group - 1 - rank, rank)
    lowest = pair_order[0]
    halves = [list(range(group)), list(range(group, 2 * group))]

    def exchange(rows):
        return lax.all_to_all(rows, axes, split_axis=0, concat_axis=0, tiled=True, axis_index_groups=halves)

    mirror = [(d, 2 * group - 1 - d) for d in range(2 * group)]
    own, other = [], []
    for _, first, count in plan.chunks:
        start = jnp.where(is_high == 1, block - first - count, first)
        block_rows = lax.dynamic_slice_in_dim(covariance, start, count, 0).astype(BF)
        if other:
            block_rows, other[-1] = lax.optimization_barrier((block_rows, other[-1]))
        else:
            block_rows, control = lax.optimization_barrier((block_rows, control))
        own.append(block_rows)
        other.append(lax.ppermute(own[-1], axes, mirror))

    def slots_of(message, fold, folded, used):
        message = jnp.where(is_high == 1, group - 1 - message, message)
        degree = message * block + fold
        upper = jnp.where(folded, degree - lowest, degrees - 1 - degree - lowest)
        upper = jnp.where(used & (upper >= 0), upper, -1)
        lower = jnp.where(used & folded & (degree <= lowest), degrees - degree, -1)
        return upper, lower

    upper, lower = slots_of(*plan.message_rows())
    sent = jnp.where(upper >= 0, upper, lower)
    received = exchange(pack(plan, control[0], pair_order, sent[:, None]))

    slot_index = jnp.arange(slots, dtype=jnp.int32)[:, None]
    tables = [
        jnp.einsum(
            "sl,sr->lr", legendre[0], (index[None, :] == slot_index).astype(BF), preferred_element_type=F32
        ).astype(BF)
        for index in (
            index[:width] for index, width in zip(slots_of(*plan.transform_rows()), plan.widths)
        )
    ]

    info = jnp.stack([is_high, mine * block])
    received, tables = lax.optimization_barrier((received, tables))
    parts, before = [], None
    for at in range(len(plan.chunks)):
        result, *rest = filter_rows(plan, at, info, received, own[at], other[at], before)
        before = rest[0] if rest else None
        parts.append(exchange(result))

    extra_block = lowest // block
    extra_message = jnp.where(is_high == 1, group - 1 - extra_block, extra_block)
    extra_row = plan.extra_row(extra_message, lowest - extra_block * block)
    where = jnp.stack([extra_message, extra_row])
    starts = jnp.cumsum(band_rows) - band_rows
    outgoing = to_bands(plan, where, starts, band_rows, parts, tables, depth, level_cols)
    outgoing = outgoing.reshape(-1, depth, level_cols)
    return lax.all_to_all(outgoing, axes, split_axis=0, concat_axis=0, tiled=True)


def solution(mesh):
    return jax.shard_map(
        per_device,
        mesh=mesh,
        in_specs=(
            P(("wave", "lev"), None, None),
            P(("wave", "lev"), None, None),
            P(("wave", "lev"), None, None),
            P(("wave", "lev")),
            P(),
        ),
        out_specs=P(None, "wave", "lev"),
        check_vma=False,
    )
```

```python
import functools

import jax
import jax.numpy as jnp
import numpy as np
from jax import lax
from jax.experimental import pallas as pl
from jax.experimental.pallas import tpu as pltpu
from jax.sharding import PartitionSpec as P

BF = jnp.bfloat16
F32 = jnp.float32
SUB = 16
DIGIT = 16


def ceil_to(value, step):
    return (value + step - 1) // step * step


class Plan:
    def __init__(self, devices, degrees):
        self.devices = devices
        self.group = devices // 2
        self.degrees = degrees
        self.block = degrees // devices
        self.chunks = []
        row, fold = 0, 0
        for count in self.fold_counts(self.block):
            self.chunks.append((row, fold, count))
            row += ceil_to(2 * count, SUB)
            fold += count
        self.rows = row
        whole = [(at, n) for at, (_, _, n) in enumerate(self.chunks) if n % SUB == 0]
        mixed = [(at, n) for at, (_, _, n) in enumerate(self.chunks) if n % SUB]
        lower = [(at, 0, n) for at, n in whole] + [(at, 0, ceil_to(2 * n, SUB)) for at, n in mixed]
        self.segments = lower + [(at, n, n) for at, n in whole]
        self.widths = [
            self.group * sum(n for _, _, n in self.segments),
            self.group * sum(n for _, _, n in lower),
        ]

    @staticmethod
    def fold_counts(block):
        return (block - 8, 8) if block % SUB == 8 and block > 8 else (block,)

    def chunk_rows(self, at):
        _, first, count = self.chunks[at]
        height = ceil_to(2 * count, SUB)
        fold = np.zeros(height, np.int32)
        fold[:2 * count] = first + np.tile(np.arange(count), 2)
        row = np.arange(height)
        return fold, row < count, row < 2 * count

    def message_rows(self):
        tables = [self.chunk_rows(at) for at in range(len(self.chunks))]
        one = [np.concatenate(column) for column in zip(*tables)]
        return [np.repeat(np.arange(self.group, dtype=np.int32), self.rows)] + [
            np.tile(column, self.group) for column in one
        ]

    def transform_rows(self):
        parts = []
        for at, first, count in self.segments:
            columns = [column[first:first + count] for column in self.chunk_rows(at)]
            parts.append(
                [np.repeat(np.arange(self.group, dtype=np.int32), count)]
                + [np.tile(column, self.group) for column in columns]
            )
        return [np.concatenate(column) for column in zip(*parts)]

    def extra_row(self, message, fold):
        base, result = 0, jnp.int32(0)
        for at, first, count in self.segments:
            if first == 0:
                start = self.chunks[at][1]
                here = (fold >= start) & (fold < start + self.chunks[at][2])
                result = jnp.where(here, base + message * count + fold - start, result)
            base += self.group * count
        return result


def pack_kernel(plan, levels, info_ref, slot_ref, control_ref, out_ref):
    slots = control_ref.shape[0]
    messages = out_ref.shape[0]
    even = slots - 1
    rows = messages * plan.rows
    slot = slot_ref[...]
    pick = (slot == lax.broadcasted_iota(jnp.int32, (rows, even), 1)).astype(F32).astype(BF)
    got = jnp.dot(pick, control_ref[:even, :], preferred_element_type=F32)
    last = control_ref[even:slots, :].astype(F32)
    got = jnp.where(slot == even, last, got).astype(BF)
    extra_slot = plan.degrees - info_ref[0]
    lane = lax.broadcasted_iota(jnp.int32, (SUB, even), 1)
    first = lax.broadcasted_iota(jnp.int32, (SUB, even), 0) == 0
    choose = jnp.where(first & (lane == extra_slot), 1.0, 0.0).astype(BF)
    extra = jnp.dot(choose, control_ref[:even, :], preferred_element_type=F32)
    extra = jnp.where(extra_slot == even, last, extra)
    place = lax.broadcasted_iota(jnp.int32, (SUB, levels), 0)
    tail = jnp.zeros((SUB, levels), F32)
    for c in range(4):
        tail = jnp.where(place == c, extra[0:1, c * levels:(c + 1) * levels], tail)
    high_digit = (info_ref[0] // DIGIT).astype(F32)
    low_digit = (info_ref[0] % DIGIT).astype(F32)
    tail = jnp.where(place == 4, high_digit, jnp.where(place == 5, low_digit, tail)).astype(BF)
    for k in range(messages):
        for c in range(4):
            out_ref[k, c * plan.rows:(c + 1) * plan.rows, :] = got[
                k * plan.rows:(k + 1) * plan.rows, c * levels:(c + 1) * levels
            ]
        out_ref[k, 4 * plan.rows:, :] = tail


def pack(plan, control, lowest, slots_of_rows):
    slots, columns = control.shape
    levels = columns // 4
    height = 4 * plan.rows + SUB
    per_step = max(1, min(plan.group, 320 // plan.rows))
    return pl.pallas_call(
        functools.partial(pack_kernel, plan, levels),
        grid=(plan.group // per_step,),
        out_shape=jax.ShapeDtypeStruct((plan.group, height, levels), BF),
        in_specs=[
            pl.BlockSpec(memory_space=pltpu.SMEM),
            pl.BlockSpec((per_step * plan.rows, 1), lambda k: (k, 0)),
            pl.BlockSpec((slots, columns), lambda k: (0, 0)),
        ],
        out_specs=pl.BlockSpec((per_step, height, levels), lambda k: (k, 0, 0)),
        compiler_params=pltpu.CompilerParams(vmem_limit_bytes=16 * 1024 * 1024),
        cost_estimate=pl.CostEstimate(flops=1, bytes_accessed=1, transcendentals=0),
        name="pack_rows",
    )(lowest, slots_of_rows, control)


def table_kernel(plan, upper_ref, lower_ref, legendre_ref, *refs):
    outs, picks = refs[:2], refs[2:]
    slots = legendre_ref.shape[0]
    even = slots - 1

    @pl.when(pl.program_id(0) == 0)
    def _():
        for index_ref, pick_ref in zip((upper_ref, lower_ref), picks):
            slot = lax.broadcasted_iota(jnp.int32, pick_ref.shape, 0)
            pick_ref[...] = jnp.where(slot == index_ref[...], 1.0, 0.0).astype(BF)

    def times(rows, picked):
        return lax.dot_general(rows, picked, (((0,), (0,)), ((), ())), preferred_element_type=F32)

    for out_ref, pick_ref in zip(outs, picks):
        got = times(legendre_ref[:even, :], pick_ref[:even, :])
        last = jnp.concatenate(
            [legendre_ref[even:slots, :].astype(F32), jnp.zeros((SUB - 1, legendre_ref.shape[1]), F32)], axis=0
        ).astype(BF)
        out_ref[...] = (got + times(last, pick_ref[even:even + SUB, :])).astype(BF)


def make_tables(plan, legendre, slots_of_rows):
    slots, latitudes = legendre.shape
    tile = 256
    index = [rows[None, :width] for rows, width in zip(slots_of_rows, plan.widths)]
    return pl.pallas_call(
        functools.partial(table_kernel, plan),
        grid=(latitudes // tile,),
        out_shape=[jax.ShapeDtypeStruct((latitudes, width), BF) for width in plan.widths],
        in_specs=[pl.BlockSpec((1, width), lambda t: (0, 0)) for width in plan.widths]
        + [pl.BlockSpec((slots, tile), lambda t: (0, t))],
        out_specs=[pl.BlockSpec((tile, width), lambda t: (t, 0)) for width in plan.widths],
        scratch_shapes=[pltpu.VMEM((slots - 1 + SUB, width), BF) for width in plan.widths],
        compiler_params=pltpu.CompilerParams(vmem_limit_bytes=32 * 1024 * 1024),
        cost_estimate=pl.CostEstimate(flops=1, bytes_accessed=1, transcendentals=0),
        name="make_tables",
    )(*index, legendre)


def swap_matrix():
    i = lax.broadcasted_iota(jnp.int32, (SUB * SUB, SUB * SUB), 0)
    j = lax.broadcasted_iota(jnp.int32, (SUB * SUB, SUB * SUB), 1)
    return jnp.where((i // SUB == j % SUB) & (i % SUB == j // SUB), 1.0, 0.0).astype(BF)


def filter_kernel(plan, levels, pieces, info_ref, rows_ref, *refs):
    own_refs, other_refs, (out_ref, x_ref, y_ref) = refs[:pieces], refs[pieces:2 * pieces], refs[2 * pieces:]
    each = plan.block // pieces
    is_high = info_ref[0] == 1
    first_fold = info_ref[1].astype(F32)
    swap = swap_matrix()

    def low_matrix(fold):
        return jnp.where(is_high, other_refs[fold // each][fold % each], own_refs[fold // each][fold % each])

    def high_matrix(fold):
        at, place = fold // each, each - 1 - fold % each
        return jnp.where(is_high, own_refs[at][place], other_refs[at][place])

    def times(rows, matrix):
        return lax.dot_general(rows, matrix, (((1,), (1,)), ((), ())), preferred_element_type=F32)

    def turn(rows):
        return jnp.dot(swap, rows, preferred_element_type=F32)

    for g in range(plan.group // SUB):
        sources = slice(g * SUB, (g + 1) * SUB)
        for r in range(0, plan.rows, SUB):
            parts = []
            for c in range(4):
                start = c * plan.rows + r
                parts.append(rows_ref[sources, start:start + SUB, :].reshape(SUB * SUB, levels))
            x_ref[r * SUB:(r + SUB) * SUB, :] = turn(jnp.concatenate(parts, axis=1)).astype(BF)
        tail = turn(rows_ref[sources, 4 * plan.rows:4 * plan.rows + SUB, :].reshape(SUB * SUB, levels))
        extra = tail[:4 * SUB].astype(BF)
        low = tail[4 * SUB:5 * SUB] * DIGIT + tail[5 * SUB:6 * SUB]
        low = jnp.concatenate([low] * 4, axis=0)
        kept = jnp.zeros((4 * SUB, levels), F32)
        for row0, fold0, count in plan.chunks:
            for i in range(count):
                def stack(row):
                    return jnp.concatenate(
                        [x_ref[row * SUB:(row + 1) * SUB, c * levels:(c + 1) * levels] for c in range(4)], axis=0
                    )

                folded, high = stack(row0 + i), stack(row0 + count + i)
                from_low = times(folded, low_matrix(fold0 + i))
                from_high = times(jnp.concatenate([folded, high, extra], axis=0), high_matrix(fold0 + i))
                fold = first_fold + (fold0 + i)
                mixed = jnp.where(low <= fold, from_low, from_high[:4 * SUB])
                kept = jnp.where(low == fold, from_high[8 * SUB:], kept)
                for row, value in ((row0 + i, mixed), (row0 + count + i, from_high[4 * SUB:8 * SUB])):
                    value = value.astype(BF)
                    for c in range(4):
                        y_ref[row * SUB:(row + 1) * SUB, c * levels:(c + 1) * levels] = value[c * SUB:(c + 1) * SUB]
            unused = ceil_to(2 * count, SUB) - 2 * count
            if unused:
                start = (row0 + 2 * count) * SUB
                y_ref[start:start + unused * SUB, :] = jnp.zeros((unused * SUB, 4 * levels), BF)
        for r in range(0, plan.rows, SUB):
            back = turn(y_ref[r * SUB:(r + SUB) * SUB, :]).astype(BF)
            for c in range(4):
                start = c * plan.rows + r
                out_ref[sources, start:start + SUB, :] = back[:, c * levels:(c + 1) * levels].reshape(
                    SUB, SUB, levels
                )
        filled = jnp.concatenate([kept, jnp.zeros((12 * SUB, levels), F32)], axis=0).astype(BF)
        out_ref[sources, 4 * plan.rows:4 * plan.rows + SUB, :] = turn(filled).astype(BF).reshape(SUB, SUB, levels)


def filter_rows(plan, info, received, own, other):
    levels = received.shape[2]
    operands = [info, received, *own, *other]
    vmem = pl.BlockSpec(memory_space=pltpu.VMEM)
    return pl.pallas_call(
        functools.partial(filter_kernel, plan, levels, len(own)),
        out_shape=jax.ShapeDtypeStruct(received.shape, BF),
        in_specs=[pl.BlockSpec(memory_space=pltpu.SMEM)] + [vmem] * (len(operands) - 1),
        out_specs=vmem,
        scratch_shapes=[
            pltpu.VMEM((plan.rows * SUB, 4 * levels), BF),
            pltpu.VMEM((plan.rows * SUB, 4 * levels), BF),
        ],
        compiler_params=pltpu.CompilerParams(vmem_limit_bytes=20 * 1024 * 1024),
        cost_estimate=pl.CostEstimate(
            flops=2 * plan.group * 16 * plan.block * levels * levels * 4,
            bytes_accessed=2 * 2 * received.size + 4 * plan.block * levels * levels,
            transcendentals=0,
        ),
        name="filter_rows",
    )(*operands)


def grid_kernel(plan, levels, latitudes, depth, level_cols, info_ref, starts_ref, bands_ref, part_ref, *refs):
    tables, (out_ref, rows_ref, grid_ref) = refs[:2], refs[2:]
    half, step = pl.program_id(0), pl.program_id(1)
    tile = tables[0].shape[0]

    @pl.when((half == 0) & (step == 0))
    def _():
        base = 0
        for at, first, rows in plan.segments:
            for k in range(plan.group):
                for c in range(4):
                    start = c * plan.rows + plan.chunks[at][0] + first
                    rows_ref[base + k * rows:base + (k + 1) * rows, c * levels:(c + 1) * levels] = part_ref[
                        k, start:start + rows, :
                    ]
            base += plan.group * rows

    @pl.when((half == 1) & (step == 0))
    def _():
        extra = part_ref[info_ref[0], 4 * plan.rows:4 * plan.rows + SUB, :]
        base = info_ref[1] // SUB * SUB
        place = pl.ds(pl.multiple_of(base, SUB), SUB)
        here = lax.broadcasted_iota(jnp.int32, (SUB, levels), 0) == info_ref[1] - base
        for c in range(4):
            cols = slice(c * levels, (c + 1) * levels)
            held = rows_ref[place, cols].astype(F32)
            rows_ref[place, cols] = jnp.where(here, extra[c:c + 1, :].astype(F32), held).astype(BF)

    for at in range(2):
        @pl.when(half == at)
        def _():
            grid_ref[pl.ds(pl.multiple_of(step * tile, tile), tile), :] = jnp.dot(
                tables[at][...], rows_ref[:plan.widths[at], :], preferred_element_type=F32
            )

    @pl.when(step == pl.num_programs(1) - 1)
    def _():
        waves = bands_ref.shape[0]
        groups = 4 * levels // level_cols
        place = lax.broadcasted_iota(jnp.int32, (8, 4 * levels), 0)
        for w in range(waves):
            start = starts_ref[w]
            base = start // 8 * 8
            offset = start - base

            def slab(at):
                held = grid_ref[pl.ds(pl.multiple_of(base + at, 8), 8), :]
                return pltpu.roll(held, (8 - offset) % 8, axis=0)

            after = slab(0)
            done = []
            for r in range(0, depth, 8):
                now, after = after, slab(r + 8)
                got = jnp.where(place < 8 - offset, now, after)
                done.append(jnp.where(place < bands_ref[w] - r, got, 0.0))
                if len(done) == 2 or r + 8 == depth:
                    rows = jnp.concatenate(done, axis=0).astype(BF)
                    first = r + 8 - rows.shape[0]
                    for g in range(groups):
                        out_ref[w * groups + g, 0, first:r + 8, :] = rows[:, g * level_cols:(g + 1) * level_cols]
                    done = []


def to_bands(plan, info, starts, bands, part, tables, depth, level_cols):
    latitudes = tables[0].shape[0]
    levels = part.shape[2]
    columns = 4 * levels
    tile = 512
    steps = latitudes // tile
    smem = pl.BlockSpec(memory_space=pltpu.SMEM)
    messages = bands.shape[0] * columns // level_cols
    return pl.pallas_call(
        functools.partial(grid_kernel, plan, levels, latitudes, depth, level_cols),
        grid=(2, steps),
        out_shape=jax.ShapeDtypeStruct((messages, 2, depth, level_cols), BF),
        in_specs=[
            smem, smem, smem,
            pl.BlockSpec(part.shape, lambda h, t: (0, 0, 0)),
            pl.BlockSpec((tile, plan.widths[0]), lambda h, t: (jnp.where(h == 0, t, steps - 1), 0)),
            pl.BlockSpec((tile, plan.widths[1]), lambda h, t: (jnp.where(h == 0, 0, t), 0)),
        ],
        out_specs=pl.BlockSpec((messages, 1, depth, level_cols), lambda h, t: (0, h, 0, 0)),
        scratch_shapes=[
            pltpu.VMEM((plan.widths[0], columns), BF),
            pltpu.VMEM((ceil_to(latitudes + depth, 8) + 8, columns), F32),
        ],
        compiler_params=pltpu.CompilerParams(vmem_limit_bytes=40 * 1024 * 1024),
        cost_estimate=pl.CostEstimate(
            flops=2 * latitudes * sum(plan.widths) * columns,
            bytes_accessed=2 * latitudes * sum(plan.widths) + 4 * messages * depth * level_cols,
            transcendentals=0,
        ),
        name="grid_bands",
    )(info, starts, bands, part, *tables)


def per_device(control, covariance, legendre, pair_order, band_rows):
    axes = ("wave", "lev")
    waves, lev_count = lax.axis_size("wave"), lax.axis_size("lev")
    _, slots, columns = control.shape
    degrees, levels = slots - 1, columns // 4
    latitudes = legendre.shape[2]
    depth = 5 * latitudes // (4 * waves)
    level_cols = columns // lev_count
    plan = Plan(waves * lev_count, degrees)
    group, block = plan.group, plan.block
    me = lax.axis_index("wave") * lev_count + lax.axis_index("lev")
    is_high = (me >= group).astype(jnp.int32)
    rank = me - group * is_high
    mine = jnp.where(is_high == 1, group - 1 - rank, rank)
    lowest = pair_order[0]
    halves = [list(range(group)), list(range(group, 2 * group))]

    def exchange(rows):
        return lax.all_to_all(rows, axes, split_axis=0, concat_axis=0, tiled=True, axis_index_groups=halves)

    mirror = [(d, 2 * group - 1 - d) for d in range(2 * group)]
    pieces = 2 if block % 2 == 0 else 1
    each = block // pieces
    own = []
    for fold in range(0, block, each):
        start = jnp.where(is_high == 1, block - fold - each, fold)
        own.append(lax.dynamic_slice_in_dim(covariance, start, each, 0).astype(BF))
    *own, control = lax.optimization_barrier((*own, control))
    other = [lax.ppermute(piece, axes, mirror) for piece in own]

    def slots_of(message, fold, folded, used):
        message = jnp.where(is_high == 1, group - 1 - message, message)
        degree = message * block + fold
        upper = jnp.where(folded, degree - lowest, degrees - 1 - degree - lowest)
        upper = jnp.where(used & (upper >= 0), upper, -1)
        lower = jnp.where(used & folded & (degree <= lowest), degrees - degree, -1)
        return upper, lower

    upper, lower = slots_of(*plan.message_rows())
    sent = jnp.where(upper >= 0, upper, lower)
    received = exchange(pack(plan, control[0], pair_order, sent[:, None]))

    tables = make_tables(plan, legendre[0], slots_of(*plan.transform_rows()))

    info = jnp.stack([is_high, mine * block])
    received, tables = lax.optimization_barrier((received, tables))
    filtered = exchange(filter_rows(plan, info, received, own, other))

    extra_block = lowest // block
    extra_message = jnp.where(is_high == 1, group - 1 - extra_block, extra_block)
    extra_row = plan.extra_row(extra_message, lowest - extra_block * block)
    where = jnp.stack([extra_message, extra_row])
    starts = jnp.cumsum(band_rows) - band_rows
    outgoing = to_bands(plan, where, starts, band_rows, filtered, tables, depth, level_cols)
    outgoing = outgoing.reshape(-1, depth, level_cols)
    return lax.all_to_all(outgoing, axes, split_axis=0, concat_axis=0, tiled=True)


def solution(mesh):
    return jax.shard_map(
        per_device,
        mesh=mesh,
        in_specs=(
            P(("wave", "lev"), None, None),
            P(("wave", "lev"), None, None),
            P(("wave", "lev"), None, None),
            P(("wave", "lev")),
            P(),
        ),
        out_specs=P(None, "wave", "lev"),
        check_vma=False,
    )
```

```python
import functools

import jax
import jax.numpy as jnp
import numpy as np
from jax import lax
from jax.experimental import pallas as pl
from jax.experimental.pallas import tpu as pltpu
from jax.sharding import PartitionSpec as P

BF = jnp.bfloat16
F32 = jnp.float32
SUB = 16
DIGIT = 16


def ceil_to(value, step):
    return (value + step - 1) // step * step


class Plan:
    def __init__(self, devices, degrees):
        self.devices = devices
        self.group = devices // 2
        self.degrees = degrees
        self.block = degrees // devices
        self.chunks = []
        row, fold = 0, 0
        for count in self.fold_counts(self.block):
            self.chunks.append((row, fold, count))
            row += ceil_to(2 * count, SUB)
            fold += count
        self.rows = row
        whole = [(at, n) for at, (_, _, n) in enumerate(self.chunks) if n % SUB == 0]
        mixed = [(at, n) for at, (_, _, n) in enumerate(self.chunks) if n % SUB]
        lower = [(at, 0, n) for at, n in whole] + [(at, 0, ceil_to(2 * n, SUB)) for at, n in mixed]
        self.segments = lower + [(at, n, n) for at, n in whole]
        self.widths = [
            self.group * sum(n for _, _, n in self.segments),
            self.group * sum(n for _, _, n in lower),
        ]

    @staticmethod
    def fold_counts(block):
        return (block - 8, 8) if block % SUB == 8 and block > 8 else (block,)

    def chunk_rows(self, at):
        _, first, count = self.chunks[at]
        height = ceil_to(2 * count, SUB)
        fold = np.zeros(height, np.int32)
        fold[:2 * count] = first + np.tile(np.arange(count), 2)
        row = np.arange(height)
        return fold, row < count, row < 2 * count

    def message_rows(self):
        tables = [self.chunk_rows(at) for at in range(len(self.chunks))]
        one = [np.concatenate(column) for column in zip(*tables)]
        return [np.repeat(np.arange(self.group, dtype=np.int32), self.rows)] + [
            np.tile(column, self.group) for column in one
        ]

    def transform_rows(self):
        parts = []
        for at, first, count in self.segments:
            columns = [column[first:first + count] for column in self.chunk_rows(at)]
            parts.append(
                [np.repeat(np.arange(self.group, dtype=np.int32), count)]
                + [np.tile(column, self.group) for column in columns]
            )
        return [np.concatenate(column) for column in zip(*parts)]

    def extra_row(self, message, fold):
        base, result = 0, jnp.int32(0)
        for at, first, count in self.segments:
            if first == 0:
                start = self.chunks[at][1]
                here = (fold >= start) & (fold < start + self.chunks[at][2])
                result = jnp.where(here, base + message * count + fold - start, result)
            base += self.group * count
        return result


def pack_kernel(plan, levels, info_ref, slot_ref, control_ref, out_ref):
    slots = control_ref.shape[0]
    messages = out_ref.shape[0]
    even = slots - 1
    rows = messages * plan.rows
    slot = slot_ref[...]
    pick = (slot == lax.broadcasted_iota(jnp.int32, (rows, even), 1)).astype(F32).astype(BF)
    got = jnp.dot(pick, control_ref[:even, :], preferred_element_type=F32)
    last = control_ref[even:slots, :].astype(F32)
    got = jnp.where(slot == even, last, got).astype(BF)
    extra_slot = plan.degrees - info_ref[0]
    lane = lax.broadcasted_iota(jnp.int32, (SUB, even), 1)
    first = lax.broadcasted_iota(jnp.int32, (SUB, even), 0) == 0
    choose = jnp.where(first & (lane == extra_slot), 1.0, 0.0).astype(BF)
    extra = jnp.dot(choose, control_ref[:even, :], preferred_element_type=F32)
    extra = jnp.where(extra_slot == even, last, extra)
    place = lax.broadcasted_iota(jnp.int32, (SUB, levels), 0)
    tail = jnp.zeros((SUB, levels), F32)
    for c in range(4):
        tail = jnp.where(place == c, extra[0:1, c * levels:(c + 1) * levels], tail)
    high_digit = (info_ref[0] // DIGIT).astype(F32)
    low_digit = (info_ref[0] % DIGIT).astype(F32)
    tail = jnp.where(place == 4, high_digit, jnp.where(place == 5, low_digit, tail)).astype(BF)
    for k in range(messages):
        for c in range(4):
            out_ref[k, c * plan.rows:(c + 1) * plan.rows, :] = got[
                k * plan.rows:(k + 1) * plan.rows, c * levels:(c + 1) * levels
            ]
        out_ref[k, 4 * plan.rows:, :] = tail


def pack(plan, control, lowest, slots_of_rows):
    slots, columns = control.shape
    levels = columns // 4
    height = 4 * plan.rows + SUB
    per_step = max(1, min(plan.group, 320 // plan.rows))
    return pl.pallas_call(
        functools.partial(pack_kernel, plan, levels),
        grid=(plan.group // per_step,),
        out_shape=jax.ShapeDtypeStruct((plan.group, height, levels), BF),
        in_specs=[
            pl.BlockSpec(memory_space=pltpu.SMEM),
            pl.BlockSpec((per_step * plan.rows, 1), lambda k: (k, 0)),
            pl.BlockSpec((slots, columns), lambda k: (0, 0)),
        ],
        out_specs=pl.BlockSpec((per_step, height, levels), lambda k: (k, 0, 0)),
        compiler_params=pltpu.CompilerParams(vmem_limit_bytes=16 * 1024 * 1024),
        cost_estimate=pl.CostEstimate(flops=1, bytes_accessed=1, transcendentals=0),
        name="pack_rows",
    )(lowest, slots_of_rows, control)


def table_kernel(plan, upper_ref, lower_ref, legendre_ref, *refs):
    outs, picks = refs[:2], refs[2:]
    slots = legendre_ref.shape[0]
    even = slots - 1

    @pl.when(pl.program_id(0) == 0)
    def _():
        for index_ref, pick_ref in zip((upper_ref, lower_ref), picks):
            slot = lax.broadcasted_iota(jnp.int32, pick_ref.shape, 0)
            pick_ref[...] = jnp.where(slot == index_ref[...], 1.0, 0.0).astype(BF)

    def times(rows, picked):
        return lax.dot_general(rows, picked, (((0,), (0,)), ((), ())), preferred_element_type=F32)

    for out_ref, pick_ref in zip(outs, picks):
        got = times(legendre_ref[:even, :], pick_ref[:even, :])
        last = jnp.concatenate(
            [legendre_ref[even:slots, :].astype(F32), jnp.zeros((SUB - 1, legendre_ref.shape[1]), F32)], axis=0
        ).astype(BF)
        out_ref[...] = (got + times(last, pick_ref[even:even + SUB, :])).astype(BF)


def make_tables(plan, legendre, slots_of_rows):
    slots, latitudes = legendre.shape
    tile = 256
    index = [rows[None, :width] for rows, width in zip(slots_of_rows, plan.widths)]
    return pl.pallas_call(
        functools.partial(table_kernel, plan),
        grid=(latitudes // tile,),
        out_shape=[jax.ShapeDtypeStruct((latitudes, width), BF) for width in plan.widths],
        in_specs=[pl.BlockSpec((1, width), lambda t: (0, 0)) for width in plan.widths]
        + [pl.BlockSpec((slots, tile), lambda t: (0, t))],
        out_specs=[pl.BlockSpec((tile, width), lambda t: (t, 0)) for width in plan.widths],
        scratch_shapes=[pltpu.VMEM((slots - 1 + SUB, width), BF) for width in plan.widths],
        compiler_params=pltpu.CompilerParams(vmem_limit_bytes=56 * 1024 * 1024),
        cost_estimate=pl.CostEstimate(flops=1, bytes_accessed=1, transcendentals=0),
        name="make_tables",
    )(*index, legendre)


def swap_matrix():
    i = lax.broadcasted_iota(jnp.int32, (SUB * SUB, SUB * SUB), 0)
    j = lax.broadcasted_iota(jnp.int32, (SUB * SUB, SUB * SUB), 1)
    return jnp.where((i // SUB == j % SUB) & (i % SUB == j // SUB), 1.0, 0.0).astype(BF)


def filter_kernel(plan, levels, pieces, info_ref, rows_ref, *refs):
    own_refs, other_refs, (out_ref, x_ref, y_ref) = refs[:pieces], refs[pieces:2 * pieces], refs[2 * pieces:]
    each = plan.block // pieces
    is_high = info_ref[0] == 1
    first_fold = info_ref[1].astype(F32)
    swap = swap_matrix()

    def low_matrix(fold):
        return jnp.where(is_high, other_refs[fold // each][fold % each], own_refs[fold // each][fold % each])

    def high_matrix(fold):
        at, place = fold // each, each - 1 - fold % each
        return jnp.where(is_high, own_refs[at][place], other_refs[at][place])

    def times(rows, matrix):
        return lax.dot_general(rows, matrix, (((1,), (1,)), ((), ())), preferred_element_type=F32)

    def turn(rows):
        return jnp.dot(swap, rows, preferred_element_type=F32)

    for g in range(plan.group // SUB):
        sources = slice(g * SUB, (g + 1) * SUB)
        for r in range(0, plan.rows, SUB):
            parts = []
            for c in range(4):
                start = c * plan.rows + r
                parts.append(rows_ref[sources, start:start + SUB, :].reshape(SUB * SUB, levels))
            x_ref[r * SUB:(r + SUB) * SUB, :] = turn(jnp.concatenate(parts, axis=1)).astype(BF)
        tail = turn(rows_ref[sources, 4 * plan.rows:4 * plan.rows + SUB, :].reshape(SUB * SUB, levels))
        extra = tail[:4 * SUB].astype(BF)
        low = tail[4 * SUB:5 * SUB] * DIGIT + tail[5 * SUB:6 * SUB]
        low = jnp.concatenate([low] * 4, axis=0)
        kept = jnp.zeros((4 * SUB, levels), F32)
        for row0, fold0, count in plan.chunks:
            for i in range(count):
                def stack(row):
                    return jnp.concatenate(
                        [x_ref[row * SUB:(row + 1) * SUB, c * levels:(c + 1) * levels] for c in range(4)], axis=0
                    )

                folded, high = stack(row0 + i), stack(row0 + count + i)
                from_low = times(folded, low_matrix(fold0 + i))
                from_high = times(jnp.concatenate([folded, high, extra], axis=0), high_matrix(fold0 + i))
                fold = first_fold + (fold0 + i)
                mixed = jnp.where(low <= fold, from_low, from_high[:4 * SUB])
                kept = jnp.where(low == fold, from_high[8 * SUB:], kept)
                for row, value in ((row0 + i, mixed), (row0 + count + i, from_high[4 * SUB:8 * SUB])):
                    value = value.astype(BF)
                    for c in range(4):
                        y_ref[row * SUB:(row + 1) * SUB, c * levels:(c + 1) * levels] = value[c * SUB:(c + 1) * SUB]
            unused = ceil_to(2 * count, SUB) - 2 * count
            if unused:
                start = (row0 + 2 * count) * SUB
                y_ref[start:start + unused * SUB, :] = jnp.zeros((unused * SUB, 4 * levels), BF)
        for r in range(0, plan.rows, SUB):
            back = turn(y_ref[r * SUB:(r + SUB) * SUB, :]).astype(BF)
            for c in range(4):
                start = c * plan.rows + r
                out_ref[sources, start:start + SUB, :] = back[:, c * levels:(c + 1) * levels].reshape(
                    SUB, SUB, levels
                )
        filled = jnp.concatenate([kept, jnp.zeros((12 * SUB, levels), F32)], axis=0).astype(BF)
        out_ref[sources, 4 * plan.rows:4 * plan.rows + SUB, :] = turn(filled).astype(BF).reshape(SUB, SUB, levels)


def filter_rows(plan, info, received, own, other):
    levels = received.shape[2]
    operands = [info, received, *own, *other]
    vmem = pl.BlockSpec(memory_space=pltpu.VMEM)
    return pl.pallas_call(
        functools.partial(filter_kernel, plan, levels, len(own)),
        out_shape=jax.ShapeDtypeStruct(received.shape, BF),
        in_specs=[pl.BlockSpec(memory_space=pltpu.SMEM)] + [vmem] * (len(operands) - 1),
        out_specs=vmem,
        scratch_shapes=[
            pltpu.VMEM((plan.rows * SUB, 4 * levels), BF),
            pltpu.VMEM((plan.rows * SUB, 4 * levels), BF),
        ],
        compiler_params=pltpu.CompilerParams(vmem_limit_bytes=20 * 1024 * 1024),
        cost_estimate=pl.CostEstimate(
            flops=2 * plan.group * 16 * plan.block * levels * levels * 4,
            bytes_accessed=2 * 2 * received.size + 4 * plan.block * levels * levels,
            transcendentals=0,
        ),
        name="filter_rows",
    )(*operands)


def grid_kernel(plan, levels, latitudes, depth, level_cols, info_ref, starts_ref, bands_ref, part_ref, *refs):
    tables, (out_ref, rows_ref, grid_ref) = refs[:2], refs[2:]
    half, step = pl.program_id(0), pl.program_id(1)
    tile = tables[0].shape[0]

    @pl.when((half == 0) & (step == 0))
    def _():
        base = 0
        for at, first, rows in plan.segments:
            for k in range(plan.group):
                for c in range(4):
                    start = c * plan.rows + plan.chunks[at][0] + first
                    rows_ref[base + k * rows:base + (k + 1) * rows, c * levels:(c + 1) * levels] = part_ref[
                        k, start:start + rows, :
                    ]
            base += plan.group * rows

    @pl.when((half == 1) & (step == 0))
    def _():
        extra = part_ref[info_ref[0], 4 * plan.rows:4 * plan.rows + SUB, :]
        base = info_ref[1] // SUB * SUB
        place = pl.ds(pl.multiple_of(base, SUB), SUB)
        here = lax.broadcasted_iota(jnp.int32, (SUB, levels), 0) == info_ref[1] - base
        for c in range(4):
            cols = slice(c * levels, (c + 1) * levels)
            held = rows_ref[place, cols].astype(F32)
            rows_ref[place, cols] = jnp.where(here, extra[c:c + 1, :].astype(F32), held).astype(BF)

    for at in range(2):
        @pl.when(half == at)
        def _():
            grid_ref[pl.ds(pl.multiple_of(step * tile, tile), tile), :] = jnp.dot(
                tables[at][...], rows_ref[:plan.widths[at], :], preferred_element_type=F32
            )

    @pl.when(step == pl.num_programs(1) - 1)
    def _():
        waves = bands_ref.shape[0]
        groups = 4 * levels // level_cols
        place = lax.broadcasted_iota(jnp.int32, (8, 4 * levels), 0)
        for w in range(waves):
            start = starts_ref[w]
            base = start // 8 * 8
            offset = start - base

            def slab(at):
                held = grid_ref[pl.ds(pl.multiple_of(base + at, 8), 8), :]
                return pltpu.roll(held, (8 - offset) % 8, axis=0)

            after = slab(0)
            done = []
            for r in range(0, depth, 8):
                now, after = after, slab(r + 8)
                got = jnp.where(place < 8 - offset, now, after)
                done.append(jnp.where(place < bands_ref[w] - r, got, 0.0))
                if len(done) == 2 or r + 8 == depth:
                    rows = jnp.concatenate(done, axis=0).astype(BF)
                    first = r + 8 - rows.shape[0]
                    for g in range(groups):
                        out_ref[w * groups + g, 0, first:r + 8, :] = rows[:, g * level_cols:(g + 1) * level_cols]
                    done = []


def to_bands(plan, info, starts, bands, part, tables, depth, level_cols):
    latitudes = tables[0].shape[0]
    levels = part.shape[2]
    columns = 4 * levels
    tile = 512
    steps = latitudes // tile
    smem = pl.BlockSpec(memory_space=pltpu.SMEM)
    messages = bands.shape[0] * columns // level_cols
    return pl.pallas_call(
        functools.partial(grid_kernel, plan, levels, latitudes, depth, level_cols),
        grid=(2, steps),
        out_shape=jax.ShapeDtypeStruct((messages, 2, depth, level_cols), BF),
        in_specs=[
            smem, smem, smem,
            pl.BlockSpec(part.shape, lambda h, t: (0, 0, 0)),
            pl.BlockSpec((tile, plan.widths[0]), lambda h, t: (jnp.where(h == 0, t, steps - 1), 0)),
            pl.BlockSpec((tile, plan.widths[1]), lambda h, t: (jnp.where(h == 0, 0, t), 0)),
        ],
        out_specs=pl.BlockSpec((messages, 1, depth, level_cols), lambda h, t: (0, h, 0, 0)),
        scratch_shapes=[
            pltpu.VMEM((plan.widths[0], columns), BF),
            pltpu.VMEM((ceil_to(latitudes + depth, 8) + 8, columns), F32),
        ],
        compiler_params=pltpu.CompilerParams(vmem_limit_bytes=56 * 1024 * 1024),
        cost_estimate=pl.CostEstimate(
            flops=2 * latitudes * sum(plan.widths) * columns,
            bytes_accessed=2 * latitudes * sum(plan.widths) + 4 * messages * depth * level_cols,
            transcendentals=0,
        ),
        name="grid_bands",
    )(info, starts, bands, part, *tables)


def per_device(control, covariance, legendre, pair_order, band_rows):
    axes = ("wave", "lev")
    waves, lev_count = lax.axis_size("wave"), lax.axis_size("lev")
    _, slots, columns = control.shape
    degrees, levels = slots - 1, columns // 4
    latitudes = legendre.shape[2]
    depth = 5 * latitudes // (4 * waves)
    level_cols = columns // lev_count
    plan = Plan(waves * lev_count, degrees)
    group, block = plan.group, plan.block
    me = lax.axis_index("wave") * lev_count + lax.axis_index("lev")
    is_high = (me >= group).astype(jnp.int32)
    rank = me - group * is_high
    mine = jnp.where(is_high == 1, group - 1 - rank, rank)
    lowest = pair_order[0]
    halves = [list(range(group)), list(range(group, 2 * group))]

    def exchange(rows):
        return lax.all_to_all(rows, axes, split_axis=0, concat_axis=0, tiled=True, axis_index_groups=halves)

    mirror = [(d, 2 * group - 1 - d) for d in range(2 * group)]
    pieces = 2 if block % 2 == 0 else 1
    each = block // pieces
    own = []
    for fold in range(0, block, each):
        start = jnp.where(is_high == 1, block - fold - each, fold)
        own.append(lax.dynamic_slice_in_dim(covariance, start, each, 0).astype(BF))
    *own, legendre = lax.optimization_barrier((*own, legendre))
    other = [lax.ppermute(piece, axes, mirror) for piece in own]

    def slots_of(message, fold, folded, used):
        message = jnp.where(is_high == 1, group - 1 - message, message)
        degree = message * block + fold
        upper = jnp.where(folded, degree - lowest, degrees - 1 - degree - lowest)
        upper = jnp.where(used & (upper >= 0), upper, -1)
        lower = jnp.where(used & folded & (degree <= lowest), degrees - degree, -1)
        return upper, lower

    tables = make_tables(plan, legendre[0], slots_of(*plan.transform_rows()))
    control, tables = lax.optimization_barrier((control, tables))
    upper, lower = slots_of(*plan.message_rows())
    sent = jnp.where(upper >= 0, upper, lower)
    received = exchange(pack(plan, control[0], pair_order, sent[:, None]))

    info = jnp.stack([is_high, mine * block])
    filtered = exchange(filter_rows(plan, info, received, own, other))

    extra_block = lowest // block
    extra_message = jnp.where(is_high == 1, group - 1 - extra_block, extra_block)
    extra_row = plan.extra_row(extra_message, lowest - extra_block * block)
    where = jnp.stack([extra_message, extra_row])
    starts = jnp.cumsum(band_rows) - band_rows
    outgoing = to_bands(plan, where, starts, band_rows, filtered, tables, depth, level_cols)
    outgoing = outgoing.reshape(-1, depth, level_cols)
    return lax.all_to_all(outgoing, axes, split_axis=0, concat_axis=0, tiled=True)


def solution(mesh):
    return jax.shard_map(
        per_device,
        mesh=mesh,
        in_specs=(
            P(("wave", "lev"), None, None),
            P(("wave", "lev"), None, None),
            P(("wave", "lev"), None, None),
            P(("wave", "lev")),
            P(),
        ),
        out_specs=P(None, "wave", "lev"),
        check_vma=False,
    )
```

```python
import functools

import jax
import jax.numpy as jnp
import numpy as np
from jax import lax
from jax.experimental import pallas as pl
from jax.experimental.pallas import tpu as pltpu
from jax.sharding import PartitionSpec as P

BF = jnp.bfloat16
F32 = jnp.float32
SUB = 16
DIGIT = 16


def ceil_to(value, step):
    return (value + step - 1) // step * step


class Plan:
    def __init__(self, devices, degrees):
        self.devices = devices
        self.group = devices // 2
        self.degrees = degrees
        self.block = degrees // devices
        self.chunks = []
        row, fold = 0, 0
        for count in self.fold_counts(self.block):
            self.chunks.append((row, fold, count))
            row += ceil_to(2 * count, SUB)
            fold += count
        self.rows = row
        whole = [(at, n) for at, (_, _, n) in enumerate(self.chunks) if n % SUB == 0]
        mixed = [(at, n) for at, (_, _, n) in enumerate(self.chunks) if n % SUB]
        lower = [(at, 0, n) for at, n in whole] + [(at, 0, ceil_to(2 * n, SUB)) for at, n in mixed]
        self.segments = lower + [(at, n, n) for at, n in whole]
        self.widths = [
            self.group * sum(n for _, _, n in self.segments),
            self.group * sum(n for _, _, n in lower),
        ]

    @staticmethod
    def fold_counts(block):
        return (block - 8, 8) if block % SUB == 8 and block > 8 else (block,)

    def chunk_rows(self, at):
        _, first, count = self.chunks[at]
        height = ceil_to(2 * count, SUB)
        fold = np.zeros(height, np.int32)
        fold[:2 * count] = first + np.tile(np.arange(count), 2)
        row = np.arange(height)
        return fold, row < count, row < 2 * count

    def message_rows(self):
        tables = [self.chunk_rows(at) for at in range(len(self.chunks))]
        one = [np.concatenate(column) for column in zip(*tables)]
        return [np.repeat(np.arange(self.group, dtype=np.int32), self.rows)] + [
            np.tile(column, self.group) for column in one
        ]

    def transform_rows(self):
        parts = []
        for at, first, count in self.segments:
            columns = [column[first:first + count] for column in self.chunk_rows(at)]
            parts.append(
                [np.repeat(np.arange(self.group, dtype=np.int32), count)]
                + [np.tile(column, self.group) for column in columns]
            )
        return [np.concatenate(column) for column in zip(*parts)]

    def extra_row(self, message, fold):
        base, result = 0, jnp.int32(0)
        for at, first, count in self.segments:
            if first == 0:
                start = self.chunks[at][1]
                here = (fold >= start) & (fold < start + self.chunks[at][2])
                result = jnp.where(here, base + message * count + fold - start, result)
            base += self.group * count
        return result


def pack_kernel(plan, levels, info_ref, slot_ref, control_ref, out_ref):
    slots = control_ref.shape[0]
    messages = out_ref.shape[0]
    even = slots - 1
    rows = messages * plan.rows
    slot = slot_ref[...]
    pick = (slot == lax.broadcasted_iota(jnp.int32, (rows, even), 1)).astype(F32).astype(BF)
    got = jnp.dot(pick, control_ref[:even, :], preferred_element_type=F32)
    last = control_ref[even:slots, :].astype(F32)
    got = jnp.where(slot == even, last, got).astype(BF)
    extra_slot = plan.degrees - info_ref[0]
    lane = lax.broadcasted_iota(jnp.int32, (SUB, even), 1)
    first = lax.broadcasted_iota(jnp.int32, (SUB, even), 0) == 0
    choose = jnp.where(first & (lane == extra_slot), 1.0, 0.0).astype(BF)
    extra = jnp.dot(choose, control_ref[:even, :], preferred_element_type=F32)
    extra = jnp.where(extra_slot == even, last, extra)
    place = lax.broadcasted_iota(jnp.int32, (SUB, levels), 0)
    tail = jnp.zeros((SUB, levels), F32)
    for c in range(4):
        tail = jnp.where(place == c, extra[0:1, c * levels:(c + 1) * levels], tail)
    high_digit = (info_ref[0] // DIGIT).astype(F32)
    low_digit = (info_ref[0] % DIGIT).astype(F32)
    tail = jnp.where(place == 4, high_digit, jnp.where(place == 5, low_digit, tail)).astype(BF)
    for k in range(messages):
        for c in range(4):
            out_ref[k, c * plan.rows:(c + 1) * plan.rows, :] = got[
                k * plan.rows:(k + 1) * plan.rows, c * levels:(c + 1) * levels
            ]
        out_ref[k, 4 * plan.rows:, :] = tail


def pack(plan, control, lowest, slots_of_rows):
    slots, columns = control.shape
    levels = columns // 4
    height = 4 * plan.rows + SUB
    per_step = max(1, min(plan.group, 320 // plan.rows))
    return pl.pallas_call(
        functools.partial(pack_kernel, plan, levels),
        grid=(plan.group // per_step,),
        out_shape=jax.ShapeDtypeStruct((plan.group, height, levels), BF),
        in_specs=[
            pl.BlockSpec(memory_space=pltpu.SMEM),
            pl.BlockSpec((per_step * plan.rows, 1), lambda k: (k, 0)),
            pl.BlockSpec((slots, columns), lambda k: (0, 0)),
        ],
        out_specs=pl.BlockSpec((per_step, height, levels), lambda k: (k, 0, 0)),
        compiler_params=pltpu.CompilerParams(vmem_limit_bytes=16 * 1024 * 1024),
        cost_estimate=pl.CostEstimate(flops=1, bytes_accessed=1, transcendentals=0),
        name="pack_rows",
    )(lowest, slots_of_rows, control)


def table_kernel(plan, upper_ref, lower_ref, legendre_ref, *refs):
    outs, picks = refs[:2], refs[2:]
    slots = legendre_ref.shape[0]
    even = slots - 1

    @pl.when(pl.program_id(0) == 0)
    def _():
        for index_ref, pick_ref in zip((upper_ref, lower_ref), picks):
            slot = lax.broadcasted_iota(jnp.int32, pick_ref.shape, 0)
            pick_ref[...] = jnp.where(slot == index_ref[...], 1.0, 0.0).astype(BF)

    def times(rows, picked):
        return lax.dot_general(rows, picked, (((0,), (0,)), ((), ())), preferred_element_type=F32)

    for out_ref, pick_ref in zip(outs, picks):
        got = times(legendre_ref[:even, :], pick_ref[:even, :])
        last = jnp.concatenate(
            [legendre_ref[even:slots, :].astype(F32), jnp.zeros((SUB - 1, legendre_ref.shape[1]), F32)], axis=0
        ).astype(BF)
        out_ref[...] = (got + times(last, pick_ref[even:even + SUB, :])).astype(BF)


def make_tables(plan, legendre, slots_of_rows):
    slots, latitudes = legendre.shape
    tile = 256
    index = [rows[None, :width] for rows, width in zip(slots_of_rows, plan.widths)]
    return pl.pallas_call(
        functools.partial(table_kernel, plan),
        grid=(latitudes // tile,),
        out_shape=[jax.ShapeDtypeStruct((latitudes, width), BF) for width in plan.widths],
        in_specs=[pl.BlockSpec((1, width), lambda t: (0, 0)) for width in plan.widths]
        + [pl.BlockSpec((slots, tile), lambda t: (0, t))],
        out_specs=[pl.BlockSpec((tile, width), lambda t: (t, 0)) for width in plan.widths],
        scratch_shapes=[pltpu.VMEM((slots - 1 + SUB, width), BF) for width in plan.widths],
        compiler_params=pltpu.CompilerParams(vmem_limit_bytes=32 * 1024 * 1024),
        cost_estimate=pl.CostEstimate(flops=1, bytes_accessed=1, transcendentals=0),
        name="make_tables",
    )(*index, legendre)


def swap_matrix():
    i = lax.broadcasted_iota(jnp.int32, (SUB * SUB, SUB * SUB), 0)
    j = lax.broadcasted_iota(jnp.int32, (SUB * SUB, SUB * SUB), 1)
    return jnp.where((i // SUB == j % SUB) & (i % SUB == j // SUB), 1.0, 0.0).astype(BF)


def filter_kernel(plan, levels, info_ref, rows_ref, both_ref, out_ref, x_ref, y_ref):
    first_fold = info_ref[0].astype(F32)
    swap = swap_matrix()

    def low_matrix(fold):
        return both_ref[0, fold]

    def high_matrix(fold):
        return both_ref[1, plan.block - 1 - fold]

    def times(rows, matrix):
        return lax.dot_general(rows, matrix, (((1,), (1,)), ((), ())), preferred_element_type=F32)

    def turn(rows):
        return jnp.dot(swap, rows, preferred_element_type=F32)

    for g in range(plan.group // SUB):
        sources = slice(g * SUB, (g + 1) * SUB)
        for r in range(0, plan.rows, SUB):
            parts = []
            for c in range(4):
                start = c * plan.rows + r
                parts.append(rows_ref[sources, start:start + SUB, :].reshape(SUB * SUB, levels))
            x_ref[r * SUB:(r + SUB) * SUB, :] = turn(jnp.concatenate(parts, axis=1)).astype(BF)
        tail = turn(rows_ref[sources, 4 * plan.rows:4 * plan.rows + SUB, :].reshape(SUB * SUB, levels))
        extra = tail[:4 * SUB].astype(BF)
        low = tail[4 * SUB:5 * SUB] * DIGIT + tail[5 * SUB:6 * SUB]
        low = jnp.concatenate([low] * 4, axis=0)
        kept = jnp.zeros((4 * SUB, levels), F32)
        for row0, fold0, count in plan.chunks:
            for i in range(count):
                def stack(row):
                    return jnp.concatenate(
                        [x_ref[row * SUB:(row + 1) * SUB, c * levels:(c + 1) * levels] for c in range(4)], axis=0
                    )

                folded, high = stack(row0 + i), stack(row0 + count + i)
                from_low = times(folded, low_matrix(fold0 + i))
                from_high = times(jnp.concatenate([folded, high, extra], axis=0), high_matrix(fold0 + i))
                fold = first_fold + (fold0 + i)
                mixed = jnp.where(low <= fold, from_low, from_high[:4 * SUB])
                kept = jnp.where(low == fold, from_high[8 * SUB:], kept)
                for row, value in ((row0 + i, mixed), (row0 + count + i, from_high[4 * SUB:8 * SUB])):
                    value = value.astype(BF)
                    for c in range(4):
                        y_ref[row * SUB:(row + 1) * SUB, c * levels:(c + 1) * levels] = value[c * SUB:(c + 1) * SUB]
            unused = ceil_to(2 * count, SUB) - 2 * count
            if unused:
                start = (row0 + 2 * count) * SUB
                y_ref[start:start + unused * SUB, :] = jnp.zeros((unused * SUB, 4 * levels), BF)
        for r in range(0, plan.rows, SUB):
            back = turn(y_ref[r * SUB:(r + SUB) * SUB, :]).astype(BF)
            for c in range(4):
                start = c * plan.rows + r
                out_ref[sources, start:start + SUB, :] = back[:, c * levels:(c + 1) * levels].reshape(
                    SUB, SUB, levels
                )
        filled = jnp.concatenate([kept, jnp.zeros((12 * SUB, levels), F32)], axis=0).astype(BF)
        out_ref[sources, 4 * plan.rows:4 * plan.rows + SUB, :] = turn(filled).astype(BF).reshape(SUB, SUB, levels)


def filter_rows(plan, info, received, both):
    levels = received.shape[2]
    vmem = pl.BlockSpec(memory_space=pltpu.VMEM)
    return pl.pallas_call(
        functools.partial(filter_kernel, plan, levels),
        out_shape=jax.ShapeDtypeStruct(received.shape, BF),
        in_specs=[pl.BlockSpec(memory_space=pltpu.SMEM), vmem, vmem],
        out_specs=vmem,
        scratch_shapes=[
            pltpu.VMEM((plan.rows * SUB, 4 * levels), BF),
            pltpu.VMEM((plan.rows * SUB, 4 * levels), BF),
        ],
        compiler_params=pltpu.CompilerParams(vmem_limit_bytes=20 * 1024 * 1024),
        cost_estimate=pl.CostEstimate(
            flops=2 * plan.group * 16 * plan.block * levels * levels * 4,
            bytes_accessed=2 * 2 * received.size + 4 * plan.block * levels * levels,
            transcendentals=0,
        ),
        name="filter_rows",
    )(info, received, both)


def grid_kernel(plan, levels, latitudes, depth, level_cols, info_ref, starts_ref, bands_ref, part_ref, *refs):
    tables, (out_ref, rows_ref, grid_ref) = refs[:2], refs[2:]
    half, step = pl.program_id(0), pl.program_id(1)
    tile = tables[0].shape[0]

    @pl.when((half == 0) & (step == 0))
    def _():
        base = 0
        for at, first, rows in plan.segments:
            for k in range(plan.group):
                for c in range(4):
                    start = c * plan.rows + plan.chunks[at][0] + first
                    rows_ref[base + k * rows:base + (k + 1) * rows, c * levels:(c + 1) * levels] = part_ref[
                        k, start:start + rows, :
                    ]
            base += plan.group * rows

    @pl.when((half == 1) & (step == 0))
    def _():
        extra = part_ref[info_ref[0], 4 * plan.rows:4 * plan.rows + SUB, :]
        base = info_ref[1] // SUB * SUB
        place = pl.ds(pl.multiple_of(base, SUB), SUB)
        here = lax.broadcasted_iota(jnp.int32, (SUB, levels), 0) == info_ref[1] - base
        for c in range(4):
            cols = slice(c * levels, (c + 1) * levels)
            held = rows_ref[place, cols].astype(F32)
            rows_ref[place, cols] = jnp.where(here, extra[c:c + 1, :].astype(F32), held).astype(BF)

    for at in range(2):
        @pl.when(half == at)
        def _():
            grid_ref[pl.ds(pl.multiple_of(step * tile, tile), tile), :] = jnp.dot(
                tables[at][...], rows_ref[:plan.widths[at], :], preferred_element_type=F32
            )

    @pl.when(step == pl.num_programs(1) - 1)
    def _():
        waves = bands_ref.shape[0]
        groups = 4 * levels // level_cols
        place = lax.broadcasted_iota(jnp.int32, (8, 4 * levels), 0)
        for w in range(waves):
            start = starts_ref[w]
            base = start // 8 * 8
            offset = start - base

            def slab(at):
                held = grid_ref[pl.ds(pl.multiple_of(base + at, 8), 8), :]
                return pltpu.roll(held, (8 - offset) % 8, axis=0)

            after = slab(0)
            done = []
            for r in range(0, depth, 8):
                now, after = after, slab(r + 8)
                got = jnp.where(place < 8 - offset, now, after)
                done.append(jnp.where(place < bands_ref[w] - r, got, 0.0))
                if len(done) == 2 or r + 8 == depth:
                    rows = jnp.concatenate(done, axis=0).astype(BF)
                    first = r + 8 - rows.shape[0]
                    for g in range(groups):
                        out_ref[w * groups + g, 0, first:r + 8, :] = rows[:, g * level_cols:(g + 1) * level_cols]
                    done = []


def to_bands(plan, info, starts, bands, part, tables, depth, level_cols):
    latitudes = tables[0].shape[0]
    levels = part.shape[2]
    columns = 4 * levels
    tile = 512
    steps = latitudes // tile
    smem = pl.BlockSpec(memory_space=pltpu.SMEM)
    messages = bands.shape[0] * columns // level_cols
    return pl.pallas_call(
        functools.partial(grid_kernel, plan, levels, latitudes, depth, level_cols),
        grid=(2, steps),
        out_shape=jax.ShapeDtypeStruct((messages, 2, depth, level_cols), BF),
        in_specs=[
            smem, smem, smem,
            pl.BlockSpec(part.shape, lambda h, t: (0, 0, 0)),
            pl.BlockSpec((tile, plan.widths[0]), lambda h, t: (jnp.where(h == 0, t, steps - 1), 0)),
            pl.BlockSpec((tile, plan.widths[1]), lambda h, t: (jnp.where(h == 0, 0, t), 0)),
        ],
        out_specs=pl.BlockSpec((messages, 1, depth, level_cols), lambda h, t: (0, h, 0, 0)),
        scratch_shapes=[
            pltpu.VMEM((plan.widths[0], columns), BF),
            pltpu.VMEM((ceil_to(latitudes + depth, 8) + 8, columns), F32),
        ],
        compiler_params=pltpu.CompilerParams(vmem_limit_bytes=40 * 1024 * 1024),
        cost_estimate=pl.CostEstimate(
            flops=2 * latitudes * sum(plan.widths) * columns,
            bytes_accessed=2 * latitudes * sum(plan.widths) + 4 * messages * depth * level_cols,
            transcendentals=0,
        ),
        name="grid_bands",
    )(info, starts, bands, part, *tables)


def per_device(control, covariance, legendre, pair_order, band_rows):
    axes = ("wave", "lev")
    waves, lev_count = lax.axis_size("wave"), lax.axis_size("lev")
    _, slots, columns = control.shape
    degrees, levels = slots - 1, columns // 4
    latitudes = legendre.shape[2]
    depth = 5 * latitudes // (4 * waves)
    level_cols = columns // lev_count
    plan = Plan(waves * lev_count, degrees)
    group, block = plan.group, plan.block
    me = lax.axis_index("wave") * lev_count + lax.axis_index("lev")
    is_high = (me >= group).astype(jnp.int32)
    rank = me - group * is_high
    mine = jnp.where(is_high == 1, group - 1 - rank, rank)
    lowest = pair_order[0]
    halves = [list(range(group)), list(range(group, 2 * group))]

    def exchange(rows):
        return lax.all_to_all(rows, axes, split_axis=0, concat_axis=0, tiled=True, axis_index_groups=halves)

    pairs = [[d, 2 * group - 1 - d] for d in range(group)]
    both = lax.all_gather(covariance.astype(BF), axes, axis_index_groups=pairs)

    def slots_of(message, fold, folded, used):
        message = jnp.where(is_high == 1, group - 1 - message, message)
        degree = message * block + fold
        upper = jnp.where(folded, degree - lowest, degrees - 1 - degree - lowest)
        upper = jnp.where(used & (upper >= 0), upper, -1)
        lower = jnp.where(used & folded & (degree <= lowest), degrees - degree, -1)
        return upper, lower

    upper, lower = slots_of(*plan.message_rows())
    sent = jnp.where(upper >= 0, upper, lower)
    received = exchange(pack(plan, control[0], pair_order, sent[:, None]))

    tables = make_tables(plan, legendre[0], slots_of(*plan.transform_rows()))

    info = (mine * block)[None]
    received, tables = lax.optimization_barrier((received, tables))
    filtered = exchange(filter_rows(plan, info, received, both))

    extra_block = lowest // block
    extra_message = jnp.where(is_high == 1, group - 1 - extra_block, extra_block)
    extra_row = plan.extra_row(extra_message, lowest - extra_block * block)
    where = jnp.stack([extra_message, extra_row])
    starts = jnp.cumsum(band_rows) - band_rows
    outgoing = to_bands(plan, where, starts, band_rows, filtered, tables, depth, level_cols)
    outgoing = outgoing.reshape(-1, depth, level_cols)
    return lax.all_to_all(outgoing, axes, split_axis=0, concat_axis=0, tiled=True)


def solution(mesh):
    return jax.shard_map(
        per_device,
        mesh=mesh,
        in_specs=(
            P(("wave", "lev"), None, None),
            P(("wave", "lev"), None, None),
            P(("wave", "lev"), None, None),
            P(("wave", "lev")),
            P(),
        ),
        out_specs=P(None, "wave", "lev"),
        check_vma=False,
    )
```

```python
import functools

import jax
import jax.numpy as jnp
import numpy as np
from jax import lax
from jax.experimental import pallas as pl
from jax.experimental.pallas import tpu as pltpu
from jax.sharding import PartitionSpec as P

BF = jnp.bfloat16
F32 = jnp.float32
SUB = 16
DIGIT = 16


def ceil_to(value, step):
    return (value + step - 1) // step * step


class Plan:
    def __init__(self, devices, degrees):
        self.devices = devices
        self.group = devices // 2
        self.degrees = degrees
        self.block = degrees // devices
        self.chunks = []
        row, fold = 0, 0
        for count in self.fold_counts(self.block):
            self.chunks.append((row, fold, count))
            row += ceil_to(2 * count, SUB)
            fold += count
        self.rows = row
        whole = [(at, n) for at, (_, _, n) in enumerate(self.chunks) if n % SUB == 0]
        mixed = [(at, n) for at, (_, _, n) in enumerate(self.chunks) if n % SUB]
        lower = [(at, 0, n) for at, n in whole] + [(at, 0, ceil_to(2 * n, SUB)) for at, n in mixed]
        self.segments = lower + [(at, n, n) for at, n in whole]
        self.widths = [
            self.group * sum(n for _, _, n in self.segments),
            self.group * sum(n for _, _, n in lower),
        ]

    @staticmethod
    def fold_counts(block):
        return (block - 8, 8) if block % SUB == 8 and block > 8 else (block,)

    def chunk_rows(self, at):
        _, first, count = self.chunks[at]
        height = ceil_to(2 * count, SUB)
        fold = np.zeros(height, np.int32)
        fold[:2 * count] = first + np.tile(np.arange(count), 2)
        row = np.arange(height)
        return fold, row < count, row < 2 * count

    def message_rows(self):
        tables = [self.chunk_rows(at) for at in range(len(self.chunks))]
        one = [np.concatenate(column) for column in zip(*tables)]
        return [np.repeat(np.arange(self.group, dtype=np.int32), self.rows)] + [
            np.tile(column, self.group) for column in one
        ]

    def transform_rows(self):
        parts = []
        for at, first, count in self.segments:
            columns = [column[first:first + count] for column in self.chunk_rows(at)]
            parts.append(
                [np.repeat(np.arange(self.group, dtype=np.int32), count)]
                + [np.tile(column, self.group) for column in columns]
            )
        return [np.concatenate(column) for column in zip(*parts)]

    def extra_row(self, message, fold):
        base, result = 0, jnp.int32(0)
        for at, first, count in self.segments:
            if first == 0:
                start = self.chunks[at][1]
                here = (fold >= start) & (fold < start + self.chunks[at][2])
                result = jnp.where(here, base + message * count + fold - start, result)
            base += self.group * count
        return result


def pack_kernel(plan, levels, info_ref, slot_ref, control_ref, out_ref):
    slots = control_ref.shape[0]
    messages = out_ref.shape[0]
    even = slots - 1
    rows = messages * plan.rows
    slot = slot_ref[...]
    pick = (slot == lax.broadcasted_iota(jnp.int32, (rows, even), 1)).astype(F32).astype(BF)
    got = jnp.dot(pick, control_ref[:even, :], preferred_element_type=F32)
    last = control_ref[even:slots, :].astype(F32)
    got = jnp.where(slot == even, last, got).astype(BF)
    extra_slot = plan.degrees - info_ref[0]
    lane = lax.broadcasted_iota(jnp.int32, (SUB, even), 1)
    first = lax.broadcasted_iota(jnp.int32, (SUB, even), 0) == 0
    choose = jnp.where(first & (lane == extra_slot), 1.0, 0.0).astype(BF)
    extra = jnp.dot(choose, control_ref[:even, :], preferred_element_type=F32)
    extra = jnp.where(extra_slot == even, last, extra)
    place = lax.broadcasted_iota(jnp.int32, (SUB, levels), 0)
    tail = jnp.zeros((SUB, levels), F32)
    for c in range(4):
        tail = jnp.where(place == c, extra[0:1, c * levels:(c + 1) * levels], tail)
    high_digit = (info_ref[0] // DIGIT).astype(F32)
    low_digit = (info_ref[0] % DIGIT).astype(F32)
    tail = jnp.where(place == 4, high_digit, jnp.where(place == 5, low_digit, tail)).astype(BF)
    for k in range(messages):
        for c in range(4):
            out_ref[k, c * plan.rows:(c + 1) * plan.rows, :] = got[
                k * plan.rows:(k + 1) * plan.rows, c * levels:(c + 1) * levels
            ]
        out_ref[k, 4 * plan.rows:, :] = tail


def pack(plan, control, lowest, slots_of_rows):
    slots, columns = control.shape
    levels = columns // 4
    height = 4 * plan.rows + SUB
    per_step = max(1, min(plan.group, 320 // plan.rows))
    return pl.pallas_call(
        functools.partial(pack_kernel, plan, levels),
        grid=(plan.group // per_step,),
        out_shape=jax.ShapeDtypeStruct((plan.group, height, levels), BF),
        in_specs=[
            pl.BlockSpec(memory_space=pltpu.SMEM),
            pl.BlockSpec((per_step * plan.rows, 1), lambda k: (k, 0)),
            pl.BlockSpec((slots, columns), lambda k: (0, 0)),
        ],
        out_specs=pl.BlockSpec((per_step, height, levels), lambda k: (k, 0, 0)),
        compiler_params=pltpu.CompilerParams(vmem_limit_bytes=16 * 1024 * 1024),
        cost_estimate=pl.CostEstimate(flops=1, bytes_accessed=1, transcendentals=0),
        name="pack_rows",
    )(lowest, slots_of_rows, control)


def table_kernel(plan, upper_ref, lower_ref, legendre_ref, *refs):
    outs, picks = refs[:2], refs[2:]
    slots = legendre_ref.shape[0]
    even = slots - 1

    @pl.when(pl.program_id(0) == 0)
    def _():
        for index_ref, pick_ref in zip((upper_ref, lower_ref), picks):
            slot = lax.broadcasted_iota(jnp.int32, pick_ref.shape, 0)
            pick_ref[...] = jnp.where(slot == index_ref[...], 1.0, 0.0).astype(BF)

    def times(rows, picked):
        return lax.dot_general(rows, picked, (((0,), (0,)), ((), ())), preferred_element_type=F32)

    for out_ref, pick_ref in zip(outs, picks):
        got = times(legendre_ref[:even, :], pick_ref[:even, :])
        last = jnp.concatenate(
            [legendre_ref[even:slots, :].astype(F32), jnp.zeros((SUB - 1, legendre_ref.shape[1]), F32)], axis=0
        ).astype(BF)
        out_ref[...] = (got + times(last, pick_ref[even:even + SUB, :])).astype(BF)


def make_tables(plan, legendre, slots_of_rows):
    slots, latitudes = legendre.shape
    tile = 256
    index = [rows[None, :width] for rows, width in zip(slots_of_rows, plan.widths)]
    return pl.pallas_call(
        functools.partial(table_kernel, plan),
        grid=(latitudes // tile,),
        out_shape=[jax.ShapeDtypeStruct((latitudes, width), BF) for width in plan.widths],
        in_specs=[pl.BlockSpec((1, width), lambda t: (0, 0)) for width in plan.widths]
        + [pl.BlockSpec((slots, tile), lambda t: (0, t))],
        out_specs=[pl.BlockSpec((tile, width), lambda t: (t, 0)) for width in plan.widths],
        scratch_shapes=[pltpu.VMEM((slots - 1 + SUB, width), BF) for width in plan.widths],
        compiler_params=pltpu.CompilerParams(vmem_limit_bytes=20 * 1024 * 1024),
        cost_estimate=pl.CostEstimate(
            flops=20 * latitudes * slots * sum(plan.widths), bytes_accessed=2 * legendre.size, transcendentals=0
        ),
        name="make_tables",
    )(*index, legendre)


def swap_matrix():
    i = lax.broadcasted_iota(jnp.int32, (SUB * SUB, SUB * SUB), 0)
    j = lax.broadcasted_iota(jnp.int32, (SUB * SUB, SUB * SUB), 1)
    return jnp.where((i // SUB == j % SUB) & (i % SUB == j // SUB), 1.0, 0.0).astype(BF)


def filter_kernel(plan, levels, pieces, info_ref, rows_ref, *refs):
    own_refs, other_refs, (out_ref, x_ref, y_ref) = refs[:pieces], refs[pieces:2 * pieces], refs[2 * pieces:]
    each = plan.block // pieces
    is_high = info_ref[0] == 1
    first_fold = info_ref[1].astype(F32)
    swap = swap_matrix()

    def low_matrix(fold):
        return jnp.where(is_high, other_refs[fold // each][fold % each], own_refs[fold // each][fold % each])

    def high_matrix(fold):
        at, place = fold // each, each - 1 - fold % each
        return jnp.where(is_high, own_refs[at][place], other_refs[at][place])

    def times(rows, matrix):
        return lax.dot_general(rows, matrix, (((1,), (1,)), ((), ())), preferred_element_type=F32)

    def turn(rows):
        return jnp.dot(swap, rows, preferred_element_type=F32)

    for g in range(plan.group // SUB):
        sources = slice(g * SUB, (g + 1) * SUB)
        for r in range(0, plan.rows, SUB):
            parts = []
            for c in range(4):
                start = c * plan.rows + r
                parts.append(rows_ref[sources, start:start + SUB, :].reshape(SUB * SUB, levels))
            x_ref[r * SUB:(r + SUB) * SUB, :] = turn(jnp.concatenate(parts, axis=1)).astype(BF)
        tail = turn(rows_ref[sources, 4 * plan.rows:4 * plan.rows + SUB, :].reshape(SUB * SUB, levels))
        extra = tail[:4 * SUB].astype(BF)
        low = tail[4 * SUB:5 * SUB] * DIGIT + tail[5 * SUB:6 * SUB]
        low = jnp.concatenate([low] * 4, axis=0)
        kept = jnp.zeros((4 * SUB, levels), F32)
        for row0, fold0, count in plan.chunks:
            for i in range(count):
                def stack(row):
                    return jnp.concatenate(
                        [x_ref[row * SUB:(row + 1) * SUB, c * levels:(c + 1) * levels] for c in range(4)], axis=0
                    )

                folded, high = stack(row0 + i), stack(row0 + count + i)
                from_low = times(folded, low_matrix(fold0 + i))
                from_high = times(jnp.concatenate([folded, high, extra], axis=0), high_matrix(fold0 + i))
                fold = first_fold + (fold0 + i)
                mixed = jnp.where(low <= fold, from_low, from_high[:4 * SUB])
                kept = jnp.where(low == fold, from_high[8 * SUB:], kept)
                for row, value in ((row0 + i, mixed), (row0 + count + i, from_high[4 * SUB:8 * SUB])):
                    value = value.astype(BF)
                    for c in range(4):
                        y_ref[row * SUB:(row + 1) * SUB, c * levels:(c + 1) * levels] = value[c * SUB:(c + 1) * SUB]
            unused = ceil_to(2 * count, SUB) - 2 * count
            if unused:
                start = (row0 + 2 * count) * SUB
                y_ref[start:start + unused * SUB, :] = jnp.zeros((unused * SUB, 4 * levels), BF)
        for r in range(0, plan.rows, SUB):
            back = turn(y_ref[r * SUB:(r + SUB) * SUB, :]).astype(BF)
            for c in range(4):
                start = c * plan.rows + r
                out_ref[sources, start:start + SUB, :] = back[:, c * levels:(c + 1) * levels].reshape(
                    SUB, SUB, levels
                )
        filled = jnp.concatenate([kept, jnp.zeros((12 * SUB, levels), F32)], axis=0).astype(BF)
        out_ref[sources, 4 * plan.rows:4 * plan.rows + SUB, :] = turn(filled).astype(BF).reshape(SUB, SUB, levels)


def filter_rows(plan, info, received, own, other):
    levels = received.shape[2]
    operands = [info, received, *own, *other]
    vmem = pl.BlockSpec(memory_space=pltpu.VMEM)
    return pl.pallas_call(
        functools.partial(filter_kernel, plan, levels, len(own)),
        out_shape=jax.ShapeDtypeStruct(received.shape, BF),
        in_specs=[pl.BlockSpec(memory_space=pltpu.SMEM)] + [vmem] * (len(operands) - 1),
        out_specs=vmem,
        scratch_shapes=[
            pltpu.VMEM((plan.rows * SUB, 4 * levels), BF),
            pltpu.VMEM((plan.rows * SUB, 4 * levels), BF),
        ],
        compiler_params=pltpu.CompilerParams(vmem_limit_bytes=12 * 1024 * 1024),
        cost_estimate=pl.CostEstimate(
            flops=2 * plan.group * 16 * plan.block * levels * levels * 4,
            bytes_accessed=2 * 2 * received.size + 4 * plan.block * levels * levels,
            transcendentals=0,
        ),
        name="filter_rows",
    )(*operands)


def grid_kernel(plan, levels, latitudes, depth, level_cols, info_ref, starts_ref, bands_ref, part_ref, *refs):
    tables, (out_ref, rows_ref, grid_ref) = refs[:2], refs[2:]
    half, step = pl.program_id(0), pl.program_id(1)
    tile = tables[0].shape[0]

    @pl.when((half == 0) & (step == 0))
    def _():
        base = 0
        for at, first, rows in plan.segments:
            for k in range(plan.group):
                for c in range(4):
                    start = c * plan.rows + plan.chunks[at][0] + first
                    rows_ref[base + k * rows:base + (k + 1) * rows, c * levels:(c + 1) * levels] = part_ref[
                        k, start:start + rows, :
                    ]
            base += plan.group * rows

    @pl.when((half == 1) & (step == 0))
    def _():
        extra = part_ref[info_ref[0], 4 * plan.rows:4 * plan.rows + SUB, :]
        base = info_ref[1] // SUB * SUB
        place = pl.ds(pl.multiple_of(base, SUB), SUB)
        here = lax.broadcasted_iota(jnp.int32, (SUB, levels), 0) == info_ref[1] - base
        for c in range(4):
            cols = slice(c * levels, (c + 1) * levels)
            held = rows_ref[place, cols].astype(F32)
            rows_ref[place, cols] = jnp.where(here, extra[c:c + 1, :].astype(F32), held).astype(BF)

    for at in range(2):
        @pl.when(half == at)
        def _():
            grid_ref[pl.ds(pl.multiple_of(step * tile, tile), tile), :] = jnp.dot(
                tables[at][...], rows_ref[:plan.widths[at], :], preferred_element_type=F32
            )

    @pl.when(step == pl.num_programs(1) - 1)
    def _():
        waves = bands_ref.shape[0]
        groups = 4 * levels // level_cols
        place = lax.broadcasted_iota(jnp.int32, (8, 4 * levels), 0)
        for w in range(waves):
            start = starts_ref[w]
            base = start // 8 * 8
            offset = start - base

            def slab(at):
                held = grid_ref[pl.ds(pl.multiple_of(base + at, 8), 8), :]
                return pltpu.roll(held, (8 - offset) % 8, axis=0)

            after = slab(0)
            done = []
            for r in range(0, depth, 8):
                now, after = after, slab(r + 8)
                got = jnp.where(place < 8 - offset, now, after)
                done.append(jnp.where(place < bands_ref[w] - r, got, 0.0))
                if len(done) == 2 or r + 8 == depth:
                    rows = jnp.concatenate(done, axis=0).astype(BF)
                    first = r + 8 - rows.shape[0]
                    for g in range(groups):
                        out_ref[w * groups + g, 0, first:r + 8, :] = rows[:, g * level_cols:(g + 1) * level_cols]
                    done = []


def to_bands(plan, info, starts, bands, part, tables, depth, level_cols):
    latitudes = tables[0].shape[0]
    levels = part.shape[2]
    columns = 4 * levels
    tile = 512
    steps = latitudes // tile
    smem = pl.BlockSpec(memory_space=pltpu.SMEM)
    messages = bands.shape[0] * columns // level_cols
    return pl.pallas_call(
        functools.partial(grid_kernel, plan, levels, latitudes, depth, level_cols),
        grid=(2, steps),
        out_shape=jax.ShapeDtypeStruct((messages, 2, depth, level_cols), BF),
        in_specs=[
            smem, smem, smem,
            pl.BlockSpec(part.shape, lambda h, t: (0, 0, 0)),
            pl.BlockSpec((tile, plan.widths[0]), lambda h, t: (jnp.where(h == 0, t, steps - 1), 0)),
            pl.BlockSpec((tile, plan.widths[1]), lambda h, t: (jnp.where(h == 0, 0, t), 0)),
        ],
        out_specs=pl.BlockSpec((messages, 1, depth, level_cols), lambda h, t: (0, h, 0, 0)),
        scratch_shapes=[
            pltpu.VMEM((plan.widths[0], columns), BF),
            pltpu.VMEM((ceil_to(latitudes + depth, 8) + 8, columns), F32),
        ],
        compiler_params=pltpu.CompilerParams(vmem_limit_bytes=26 * 1024 * 1024),
        cost_estimate=pl.CostEstimate(
            flops=2 * latitudes * sum(plan.widths) * columns,
            bytes_accessed=2 * latitudes * sum(plan.widths) + 4 * messages * depth * level_cols,
            transcendentals=0,
        ),
        name="grid_bands",
    )(info, starts, bands, part, *tables)


def per_device(control, covariance, legendre, pair_order, band_rows):
    axes = ("wave", "lev")
    waves, lev_count = lax.axis_size("wave"), lax.axis_size("lev")
    _, slots, columns = control.shape
    degrees, levels = slots - 1, columns // 4
    latitudes = legendre.shape[2]
    depth = 5 * latitudes // (4 * waves)
    level_cols = columns // lev_count
    plan = Plan(waves * lev_count, degrees)
    group, block = plan.group, plan.block
    me = lax.axis_index("wave") * lev_count + lax.axis_index("lev")
    is_high = (me >= group).astype(jnp.int32)
    rank = me - group * is_high
    mine = jnp.where(is_high == 1, group - 1 - rank, rank)
    lowest = pair_order[0]
    halves = [list(range(group)), list(range(group, 2 * group))]

    def exchange(rows):
        return lax.all_to_all(rows, axes, split_axis=0, concat_axis=0, tiled=True, axis_index_groups=halves)

    mirror = [(d, 2 * group - 1 - d) for d in range(2 * group)]
    pieces = 2 if block % 2 == 0 else 1
    each = block // pieces
    own = []
    for fold in range(0, block, each):
        start = jnp.where(is_high == 1, block - fold - each, fold)
        own.append(lax.dynamic_slice_in_dim(covariance, start, each, 0).astype(BF))
    *own, control = lax.optimization_barrier((*own, control))
    other = [lax.ppermute(piece, axes, mirror) for piece in own]

    def slots_of(message, fold, folded, used):
        message = jnp.where(is_high == 1, group - 1 - message, message)
        degree = message * block + fold
        upper = jnp.where(folded, degree - lowest, degrees - 1 - degree - lowest)
        upper = jnp.where(used & (upper >= 0), upper, -1)
        lower = jnp.where(used & folded & (degree <= lowest), degrees - degree, -1)
        return upper, lower

    upper, lower = slots_of(*plan.message_rows())
    sent = jnp.where(upper >= 0, upper, lower)
    received = exchange(pack(plan, control[0], pair_order, sent[:, None]))

    tables = make_tables(plan, legendre[0], slots_of(*plan.transform_rows()))

    info = jnp.stack([is_high, mine * block])
    received, tables = lax.optimization_barrier((received, tables))
    filtered = exchange(filter_rows(plan, info, received, own, other))

    extra_block = lowest // block
    extra_message = jnp.where(is_high == 1, group - 1 - extra_block, extra_block)
    extra_row = plan.extra_row(extra_message, lowest - extra_block * block)
    where = jnp.stack([extra_message, extra_row])
    starts = jnp.cumsum(band_rows) - band_rows
    outgoing = to_bands(plan, where, starts, band_rows, filtered, tables, depth, level_cols)
    outgoing = outgoing.reshape(-1, depth, level_cols)
    return lax.all_to_all(outgoing, axes, split_axis=0, concat_axis=0, tiled=True)


def solution(mesh):
    return jax.shard_map(
        per_device,
        mesh=mesh,
        in_specs=(
            P(("wave", "lev"), None, None),
            P(("wave", "lev"), None, None),
            P(("wave", "lev"), None, None),
            P(("wave", "lev")),
            P(),
        ),
        out_specs=P(None, "wave", "lev"),
        check_vma=False,
    )
```

```python
import functools

import jax
import jax.numpy as jnp
import numpy as np
from jax import lax
from jax.experimental import pallas as pl
from jax.experimental.pallas import tpu as pltpu
from jax.sharding import PartitionSpec as P

BF = jnp.bfloat16
F32 = jnp.float32
SUB = 16
DIGIT = 16


def ceil_to(value, step):
    return (value + step - 1) // step * step


class Plan:
    def __init__(self, devices, degrees):
        self.devices = devices
        self.group = devices // 2
        self.degrees = degrees
        self.block = degrees // devices
        self.chunks = []
        row, fold = 0, 0
        for count in self.fold_counts(self.block):
            self.chunks.append((row, fold, count))
            row += ceil_to(2 * count, SUB)
            fold += count
        self.rows = row
        whole = [(at, n) for at, (_, _, n) in enumerate(self.chunks) if n % SUB == 0]
        mixed = [(at, n) for at, (_, _, n) in enumerate(self.chunks) if n % SUB]
        lower = [(at, 0, n) for at, n in whole] + [(at, 0, ceil_to(2 * n, SUB)) for at, n in mixed]
        self.segments = lower + [(at, n, n) for at, n in whole]
        self.widths = [
            self.group * sum(n for _, _, n in self.segments),
            self.group * sum(n for _, _, n in lower),
        ]

    @staticmethod
    def fold_counts(block):
        return (block - 8, 8) if block % SUB == 8 and block > 8 else (block,)

    def chunk_rows(self, at):
        _, first, count = self.chunks[at]
        height = ceil_to(2 * count, SUB)
        fold = np.zeros(height, np.int32)
        fold[:2 * count] = first + np.tile(np.arange(count), 2)
        row = np.arange(height)
        return fold, row < count, row < 2 * count

    def message_rows(self):
        tables = [self.chunk_rows(at) for at in range(len(self.chunks))]
        one = [np.concatenate(column) for column in zip(*tables)]
        return [np.repeat(np.arange(self.group, dtype=np.int32), self.rows)] + [
            np.tile(column, self.group) for column in one
        ]

    def transform_rows(self):
        parts = []
        for at, first, count in self.segments:
            columns = [column[first:first + count] for column in self.chunk_rows(at)]
            parts.append(
                [np.repeat(np.arange(self.group, dtype=np.int32), count)]
                + [np.tile(column, self.group) for column in columns]
            )
        return [np.concatenate(column) for column in zip(*parts)]

    def extra_row(self, message, fold):
        base, result = 0, jnp.int32(0)
        for at, first, count in self.segments:
            if first == 0:
                start = self.chunks[at][1]
                here = (fold >= start) & (fold < start + self.chunks[at][2])
                result = jnp.where(here, base + message * count + fold - start, result)
            base += self.group * count
        return result


def pack_kernel(plan, levels, info_ref, slot_ref, control_ref, out_ref):
    slots = control_ref.shape[0]
    messages = out_ref.shape[0]
    even = slots - 1
    rows = messages * plan.rows
    slot = slot_ref[...]
    pick = (slot == lax.broadcasted_iota(jnp.int32, (rows, even), 1)).astype(F32).astype(BF)
    got = jnp.dot(pick, control_ref[:even, :], preferred_element_type=F32)
    last = control_ref[even:slots, :].astype(F32)
    got = jnp.where(slot == even, last, got).astype(BF)
    extra_slot = plan.degrees - info_ref[0]
    lane = lax.broadcasted_iota(jnp.int32, (SUB, even), 1)
    first = lax.broadcasted_iota(jnp.int32, (SUB, even), 0) == 0
    choose = jnp.where(first & (lane == extra_slot), 1.0, 0.0).astype(BF)
    extra = jnp.dot(choose, control_ref[:even, :], preferred_element_type=F32)
    extra = jnp.where(extra_slot == even, last, extra)
    place = lax.broadcasted_iota(jnp.int32, (SUB, levels), 0)
    tail = jnp.zeros((SUB, levels), F32)
    for c in range(4):
        tail = jnp.where(place == c, extra[0:1, c * levels:(c + 1) * levels], tail)
    high_digit = (info_ref[0] // DIGIT).astype(F32)
    low_digit = (info_ref[0] % DIGIT).astype(F32)
    tail = jnp.where(place == 4, high_digit, jnp.where(place == 5, low_digit, tail)).astype(BF)
    for k in range(messages):
        for c in range(4):
            out_ref[k, c * plan.rows:(c + 1) * plan.rows, :] = got[
                k * plan.rows:(k + 1) * plan.rows, c * levels:(c + 1) * levels
            ]
        out_ref[k, 4 * plan.rows:, :] = tail


def pack(plan, control, lowest, slots_of_rows):
    slots, columns = control.shape
    levels = columns // 4
    height = 4 * plan.rows + SUB
    per_step = max(1, min(plan.group, 320 // plan.rows))
    return pl.pallas_call(
        functools.partial(pack_kernel, plan, levels),
        grid=(plan.group // per_step,),
        out_shape=jax.ShapeDtypeStruct((plan.group, height, levels), BF),
        in_specs=[
            pl.BlockSpec(memory_space=pltpu.SMEM),
            pl.BlockSpec((per_step * plan.rows, 1), lambda k: (k, 0)),
            pl.BlockSpec((slots, columns), lambda k: (0, 0)),
        ],
        out_specs=pl.BlockSpec((per_step, height, levels), lambda k: (k, 0, 0)),
        compiler_params=pltpu.CompilerParams(vmem_limit_bytes=16 * 1024 * 1024),
        cost_estimate=pl.CostEstimate(flops=1, bytes_accessed=1, transcendentals=0),
        name="pack_rows",
    )(lowest, slots_of_rows, control)


def table_kernel(plan, upper_ref, lower_ref, legendre_ref, *refs):
    outs, picks = refs[:2], refs[2:]
    slots = legendre_ref.shape[0]
    even = slots - 1

    @pl.when(pl.program_id(0) == 0)
    def _():
        for index_ref, pick_ref in zip((upper_ref, lower_ref), picks):
            slot = lax.broadcasted_iota(jnp.int32, pick_ref.shape, 0)
            pick_ref[...] = jnp.where(slot == index_ref[...], 1.0, 0.0).astype(BF)

    def times(rows, picked):
        return lax.dot_general(rows, picked, (((0,), (0,)), ((), ())), preferred_element_type=F32)

    for out_ref, pick_ref in zip(outs, picks):
        got = times(legendre_ref[:even, :], pick_ref[:even, :])
        last = jnp.concatenate(
            [legendre_ref[even:slots, :].astype(F32), jnp.zeros((SUB - 1, legendre_ref.shape[1]), F32)], axis=0
        ).astype(BF)
        out_ref[...] = (got + times(last, pick_ref[even:even + SUB, :])).astype(BF)


def make_tables(plan, legendre, slots_of_rows):
    slots, latitudes = legendre.shape
    tile = 256
    index = [rows[None, :width] for rows, width in zip(slots_of_rows, plan.widths)]
    return pl.pallas_call(
        functools.partial(table_kernel, plan),
        grid=(latitudes // tile,),
        out_shape=[jax.ShapeDtypeStruct((latitudes, width), BF) for width in plan.widths],
        in_specs=[pl.BlockSpec((1, width), lambda t: (0, 0)) for width in plan.widths]
        + [pl.BlockSpec((slots, tile), lambda t: (0, t))],
        out_specs=[pl.BlockSpec((tile, width), lambda t: (t, 0)) for width in plan.widths],
        scratch_shapes=[pltpu.VMEM((slots - 1 + SUB, width), BF) for width in plan.widths],
        compiler_params=pltpu.CompilerParams(vmem_limit_bytes=20 * 1024 * 1024),
        cost_estimate=pl.CostEstimate(
            flops=20 * latitudes * slots * sum(plan.widths), bytes_accessed=2 * legendre.size, transcendentals=0
        ),
        name="make_tables",
    )(*index, legendre)


def swap_matrix():
    i = lax.broadcasted_iota(jnp.int32, (SUB * SUB, SUB * SUB), 0)
    j = lax.broadcasted_iota(jnp.int32, (SUB * SUB, SUB * SUB), 1)
    return jnp.where((i // SUB == j % SUB) & (i % SUB == j // SUB), 1.0, 0.0).astype(BF)


def filter_kernel(plan, levels, info_ref, rows_ref, near_ref, far_ref, out_ref, x_ref, y_ref):
    is_high = info_ref[0] == 1
    first_fold = info_ref[1].astype(F32)
    swap = swap_matrix()

    def low_matrix(fold):
        return jnp.where(is_high, far_ref[fold], near_ref[fold])

    def high_matrix(fold):
        at = plan.block - 1 - fold
        return jnp.where(is_high, near_ref[at], far_ref[at])

    def times(rows, matrix):
        return lax.dot_general(rows, matrix, (((1,), (1,)), ((), ())), preferred_element_type=F32)

    def turn(rows):
        return jnp.dot(swap, rows, preferred_element_type=F32)

    for g in range(plan.group // SUB):
        sources = slice(g * SUB, (g + 1) * SUB)
        for r in range(0, plan.rows, SUB):
            parts = []
            for c in range(4):
                start = c * plan.rows + r
                parts.append(rows_ref[sources, start:start + SUB, :].reshape(SUB * SUB, levels))
            x_ref[r * SUB:(r + SUB) * SUB, :] = turn(jnp.concatenate(parts, axis=1)).astype(BF)
        tail = turn(rows_ref[sources, 4 * plan.rows:4 * plan.rows + SUB, :].reshape(SUB * SUB, levels))
        extra = tail[:4 * SUB].astype(BF)
        low = tail[4 * SUB:5 * SUB] * DIGIT + tail[5 * SUB:6 * SUB]
        low = jnp.concatenate([low] * 4, axis=0)
        kept = jnp.zeros((4 * SUB, levels), F32)
        for row0, fold0, count in plan.chunks:
            for i in range(count):
                def stack(row):
                    return jnp.concatenate(
                        [x_ref[row * SUB:(row + 1) * SUB, c * levels:(c + 1) * levels] for c in range(4)], axis=0
                    )

                folded, high = stack(row0 + i), stack(row0 + count + i)
                from_low = times(folded, low_matrix(fold0 + i))
                from_high = times(jnp.concatenate([folded, high, extra], axis=0), high_matrix(fold0 + i))
                fold = first_fold + (fold0 + i)
                mixed = jnp.where(low <= fold, from_low, from_high[:4 * SUB])
                kept = jnp.where(low == fold, from_high[8 * SUB:], kept)
                for row, value in ((row0 + i, mixed), (row0 + count + i, from_high[4 * SUB:8 * SUB])):
                    value = value.astype(BF)
                    for c in range(4):
                        y_ref[row * SUB:(row + 1) * SUB, c * levels:(c + 1) * levels] = value[c * SUB:(c + 1) * SUB]
            unused = ceil_to(2 * count, SUB) - 2 * count
            if unused:
                start = (row0 + 2 * count) * SUB
                y_ref[start:start + unused * SUB, :] = jnp.zeros((unused * SUB, 4 * levels), BF)
        for r in range(0, plan.rows, SUB):
            back = turn(y_ref[r * SUB:(r + SUB) * SUB, :]).astype(BF)
            for c in range(4):
                start = c * plan.rows + r
                out_ref[sources, start:start + SUB, :] = back[:, c * levels:(c + 1) * levels].reshape(
                    SUB, SUB, levels
                )
        filled = jnp.concatenate([kept, jnp.zeros((12 * SUB, levels), F32)], axis=0).astype(BF)
        out_ref[sources, 4 * plan.rows:4 * plan.rows + SUB, :] = turn(filled).astype(BF).reshape(SUB, SUB, levels)


def filter_rows(plan, info, received, near_block, far_block):
    levels = received.shape[2]
    vmem = pl.BlockSpec(memory_space=pltpu.VMEM)
    return pl.pallas_call(
        functools.partial(filter_kernel, plan, levels),
        out_shape=jax.ShapeDtypeStruct(received.shape, BF),
        in_specs=[pl.BlockSpec(memory_space=pltpu.SMEM), vmem, vmem, vmem],
        out_specs=vmem,
        scratch_shapes=[
            pltpu.VMEM((plan.rows * SUB, 4 * levels), BF),
            pltpu.VMEM((plan.rows * SUB, 4 * levels), BF),
        ],
        compiler_params=pltpu.CompilerParams(vmem_limit_bytes=12 * 1024 * 1024),
        cost_estimate=pl.CostEstimate(
            flops=2 * plan.group * 16 * plan.block * levels * levels * 4,
            bytes_accessed=2 * 2 * received.size + 4 * plan.block * levels * levels,
            transcendentals=0,
        ),
        name="filter_rows",
    )(info, received, near_block, far_block)


def grid_kernel(plan, levels, latitudes, depth, level_cols, tile, info_ref, starts_ref, bands_ref, part_ref, *refs):
    tables, out_ref, held_tables, (upper_ref, lower_ref, *grids, sems) = refs[:2], refs[2], refs[3:5], refs[5:]
    tiles = [slice(at, at + tile) for at in range(0, latitudes, tile)]

    def copy(half, at):
        rows = tiles[at]
        return pltpu.make_async_copy(tables[half].at[rows], held_tables[half].at[rows], sems.at[half, at])

    for half in range(2):
        for at in range(len(tiles)):
            copy(half, at).start()

    base = 0
    for at, first, rows in plan.segments:
        for k in range(plan.group):
            for c in range(4):
                start = c * plan.rows + plan.chunks[at][0] + first
                cols = slice(c * levels, (c + 1) * levels)
                value = part_ref[k, start:start + rows, :]
                upper_ref[base + k * rows:base + (k + 1) * rows, cols] = value
                if base < plan.widths[1]:
                    lower_ref[base + k * rows:base + (k + 1) * rows, cols] = value
        base += plan.group * rows

    extra = part_ref[info_ref[0], 4 * plan.rows:4 * plan.rows + SUB, :]
    base = info_ref[1] // SUB * SUB
    place = pl.ds(pl.multiple_of(base, SUB), SUB)
    here = lax.broadcasted_iota(jnp.int32, (SUB, levels), 0) == info_ref[1] - base
    for c in range(4):
        cols = slice(c * levels, (c + 1) * levels)
        held = upper_ref[place, cols].astype(F32)
        lower_ref[place, cols] = jnp.where(here, extra[c:c + 1, :].astype(F32), held).astype(BF)

    def transform(half):
        for at, rows in enumerate(tiles):
            copy(half, at).wait()
            grids[half][rows, :] = jnp.dot(
                held_tables[half][rows, :], (upper_ref, lower_ref)[half][...], preferred_element_type=F32
            )

    def cut(half):
        grid_ref = grids[half]
        waves = bands_ref.shape[0]
        groups = 4 * levels // level_cols
        place = lax.broadcasted_iota(jnp.int32, (8, 4 * levels), 0)
        for w in range(waves):
            start = starts_ref[w]
            base = start // 8 * 8
            offset = start - base

            def slab(at):
                held = grid_ref[pl.ds(pl.multiple_of(base + at, 8), 8), :]
                return pltpu.roll(held, (8 - offset) % 8, axis=0)

            after = slab(0)
            done = []
            for r in range(0, depth, 8):
                now, after = after, slab(r + 8)
                got = jnp.where(place < 8 - offset, now, after)
                done.append(jnp.where(place < bands_ref[w] - r, got, 0.0))
                if len(done) == 2 or r + 8 == depth:
                    rows = jnp.concatenate(done, axis=0).astype(BF)
                    first = r + 8 - rows.shape[0]
                    for g in range(groups):
                        out_ref[w * groups + g, half, first:r + 8, :] = rows[:, g * level_cols:(g + 1) * level_cols]
                    done = []

    transform(0)
    cut(0)
    transform(1)
    cut(1)


def to_bands(plan, info, starts, bands, part, tables, depth, level_cols):
    latitudes = tables[0].shape[0]
    levels = part.shape[2]
    columns = 4 * levels
    tile = 512
    smem, vmem = pl.BlockSpec(memory_space=pltpu.SMEM), pl.BlockSpec(memory_space=pltpu.VMEM)
    messages = bands.shape[0] * columns // level_cols
    grid = pltpu.VMEM((ceil_to(latitudes + depth, 8) + 8, columns), F32)
    held = 2 * (latitudes + columns) * sum(plan.widths) + 8 * (latitudes + depth) * columns
    held += 4 * messages * depth * ceil_to(level_cols, 128) + 2 * part.size
    limit = max(52 * 1024 * 1024, held + 4 * 1024 * 1024)
    return pl.pallas_call(
        functools.partial(grid_kernel, plan, levels, latitudes, depth, level_cols, tile),
        out_shape=jax.ShapeDtypeStruct((messages, 2, depth, level_cols), BF),
        in_specs=[smem, smem, smem, vmem] + [pl.BlockSpec(memory_space=pl.ANY)] * 2,
        out_specs=vmem,
        scratch_shapes=[
            pltpu.VMEM(tables[0].shape, BF),
            pltpu.VMEM(tables[1].shape, BF),
            pltpu.VMEM((plan.widths[0], columns), BF),
            pltpu.VMEM((plan.widths[1], columns), BF),
            grid,
            grid,
            pltpu.SemaphoreType.DMA((2, latitudes // tile)),
        ],
        compiler_params=pltpu.CompilerParams(vmem_limit_bytes=limit),
        cost_estimate=pl.CostEstimate(
            flops=2 * latitudes * sum(plan.widths) * columns,
            bytes_accessed=2 * latitudes * sum(plan.widths) + 4 * messages * depth * level_cols,
            transcendentals=0,
        ),
        name="grid_bands",
    )(info, starts, bands, part, *tables)


def per_device(control, covariance, legendre, pair_order, band_rows):
    axes = ("wave", "lev")
    waves, lev_count = lax.axis_size("wave"), lax.axis_size("lev")
    _, slots, columns = control.shape
    degrees, levels = slots - 1, columns // 4
    latitudes = legendre.shape[2]
    depth = 5 * latitudes // (4 * waves)
    level_cols = columns // lev_count
    plan = Plan(waves * lev_count, degrees)
    group, block = plan.group, plan.block
    me = lax.axis_index("wave") * lev_count + lax.axis_index("lev")
    is_high = (me >= group).astype(jnp.int32)
    lowest = pair_order[0]
    halves = [list(range(group)), list(range(group, 2 * group))]

    def exchange(rows):
        return lax.all_to_all(rows, axes, split_axis=0, concat_axis=0, tiled=True, axis_index_groups=halves)

    plane = group // 2
    whole = range(2 * group)
    far = [(d, (3 - d // plane) * plane + d % plane) for d in whole]
    near = [(d, d // plane * plane + plane - 1 - d % plane) for d in whole]
    own = covariance.astype(BF)
    own, control = lax.optimization_barrier((own, control))
    far_block = lax.ppermute(own, axes, far)
    near_block = lax.ppermute(own, axes, near)

    def fold_block(rank):
        rank = jnp.where(is_high == 1, group - 1 - rank, rank)
        return rank // plane * plane + plane - 1 - rank % plane

    def slots_of(message, fold, folded, used):
        degree = fold_block(message) * block + fold
        upper = jnp.where(folded, degree - lowest, degrees - 1 - degree - lowest)
        upper = jnp.where(used & (upper >= 0), upper, -1)
        lower = jnp.where(used & folded & (degree <= lowest), degrees - degree, -1)
        return upper, lower

    upper, lower = slots_of(*plan.message_rows())
    sent = jnp.where(upper >= 0, upper, lower)
    received = exchange(pack(plan, control[0], pair_order, sent[:, None]))

    tables = make_tables(plan, legendre[0], slots_of(*plan.transform_rows()))

    info = jnp.stack([is_high, fold_block(me - group * is_high) * block])
    received, tables = lax.optimization_barrier((received, tables))
    filtered = exchange(filter_rows(plan, info, received, near_block, far_block))

    extra_block = lowest // block
    extra_message = fold_block(extra_block)
    extra_row = plan.extra_row(extra_message, lowest - extra_block * block)
    where = jnp.stack([extra_message, extra_row])
    starts = jnp.cumsum(band_rows) - band_rows
    outgoing = to_bands(plan, where, starts, band_rows, filtered, tables, depth, level_cols)
    outgoing = outgoing.reshape(-1, depth, level_cols)
    return lax.all_to_all(outgoing, axes, split_axis=0, concat_axis=0, tiled=True)


def solution(mesh):
    return jax.shard_map(
        per_device,
        mesh=mesh,
        in_specs=(
            P(("wave", "lev"), None, None),
            P(("wave", "lev"), None, None),
            P(("wave", "lev"), None, None),
            P(("wave", "lev")),
            P(),
        ),
        out_specs=P(None, "wave", "lev"),
        check_vma=False,
    )
```

```python
import functools

import jax
import jax.numpy as jnp
import numpy as np
from jax import lax
from jax.experimental import pallas as pl
from jax.experimental.pallas import tpu as pltpu
from jax.sharding import PartitionSpec as P

BF = jnp.bfloat16
F32 = jnp.float32
SUB = 16
DIGIT = 16


def ceil_to(value, step):
    return (value + step - 1) // step * step


class Plan:
    def __init__(self, devices, degrees):
        self.devices = devices
        self.group = devices // 2
        self.degrees = degrees
        self.block = degrees // devices
        self.chunks = []
        row, fold = 0, 0
        for count in self.fold_counts(self.block):
            self.chunks.append((row, fold, count))
            row += ceil_to(2 * count, SUB)
            fold += count
        self.rows = row
        whole = [(at, n) for at, (_, _, n) in enumerate(self.chunks) if n % SUB == 0]
        mixed = [(at, n) for at, (_, _, n) in enumerate(self.chunks) if n % SUB]
        lower = [(at, 0, n) for at, n in whole] + [(at, 0, ceil_to(2 * n, SUB)) for at, n in mixed]
        self.segments = lower + [(at, n, n) for at, n in whole]
        self.widths = [
            self.group * sum(n for _, _, n in self.segments),
            self.group * sum(n for _, _, n in lower),
        ]

    @staticmethod
    def fold_counts(block):
        return (block - 8, 8) if block % SUB == 8 and block > 8 else (block,)

    def chunk_rows(self, at):
        _, first, count = self.chunks[at]
        height = ceil_to(2 * count, SUB)
        fold = np.zeros(height, np.int32)
        fold[:2 * count] = first + np.tile(np.arange(count), 2)
        row = np.arange(height)
        return fold, row < count, row < 2 * count

    def message_rows(self):
        tables = [self.chunk_rows(at) for at in range(len(self.chunks))]
        one = [np.concatenate(column) for column in zip(*tables)]
        return [np.repeat(np.arange(self.group, dtype=np.int32), self.rows)] + [
            np.tile(column, self.group) for column in one
        ]

    def transform_rows(self):
        parts = []
        for at, first, count in self.segments:
            columns = [column[first:first + count] for column in self.chunk_rows(at)]
            parts.append(
                [np.repeat(np.arange(self.group, dtype=np.int32), count)]
                + [np.tile(column, self.group) for column in columns]
            )
        return [np.concatenate(column) for column in zip(*parts)]

    def extra_row(self, message, fold):
        base, result = 0, jnp.int32(0)
        for at, first, count in self.segments:
            if first == 0:
                start = self.chunks[at][1]
                here = (fold >= start) & (fold < start + self.chunks[at][2])
                result = jnp.where(here, base + message * count + fold - start, result)
            base += self.group * count
        return result


def pack_kernel(plan, levels, info_ref, slot_ref, control_ref, out_ref):
    slots = control_ref.shape[0]
    messages = out_ref.shape[0]
    even = slots - 1
    rows = messages * plan.rows
    slot = slot_ref[...]
    pick = (slot == lax.broadcasted_iota(jnp.int32, (rows, even), 1)).astype(F32).astype(BF)
    got = jnp.dot(pick, control_ref[:even, :], preferred_element_type=F32)
    last = control_ref[even:slots, :].astype(F32)
    got = jnp.where(slot == even, last, got).astype(BF)
    extra_slot = plan.degrees - info_ref[0]
    lane = lax.broadcasted_iota(jnp.int32, (SUB, even), 1)
    first = lax.broadcasted_iota(jnp.int32, (SUB, even), 0) == 0
    choose = jnp.where(first & (lane == extra_slot), 1.0, 0.0).astype(BF)
    extra = jnp.dot(choose, control_ref[:even, :], preferred_element_type=F32)
    extra = jnp.where(extra_slot == even, last, extra)
    place = lax.broadcasted_iota(jnp.int32, (SUB, levels), 0)
    tail = jnp.zeros((SUB, levels), F32)
    for c in range(4):
        tail = jnp.where(place == c, extra[0:1, c * levels:(c + 1) * levels], tail)
    high_digit = (info_ref[0] // DIGIT).astype(F32)
    low_digit = (info_ref[0] % DIGIT).astype(F32)
    tail = jnp.where(place == 4, high_digit, jnp.where(place == 5, low_digit, tail)).astype(BF)
    for k in range(messages):
        for c in range(4):
            out_ref[k, c * plan.rows:(c + 1) * plan.rows, :] = got[
                k * plan.rows:(k + 1) * plan.rows, c * levels:(c + 1) * levels
            ]
        out_ref[k, 4 * plan.rows:, :] = tail


def pack(plan, control, lowest, slots_of_rows):
    slots, columns = control.shape
    levels = columns // 4
    height = 4 * plan.rows + SUB
    per_step = max(1, min(plan.group, 320 // plan.rows))
    return pl.pallas_call(
        functools.partial(pack_kernel, plan, levels),
        grid=(plan.group // per_step,),
        out_shape=jax.ShapeDtypeStruct((plan.group, height, levels), BF),
        in_specs=[
            pl.BlockSpec(memory_space=pltpu.SMEM),
            pl.BlockSpec((per_step * plan.rows, 1), lambda k: (k, 0)),
            pl.BlockSpec((slots, columns), lambda k: (0, 0)),
        ],
        out_specs=pl.BlockSpec((per_step, height, levels), lambda k: (k, 0, 0)),
        compiler_params=pltpu.CompilerParams(vmem_limit_bytes=16 * 1024 * 1024),
        cost_estimate=pl.CostEstimate(flops=1, bytes_accessed=1, transcendentals=0),
        name="pack_rows",
    )(lowest, slots_of_rows, control)


def table_kernel(plan, upper_ref, lower_ref, legendre_ref, *refs):
    outs, picks = refs[:2], refs[2:]
    slots = legendre_ref.shape[0]
    even = slots - 1

    @pl.when(pl.program_id(0) == 0)
    def _():
        for index_ref, pick_ref in zip((upper_ref, lower_ref), picks):
            slot = lax.broadcasted_iota(jnp.int32, pick_ref.shape, 0)
            pick_ref[...] = jnp.where(slot == index_ref[...], 1.0, 0.0).astype(BF)

    def times(rows, picked):
        return lax.dot_general(rows, picked, (((0,), (0,)), ((), ())), preferred_element_type=F32)

    for out_ref, pick_ref in zip(outs, picks):
        got = times(legendre_ref[:even, :], pick_ref[:even, :])
        last = jnp.concatenate(
            [legendre_ref[even:slots, :].astype(F32), jnp.zeros((SUB - 1, legendre_ref.shape[1]), F32)], axis=0
        ).astype(BF)
        out_ref[...] = (got + times(last, pick_ref[even:even + SUB, :])).astype(BF)


def make_tables(plan, legendre, slots_of_rows):
    slots, latitudes = legendre.shape
    tile = 256
    index = [rows[None, :width] for rows, width in zip(slots_of_rows, plan.widths)]
    return pl.pallas_call(
        functools.partial(table_kernel, plan),
        grid=(latitudes // tile,),
        out_shape=[jax.ShapeDtypeStruct((latitudes, width), BF) for width in plan.widths],
        in_specs=[pl.BlockSpec((1, width), lambda t: (0, 0)) for width in plan.widths]
        + [pl.BlockSpec((slots, tile), lambda t: (0, t))],
        out_specs=[pl.BlockSpec((tile, width), lambda t: (t, 0)) for width in plan.widths],
        scratch_shapes=[pltpu.VMEM((slots - 1 + SUB, width), BF) for width in plan.widths],
        compiler_params=pltpu.CompilerParams(vmem_limit_bytes=20 * 1024 * 1024),
        cost_estimate=pl.CostEstimate(
            flops=20 * latitudes * slots * sum(plan.widths), bytes_accessed=2 * legendre.size, transcendentals=0
        ),
        name="make_tables",
    )(*index, legendre)


def swap_matrix():
    i = lax.broadcasted_iota(jnp.int32, (SUB * SUB, SUB * SUB), 0)
    j = lax.broadcasted_iota(jnp.int32, (SUB * SUB, SUB * SUB), 1)
    return jnp.where((i // SUB == j % SUB) & (i % SUB == j // SUB), 1.0, 0.0).astype(BF)


def filter_kernel(plan, levels, info_ref, rows_ref, *refs):
    pieces = len(refs) // 2 - 3
    blocks, out_ref = refs[:pieces], refs[pieces]
    held_blocks, (x_ref, y_ref, z_ref, in_sems, out_sems) = refs[pieces + 1:2 * pieces + 1], refs[2 * pieces + 1:]
    each = blocks[0].shape[0]
    is_high = info_ref[0] == 1
    first_fold = info_ref[1].astype(F32)
    swap = swap_matrix()
    arrivals = [pltpu.make_async_copy(blocks[at], held_blocks[at], in_sems.at[at]) for at in range(pieces)]
    for arrival in arrivals:
        arrival.start()
    near_refs, far_refs = held_blocks[:pieces // 2], held_blocks[pieces // 2:]

    def matrix(refs, fold):
        return refs[fold // each][fold % each]

    def low_matrix(fold):
        return jnp.where(is_high, matrix(far_refs, fold), matrix(near_refs, fold))

    def high_matrix(fold):
        at = plan.block - 1 - fold
        return jnp.where(is_high, matrix(near_refs, at), matrix(far_refs, at))

    def times(rows, matrix):
        return lax.dot_general(rows, matrix, (((1,), (1,)), ((), ())), preferred_element_type=F32)

    def turn(rows):
        return jnp.dot(swap, rows, preferred_element_type=F32)

    groups = plan.group // SUB
    held = plan.rows * SUB
    for g in range(groups):
        sources = slice(g * SUB, (g + 1) * SUB)
        for r in range(0, plan.rows, SUB):
            parts = []
            for c in range(4):
                start = c * plan.rows + r
                parts.append(rows_ref[sources, start:start + SUB, :].reshape(SUB * SUB, levels))
            x_ref[g * held + r * SUB:g * held + (r + SUB) * SUB, :] = turn(jnp.concatenate(parts, axis=1)).astype(BF)

    for arrival in arrivals:
        arrival.wait()

    departures = []

    def send(rows):
        at = len(departures)
        departures.append(pltpu.make_async_copy(z_ref.at[:, rows, :], out_ref.at[:, rows, :], out_sems.at[at]))
        departures[at].start()

    tails = []
    for g in range(groups):
        sources = slice(g * SUB, (g + 1) * SUB)
        tail = turn(rows_ref[sources, 4 * plan.rows:4 * plan.rows + SUB, :].reshape(SUB * SUB, levels))
        low = tail[4 * SUB:5 * SUB] * DIGIT + tail[5 * SUB:6 * SUB]
        tails.append([tail[:4 * SUB].astype(BF), jnp.concatenate([low] * 4, axis=0), jnp.zeros((4 * SUB, levels), F32)])

    for row0, fold0, count in plan.chunks:
        height = ceil_to(2 * count, SUB)
        for g in range(groups):
            sources = slice(g * SUB, (g + 1) * SUB)
            extra, low, kept = tails[g]
            for i in range(count):
                def stack(row):
                    at = g * held + row * SUB
                    return jnp.concatenate(
                        [x_ref[at:at + SUB, c * levels:(c + 1) * levels] for c in range(4)], axis=0
                    )

                folded, high = stack(row0 + i), stack(row0 + count + i)
                from_low = times(folded, low_matrix(fold0 + i))
                from_high = times(jnp.concatenate([folded, high, extra], axis=0), high_matrix(fold0 + i))
                fold = first_fold + (fold0 + i)
                mixed = jnp.where(low <= fold, from_low, from_high[:4 * SUB])
                kept = jnp.where(low == fold, from_high[8 * SUB:], kept)
                for row, value in ((row0 + i, mixed), (row0 + count + i, from_high[4 * SUB:8 * SUB])):
                    value = value.astype(BF)
                    for c in range(4):
                        y_ref[row * SUB:(row + 1) * SUB, c * levels:(c + 1) * levels] = value[c * SUB:(c + 1) * SUB]
            tails[g][2] = kept
            if height > 2 * count:
                y_ref[(row0 + 2 * count) * SUB:(row0 + height) * SUB, :] = jnp.zeros(
                    ((height - 2 * count) * SUB, 4 * levels), BF
                )
            for r in range(row0, row0 + height, SUB):
                back = turn(y_ref[r * SUB:(r + SUB) * SUB, :]).astype(BF)
                for c in range(4):
                    start = c * plan.rows + r
                    z_ref[sources, start:start + SUB, :] = back[:, c * levels:(c + 1) * levels].reshape(
                        SUB, SUB, levels
                    )
        for c in range(4):
            send(pl.ds(c * plan.rows + row0, height))
    for g in range(groups):
        sources = slice(g * SUB, (g + 1) * SUB)
        filled = jnp.concatenate([tails[g][2], jnp.zeros((12 * SUB, levels), F32)], axis=0).astype(BF)
        z_ref[sources, 4 * plan.rows:4 * plan.rows + SUB, :] = turn(filled).astype(BF).reshape(SUB, SUB, levels)
    send(pl.ds(4 * plan.rows, SUB))
    for departure in departures:
        departure.wait()


def filter_rows(plan, info, received, near_blocks, far_blocks):
    levels = received.shape[2]
    blocks = [*near_blocks, *far_blocks]
    smem, vmem = pl.BlockSpec(memory_space=pltpu.SMEM), pl.BlockSpec(memory_space=pltpu.VMEM)
    anywhere = pl.BlockSpec(memory_space=pl.ANY)
    return pl.pallas_call(
        functools.partial(filter_kernel, plan, levels),
        out_shape=jax.ShapeDtypeStruct(received.shape, BF),
        in_specs=[smem, vmem] + [anywhere] * len(blocks),
        out_specs=anywhere,
        scratch_shapes=[pltpu.VMEM(part.shape, BF) for part in blocks]
        + [
            pltpu.VMEM((plan.group * plan.rows, 4 * levels), BF),
            pltpu.VMEM((plan.rows * SUB, 4 * levels), BF),
            pltpu.VMEM(received.shape, BF),
            pltpu.SemaphoreType.DMA((len(blocks),)),
            pltpu.SemaphoreType.DMA((4 * len(plan.chunks) + 1,)),
        ],
        compiler_params=pltpu.CompilerParams(vmem_limit_bytes=20 * 1024 * 1024),
        cost_estimate=pl.CostEstimate(
            flops=2 * plan.group * 16 * plan.block * levels * levels * 4,
            bytes_accessed=2 * 2 * received.size + 4 * plan.block * levels * levels,
            transcendentals=0,
        ),
        name="filter_rows",
    )(info, received, *blocks)


def grid_kernel(plan, levels, latitudes, depth, level_cols, tile, info_ref, starts_ref, bands_ref, part_ref, *refs):
    tables, out_ref, held_tables = refs[:2], refs[2], refs[3:5]
    upper_ref, lower_ref, *grids, cut_ref, sems, out_sems = refs[5:]
    waves = bands_ref.shape[0]
    groups = 4 * levels // level_cols
    tiles = [slice(at, at + tile) for at in range(0, latitudes, tile)]

    def copy(half, at):
        rows = tiles[at]
        return pltpu.make_async_copy(tables[half].at[rows], held_tables[half].at[rows], sems.at[half, at])

    for half in range(2):
        for at in range(len(tiles)):
            copy(half, at).start()

    base = 0
    for at, first, rows in plan.segments:
        for k in range(plan.group):
            for c in range(4):
                start = c * plan.rows + plan.chunks[at][0] + first
                cols = slice(c * levels, (c + 1) * levels)
                value = part_ref[k, start:start + rows, :]
                upper_ref[base + k * rows:base + (k + 1) * rows, cols] = value
                if base < plan.widths[1]:
                    lower_ref[base + k * rows:base + (k + 1) * rows, cols] = value
        base += plan.group * rows

    extra = part_ref[info_ref[0], 4 * plan.rows:4 * plan.rows + SUB, :]
    base = info_ref[1] // SUB * SUB
    place = pl.ds(pl.multiple_of(base, SUB), SUB)
    here = lax.broadcasted_iota(jnp.int32, (SUB, levels), 0) == info_ref[1] - base
    for c in range(4):
        cols = slice(c * levels, (c + 1) * levels)
        held = upper_ref[place, cols].astype(F32)
        lower_ref[place, cols] = jnp.where(here, extra[c:c + 1, :].astype(F32), held).astype(BF)

    def transform(half, at):
        copy(half, at).wait()
        rows = tiles[at]
        grids[half][rows, :] = jnp.dot(
            held_tables[half][rows, :], (upper_ref, lower_ref)[half][...], preferred_element_type=F32
        )

    def departure(half, w):
        messages = pl.ds(w * groups, groups)
        return pltpu.make_async_copy(cut_ref.at[messages, half], out_ref.at[messages, half], out_sems.at[half, w])

    def cut(half, w):
        place = lax.broadcasted_iota(jnp.int32, (8, 4 * levels), 0)
        start = starts_ref[w]
        base = start // 8 * 8
        offset = start - base

        def slab(at):
            held = grids[half][pl.ds(pl.multiple_of(base + at, 8), 8), :]
            return pltpu.roll(held, (8 - offset) % 8, axis=0)

        after = slab(0)
        done = []
        for r in range(0, depth, 8):
            now, after = after, slab(r + 8)
            got = jnp.where(place < 8 - offset, now, after)
            done.append(jnp.where(place < bands_ref[w] - r, got, 0.0))
            if len(done) == 2 or r + 8 == depth:
                rows = jnp.concatenate(done, axis=0).astype(BF)
                first = r + 8 - rows.shape[0]
                for g in range(groups):
                    cut_ref[w * groups + g, half, first:r + 8, :] = rows[:, g * level_cols:(g + 1) * level_cols]
                done = []
        departure(half, w).start()

    for at in range(len(tiles)):
        transform(0, at)
    for at in range(len(tiles)):
        transform(1, at)
        for w in range(at * waves // len(tiles), (at + 1) * waves // len(tiles)):
            cut(0, w)
    for w in range(waves):
        cut(1, w)
    for half in range(2):
        for w in range(waves):
            departure(half, w).wait()


def to_bands(plan, info, starts, bands, part, tables, depth, level_cols):
    latitudes = tables[0].shape[0]
    levels = part.shape[2]
    columns = 4 * levels
    tile = 512
    smem, vmem = pl.BlockSpec(memory_space=pltpu.SMEM), pl.BlockSpec(memory_space=pltpu.VMEM)
    messages = bands.shape[0] * columns // level_cols
    grid = pltpu.VMEM((ceil_to(latitudes + depth, 8) + 8, columns), F32)
    held = 2 * (latitudes + columns) * sum(plan.widths) + 8 * (latitudes + depth) * columns
    held += 4 * messages * depth * ceil_to(level_cols, 128) + 2 * part.size
    limit = max(52 * 1024 * 1024, held + 4 * 1024 * 1024)
    return pl.pallas_call(
        functools.partial(grid_kernel, plan, levels, latitudes, depth, level_cols, tile),
        out_shape=jax.ShapeDtypeStruct((messages, 2, depth, level_cols), BF),
        in_specs=[smem, smem, smem, vmem] + [pl.BlockSpec(memory_space=pl.ANY)] * 2,
        out_specs=pl.BlockSpec(memory_space=pl.ANY),
        scratch_shapes=[
            pltpu.VMEM(tables[0].shape, BF),
            pltpu.VMEM(tables[1].shape, BF),
            pltpu.VMEM((plan.widths[0], columns), BF),
            pltpu.VMEM((plan.widths[1], columns), BF),
            grid,
            grid,
            pltpu.VMEM((messages, 2, depth, level_cols), BF),
            pltpu.SemaphoreType.DMA((2, latitudes // tile)),
            pltpu.SemaphoreType.DMA((2, bands.shape[0])),
        ],
        compiler_params=pltpu.CompilerParams(vmem_limit_bytes=limit),
        cost_estimate=pl.CostEstimate(
            flops=2 * latitudes * sum(plan.widths) * columns,
            bytes_accessed=2 * latitudes * sum(plan.widths) + 4 * messages * depth * level_cols,
            transcendentals=0,
        ),
        name="grid_bands",
    )(info, starts, bands, part, *tables)


def per_device(control, covariance, legendre, pair_order, band_rows):
    axes = ("wave", "lev")
    waves, lev_count = lax.axis_size("wave"), lax.axis_size("lev")
    _, slots, columns = control.shape
    degrees, levels = slots - 1, columns // 4
    latitudes = legendre.shape[2]
    depth = 5 * latitudes // (4 * waves)
    level_cols = columns // lev_count
    plan = Plan(waves * lev_count, degrees)
    group, block = plan.group, plan.block
    me = lax.axis_index("wave") * lev_count + lax.axis_index("lev")
    is_high = (me >= group).astype(jnp.int32)
    lowest = pair_order[0]
    halves = [list(range(group)), list(range(group, 2 * group))]

    def exchange(rows):
        return lax.all_to_all(rows, axes, split_axis=0, concat_axis=0, tiled=True, axis_index_groups=halves)

    plane = group // 2
    whole = range(2 * group)
    far = [(d, (3 - d // plane) * plane + d % plane) for d in whole]
    near = [(d, d // plane * plane + plane - 1 - d % plane) for d in whole]
    pieces = 2 if block % 2 == 0 else 1
    own = [part.astype(BF) for part in jnp.split(covariance, pieces)]
    *own, control = lax.optimization_barrier((*own, control))
    far_blocks = [lax.ppermute(part, axes, far) for part in own]
    near_blocks = [lax.ppermute(part, axes, near) for part in own]

    def fold_block(rank):
        rank = jnp.where(is_high == 1, group - 1 - rank, rank)
        return rank // plane * plane + plane - 1 - rank % plane

    def slots_of(message, fold, folded, used):
        degree = fold_block(message) * block + fold
        upper = jnp.where(folded, degree - lowest, degrees - 1 - degree - lowest)
        upper = jnp.where(used & (upper >= 0), upper, -1)
        lower = jnp.where(used & folded & (degree <= lowest), degrees - degree, -1)
        return upper, lower

    upper, lower = slots_of(*plan.message_rows())
    sent = jnp.where(upper >= 0, upper, lower)
    received = exchange(pack(plan, control[0], pair_order, sent[:, None]))

    tables = make_tables(plan, legendre[0], slots_of(*plan.transform_rows()))

    info = jnp.stack([is_high, fold_block(me - group * is_high) * block])
    received, tables = lax.optimization_barrier((received, tables))
    filtered = exchange(filter_rows(plan, info, received, near_blocks, far_blocks))

    extra_block = lowest // block
    extra_message = fold_block(extra_block)
    extra_row = plan.extra_row(extra_message, lowest - extra_block * block)
    where = jnp.stack([extra_message, extra_row])
    starts = jnp.cumsum(band_rows) - band_rows
    outgoing = to_bands(plan, where, starts, band_rows, filtered, tables, depth, level_cols)
    outgoing = outgoing.reshape(-1, depth, level_cols)
    return lax.all_to_all(outgoing, axes, split_axis=0, concat_axis=0, tiled=True)


def solution(mesh):
    return jax.shard_map(
        per_device,
        mesh=mesh,
        in_specs=(
            P(("wave", "lev"), None, None),
            P(("wave", "lev"), None, None),
            P(("wave", "lev"), None, None),
            P(("wave", "lev")),
            P(),
        ),
        out_specs=P(None, "wave", "lev"),
        check_vma=False,
    )
```

```python
import functools

import jax
import jax.numpy as jnp
import numpy as np
from jax import lax
from jax.experimental import pallas as pl
from jax.experimental.pallas import tpu as pltpu
from jax.sharding import PartitionSpec as P

BF = jnp.bfloat16
F32 = jnp.float32
SUB = 16
DIGIT = 16


def ceil_to(value, step):
    return (value + step - 1) // step * step


class Plan:
    def __init__(self, devices, degrees):
        self.devices = devices
        self.group = devices // 2
        self.degrees = degrees
        self.block = degrees // devices
        self.chunks = []
        row, fold = 0, 0
        for count in self.fold_counts(self.block):
            self.chunks.append((row, fold, count))
            row += ceil_to(2 * count, SUB)
            fold += count
        self.rows = row
        whole = [(at, n) for at, (_, _, n) in enumerate(self.chunks) if n % SUB == 0]
        mixed = [(at, n) for at, (_, _, n) in enumerate(self.chunks) if n % SUB]
        lower = [(at, 0, n) for at, n in whole] + [(at, 0, ceil_to(2 * n, SUB)) for at, n in mixed]
        self.segments = lower + [(at, n, n) for at, n in whole]
        self.widths = [
            self.group * sum(n for _, _, n in self.segments),
            self.group * sum(n for _, _, n in lower),
        ]

    @staticmethod
    def fold_counts(block):
        return (block - 8, 8) if block % SUB == 8 and block > 8 else (block,)

    def chunk_rows(self, at):
        _, first, count = self.chunks[at]
        height = ceil_to(2 * count, SUB)
        fold = np.zeros(height, np.int32)
        fold[:2 * count] = first + np.tile(np.arange(count), 2)
        row = np.arange(height)
        return fold, row < count, row < 2 * count

    def message_rows(self):
        tables = [self.chunk_rows(at) for at in range(len(self.chunks))]
        one = [np.concatenate(column) for column in zip(*tables)]
        return [np.repeat(np.arange(self.group, dtype=np.int32), self.rows)] + [
            np.tile(column, self.group) for column in one
        ]

    def transform_rows(self):
        parts = []
        for at, first, count in self.segments:
            columns = [column[first:first + count] for column in self.chunk_rows(at)]
            parts.append(
                [np.repeat(np.arange(self.group, dtype=np.int32), count)]
                + [np.tile(column, self.group) for column in columns]
            )
        return [np.concatenate(column) for column in zip(*parts)]

    def extra_row(self, message, fold):
        base, result = 0, jnp.int32(0)
        for at, first, count in self.segments:
            if first == 0:
                start = self.chunks[at][1]
                here = (fold >= start) & (fold < start + self.chunks[at][2])
                result = jnp.where(here, base + message * count + fold - start, result)
            base += self.group * count
        return result


def pack_kernel(plan, levels, info_ref, slot_ref, control_ref, out_ref):
    slots = control_ref.shape[0]
    messages = out_ref.shape[0]
    even = slots - 1
    rows = messages * plan.rows
    slot = slot_ref[...]
    pick = (slot == lax.broadcasted_iota(jnp.int32, (rows, even), 1)).astype(F32).astype(BF)
    got = jnp.dot(pick, control_ref[:even, :], preferred_element_type=F32)
    last = control_ref[even:slots, :].astype(F32)
    got = jnp.where(slot == even, last, got).astype(BF)
    extra_slot = plan.degrees - info_ref[0]
    lane = lax.broadcasted_iota(jnp.int32, (SUB, even), 1)
    first = lax.broadcasted_iota(jnp.int32, (SUB, even), 0) == 0
    choose = jnp.where(first & (lane == extra_slot), 1.0, 0.0).astype(BF)
    extra = jnp.dot(choose, control_ref[:even, :], preferred_element_type=F32)
    extra = jnp.where(extra_slot == even, last, extra)
    place = lax.broadcasted_iota(jnp.int32, (SUB, levels), 0)
    tail = jnp.zeros((SUB, levels), F32)
    for c in range(4):
        tail = jnp.where(place == c, extra[0:1, c * levels:(c + 1) * levels], tail)
    high_digit = (info_ref[0] // DIGIT).astype(F32)
    low_digit = (info_ref[0] % DIGIT).astype(F32)
    tail = jnp.where(place == 4, high_digit, jnp.where(place == 5, low_digit, tail)).astype(BF)
    for k in range(messages):
        for c in range(4):
            out_ref[k, c * plan.rows:(c + 1) * plan.rows, :] = got[
                k * plan.rows:(k + 1) * plan.rows, c * levels:(c + 1) * levels
            ]
        out_ref[k, 4 * plan.rows:, :] = tail


def pack(plan, control, lowest, slots_of_rows):
    slots, columns = control.shape
    levels = columns // 4
    height = 4 * plan.rows + SUB
    per_step = max(1, min(plan.group, 320 // plan.rows))
    return pl.pallas_call(
        functools.partial(pack_kernel, plan, levels),
        grid=(plan.group // per_step,),
        out_shape=jax.ShapeDtypeStruct((plan.group, height, levels), BF),
        in_specs=[
            pl.BlockSpec(memory_space=pltpu.SMEM),
            pl.BlockSpec((per_step * plan.rows, 1), lambda k: (k, 0)),
            pl.BlockSpec((slots, columns), lambda k: (0, 0)),
        ],
        out_specs=pl.BlockSpec((per_step, height, levels), lambda k: (k, 0, 0)),
        compiler_params=pltpu.CompilerParams(vmem_limit_bytes=16 * 1024 * 1024),
        cost_estimate=pl.CostEstimate(flops=1, bytes_accessed=1, transcendentals=0),
        name="pack_rows",
    )(lowest, slots_of_rows, control)


def table_kernel(plan, upper_ref, lower_ref, legendre_ref, *refs):
    outs, picks = refs[:2], refs[2:]
    slots = legendre_ref.shape[0]
    even = slots - 1

    @pl.when(pl.program_id(0) == 0)
    def _():
        for index_ref, pick_ref in zip((upper_ref, lower_ref), picks):
            slot = lax.broadcasted_iota(jnp.int32, pick_ref.shape, 0)
            pick_ref[...] = jnp.where(slot == index_ref[...], 1.0, 0.0).astype(BF)

    def times(rows, picked):
        return lax.dot_general(rows, picked, (((0,), (0,)), ((), ())), preferred_element_type=F32)

    for out_ref, pick_ref in zip(outs, picks):
        got = times(legendre_ref[:even, :], pick_ref[:even, :])
        last = jnp.concatenate(
            [legendre_ref[even:slots, :].astype(F32), jnp.zeros((SUB - 1, legendre_ref.shape[1]), F32)], axis=0
        ).astype(BF)
        out_ref[...] = (got + times(last, pick_ref[even:even + SUB, :])).astype(BF)


def make_tables(plan, legendre, slots_of_rows):
    slots, latitudes = legendre.shape
    tile = 256
    index = [rows[None, :width] for rows, width in zip(slots_of_rows, plan.widths)]
    return pl.pallas_call(
        functools.partial(table_kernel, plan),
        grid=(latitudes // tile,),
        out_shape=[jax.ShapeDtypeStruct((latitudes, width), BF) for width in plan.widths],
        in_specs=[pl.BlockSpec((1, width), lambda t: (0, 0)) for width in plan.widths]
        + [pl.BlockSpec((slots, tile), lambda t: (0, t))],
        out_specs=[pl.BlockSpec((tile, width), lambda t: (t, 0)) for width in plan.widths],
        scratch_shapes=[pltpu.VMEM((slots - 1 + SUB, width), BF) for width in plan.widths],
        compiler_params=pltpu.CompilerParams(vmem_limit_bytes=20 * 1024 * 1024),
        cost_estimate=pl.CostEstimate(
            flops=20 * latitudes * slots * sum(plan.widths), bytes_accessed=2 * legendre.size, transcendentals=0
        ),
        name="make_tables",
    )(*index, legendre)


def swap_matrix():
    i = lax.broadcasted_iota(jnp.int32, (SUB * SUB, SUB * SUB), 0)
    j = lax.broadcasted_iota(jnp.int32, (SUB * SUB, SUB * SUB), 1)
    return jnp.where((i // SUB == j % SUB) & (i % SUB == j // SUB), 1.0, 0.0).astype(BF)


def filter_kernel(plan, levels, info_ref, rows_ref, *refs):
    pieces = len(refs) // 2 - 3
    blocks, out_ref = refs[:pieces], refs[pieces]
    held_blocks, (x_ref, y_ref, z_ref, in_sems, out_sems) = refs[pieces + 1:2 * pieces + 1], refs[2 * pieces + 1:]
    each = blocks[0].shape[0]
    is_high = info_ref[0] == 1
    first_fold = info_ref[1].astype(F32)
    swap = swap_matrix()
    arrivals = [pltpu.make_async_copy(blocks[at], held_blocks[at], in_sems.at[at]) for at in range(pieces)]
    for arrival in arrivals:
        arrival.start()
    near_refs, far_refs = held_blocks[:pieces // 2], held_blocks[pieces // 2:]

    def low_matrix(fold):
        piece, at = fold // each, fold % each
        return jnp.where(is_high, far_refs[piece][at], near_refs[piece][at])

    def high_matrix(fold):
        piece, at = fold // each, each - 1 - fold % each
        return jnp.where(is_high, near_refs[piece][at], far_refs[piece][at])

    def times(rows, matrix):
        return lax.dot_general(rows, matrix, (((1,), (1,)), ((), ())), preferred_element_type=F32)

    def turn(rows):
        return jnp.dot(swap, rows, preferred_element_type=F32)

    groups = plan.group // SUB
    held = plan.rows * SUB
    for g in range(groups):
        sources = slice(g * SUB, (g + 1) * SUB)
        for r in range(0, plan.rows, SUB):
            parts = []
            for c in range(4):
                start = c * plan.rows + r
                parts.append(rows_ref[sources, start:start + SUB, :].reshape(SUB * SUB, levels))
            x_ref[g * held + r * SUB:g * held + (r + SUB) * SUB, :] = turn(jnp.concatenate(parts, axis=1)).astype(BF)

    for arrival in arrivals:
        arrival.wait()

    departures = []

    def send(rows):
        at = len(departures)
        departures.append(pltpu.make_async_copy(z_ref.at[:, rows, :], out_ref.at[:, rows, :], out_sems.at[at]))
        departures[at].start()

    tails = []
    for g in range(groups):
        sources = slice(g * SUB, (g + 1) * SUB)
        tail = turn(rows_ref[sources, 4 * plan.rows:4 * plan.rows + SUB, :].reshape(SUB * SUB, levels))
        low = tail[4 * SUB:5 * SUB] * DIGIT + tail[5 * SUB:6 * SUB]
        tails.append([tail[:4 * SUB].astype(BF), jnp.concatenate([low] * 4, axis=0), jnp.zeros((4 * SUB, levels), F32)])

    for row0, fold0, count in plan.chunks:
        height = ceil_to(2 * count, SUB)
        for g in range(groups):
            sources = slice(g * SUB, (g + 1) * SUB)
            extra, low, kept = tails[g]
            for i in range(count):
                def stack(row):
                    at = g * held + row * SUB
                    return jnp.concatenate(
                        [x_ref[at:at + SUB, c * levels:(c + 1) * levels] for c in range(4)], axis=0
                    )

                folded, high = stack(row0 + i), stack(row0 + count + i)
                from_low = times(folded, low_matrix(fold0 + i))
                from_high = times(jnp.concatenate([folded, high, extra], axis=0), high_matrix(fold0 + i))
                fold = first_fold + (fold0 + i)
                mixed = jnp.where(low <= fold, from_low, from_high[:4 * SUB])
                kept = jnp.where(low == fold, from_high[8 * SUB:], kept)
                for row, value in ((row0 + i, mixed), (row0 + count + i, from_high[4 * SUB:8 * SUB])):
                    value = value.astype(BF)
                    for c in range(4):
                        y_ref[row * SUB:(row + 1) * SUB, c * levels:(c + 1) * levels] = value[c * SUB:(c + 1) * SUB]
            tails[g][2] = kept
            if height > 2 * count:
                y_ref[(row0 + 2 * count) * SUB:(row0 + height) * SUB, :] = jnp.zeros(
                    ((height - 2 * count) * SUB, 4 * levels), BF
                )
            for r in range(row0, row0 + height, SUB):
                back = turn(y_ref[r * SUB:(r + SUB) * SUB, :]).astype(BF)
                for c in range(4):
                    start = c * plan.rows + r
                    z_ref[sources, start:start + SUB, :] = back[:, c * levels:(c + 1) * levels].reshape(
                        SUB, SUB, levels
                    )
        for c in range(4):
            send(pl.ds(c * plan.rows + row0, height))
    for g in range(groups):
        sources = slice(g * SUB, (g + 1) * SUB)
        filled = jnp.concatenate([tails[g][2], jnp.zeros((12 * SUB, levels), F32)], axis=0).astype(BF)
        z_ref[sources, 4 * plan.rows:4 * plan.rows + SUB, :] = turn(filled).astype(BF).reshape(SUB, SUB, levels)
    send(pl.ds(4 * plan.rows, SUB))
    for departure in departures:
        departure.wait()


def filter_rows(plan, info, received, near_blocks, far_blocks):
    levels = received.shape[2]
    blocks = [*near_blocks, *far_blocks]
    smem, vmem = pl.BlockSpec(memory_space=pltpu.SMEM), pl.BlockSpec(memory_space=pltpu.VMEM)
    anywhere = pl.BlockSpec(memory_space=pl.ANY)
    return pl.pallas_call(
        functools.partial(filter_kernel, plan, levels),
        out_shape=jax.ShapeDtypeStruct(received.shape, BF),
        in_specs=[smem, vmem] + [anywhere] * len(blocks),
        out_specs=anywhere,
        scratch_shapes=[pltpu.VMEM(part.shape, BF) for part in blocks]
        + [
            pltpu.VMEM((plan.group * plan.rows, 4 * levels), BF),
            pltpu.VMEM((plan.rows * SUB, 4 * levels), BF),
            pltpu.VMEM(received.shape, BF),
            pltpu.SemaphoreType.DMA((len(blocks),)),
            pltpu.SemaphoreType.DMA((4 * len(plan.chunks) + 1,)),
        ],
        compiler_params=pltpu.CompilerParams(vmem_limit_bytes=20 * 1024 * 1024),
        cost_estimate=pl.CostEstimate(
            flops=2 * plan.group * 16 * plan.block * levels * levels * 4,
            bytes_accessed=2 * 2 * received.size + 4 * plan.block * levels * levels,
            transcendentals=0,
        ),
        name="filter_rows",
    )(info, received, *blocks)


def grid_kernel(plan, levels, latitudes, depth, level_cols, tile, info_ref, starts_ref, bands_ref, part_ref, *refs):
    tables, out_ref, held_tables = refs[:2], refs[2], refs[3:5]
    upper_ref, lower_ref, *grids, cut_ref, sems, out_sems = refs[5:]
    waves = bands_ref.shape[0]
    groups = 4 * levels // level_cols
    tiles = [slice(start, stop) for start, stop in zip(tile, tile[1:])]

    def copy(half, at):
        rows = tiles[at]
        return pltpu.make_async_copy(tables[half].at[rows], held_tables[half].at[rows], sems.at[half, at])

    for half in (1, 0):
        for at in range(len(tiles)):
            copy(half, at).start()

    base = 0
    for at, first, rows in plan.segments:
        for k in range(plan.group):
            for c in range(4):
                start = c * plan.rows + plan.chunks[at][0] + first
                cols = slice(c * levels, (c + 1) * levels)
                value = part_ref[k, start:start + rows, :]
                upper_ref[base + k * rows:base + (k + 1) * rows, cols] = value
                if base < plan.widths[1]:
                    lower_ref[base + k * rows:base + (k + 1) * rows, cols] = value
        base += plan.group * rows

    extra = part_ref[info_ref[0], 4 * plan.rows:4 * plan.rows + SUB, :]
    base = info_ref[1] // SUB * SUB
    place = pl.ds(pl.multiple_of(base, SUB), SUB)
    here = lax.broadcasted_iota(jnp.int32, (SUB, levels), 0) == info_ref[1] - base
    for c in range(4):
        cols = slice(c * levels, (c + 1) * levels)
        held = upper_ref[place, cols].astype(F32)
        lower_ref[place, cols] = jnp.where(here, extra[c:c + 1, :].astype(F32), held).astype(BF)

    def transform(half, at):
        copy(half, at).wait()
        rows = tiles[at]
        grids[half][rows, :] = jnp.dot(
            held_tables[half][rows, :], (upper_ref, lower_ref)[half][...], preferred_element_type=F32
        )

    def departure(half, w):
        messages = pl.ds(w * groups, groups)
        return pltpu.make_async_copy(cut_ref.at[messages, half], out_ref.at[messages, half], out_sems.at[half, w])

    def cut(half, w):
        place = lax.broadcasted_iota(jnp.int32, (8, 4 * levels), 0)
        start = starts_ref[w]
        base = start // 8 * 8
        offset = start - base

        def slab(at):
            held = grids[half][pl.ds(pl.multiple_of(base + at, 8), 8), :]
            return pltpu.roll(held, (8 - offset) % 8, axis=0)

        after = slab(0)
        done = []
        for r in range(0, depth, 8):
            now, after = after, slab(r + 8)
            got = jnp.where(place < 8 - offset, now, after)
            done.append(jnp.where(place < bands_ref[w] - r, got, 0.0))
            if len(done) == 2 or r + 8 == depth:
                rows = jnp.concatenate(done, axis=0).astype(BF)
                first = r + 8 - rows.shape[0]
                for g in range(groups):
                    cut_ref[w * groups + g, half, first:r + 8, :] = rows[:, g * level_cols:(g + 1) * level_cols]
                done = []
        departure(half, w).start()

    for at in range(len(tiles)):
        transform(1, at)
    for at in range(len(tiles)):
        transform(0, at)
        for w in range(at * waves // len(tiles), (at + 1) * waves // len(tiles)):
            cut(1, w)
    for w in range(waves):
        cut(0, w)
    for half in range(2):
        for w in range(waves):
            departure(half, w).wait()


def to_bands(plan, info, starts, bands, part, tables, depth, level_cols):
    latitudes = tables[0].shape[0]
    levels = part.shape[2]
    columns = 4 * levels
    tile = [0] + list(range(latitudes // 5, latitudes + 1, 2 * latitudes // 5))
    smem, vmem = pl.BlockSpec(memory_space=pltpu.SMEM), pl.BlockSpec(memory_space=pltpu.VMEM)
    messages = bands.shape[0] * columns // level_cols
    grid = pltpu.VMEM((ceil_to(latitudes + depth, 8) + 8, columns), F32)
    held = 2 * (latitudes + columns) * sum(plan.widths) + 8 * (latitudes + depth) * columns
    held += 4 * messages * depth * ceil_to(level_cols, 128) + 2 * part.size
    limit = max(52 * 1024 * 1024, held + 4 * 1024 * 1024)
    return pl.pallas_call(
        functools.partial(grid_kernel, plan, levels, latitudes, depth, level_cols, tile),
        out_shape=jax.ShapeDtypeStruct((messages, 2, depth, level_cols), BF),
        in_specs=[smem, smem, smem, vmem] + [pl.BlockSpec(memory_space=pl.ANY)] * 2,
        out_specs=pl.BlockSpec(memory_space=pl.ANY),
        scratch_shapes=[
            pltpu.VMEM(tables[0].shape, BF),
            pltpu.VMEM(tables[1].shape, BF),
            pltpu.VMEM((plan.widths[0], columns), BF),
            pltpu.VMEM((plan.widths[1], columns), BF),
            grid,
            grid,
            pltpu.VMEM((messages, 2, depth, level_cols), BF),
            pltpu.SemaphoreType.DMA((2, len(tile) - 1)),
            pltpu.SemaphoreType.DMA((2, bands.shape[0])),
        ],
        compiler_params=pltpu.CompilerParams(vmem_limit_bytes=limit),
        cost_estimate=pl.CostEstimate(
            flops=2 * latitudes * sum(plan.widths) * columns,
            bytes_accessed=2 * latitudes * sum(plan.widths) + 4 * messages * depth * level_cols,
            transcendentals=0,
        ),
        name="grid_bands",
    )(info, starts, bands, part, *tables)


def per_device(control, covariance, legendre, pair_order, band_rows):
    axes = ("wave", "lev")
    waves, lev_count = lax.axis_size("wave"), lax.axis_size("lev")
    _, slots, columns = control.shape
    degrees, levels = slots - 1, columns // 4
    latitudes = legendre.shape[2]
    depth = 5 * latitudes // (4 * waves)
    level_cols = columns // lev_count
    plan = Plan(waves * lev_count, degrees)
    group, block = plan.group, plan.block
    me = lax.axis_index("wave") * lev_count + lax.axis_index("lev")
    is_high = (me >= group).astype(jnp.int32)
    lowest = pair_order[0]
    halves = [list(range(group)), list(range(group, 2 * group))]

    def exchange(rows):
        return lax.all_to_all(rows, axes, split_axis=0, concat_axis=0, tiled=True, axis_index_groups=halves)

    plane = group // 2
    whole = range(2 * group)
    far = [(d, (3 - d // plane) * plane + d % plane) for d in whole]
    near = [(d, d // plane * plane + plane - 1 - d % plane) for d in whole]
    pieces = 2 if block % 2 == 0 else 1
    each = block // pieces
    own = []
    for fold in range(0, block, each):
        start = jnp.where(is_high == 1, block - fold - each, fold)
        own.append(lax.dynamic_slice_in_dim(covariance, start, each, 0).astype(BF))
    *own, control = lax.optimization_barrier((*own, control))
    far_blocks = [lax.ppermute(part, axes, far) for part in own]
    near_blocks = [lax.ppermute(part, axes, near) for part in own]

    def fold_block(rank):
        rank = jnp.where(is_high == 1, group - 1 - rank, rank)
        return rank // plane * plane + plane - 1 - rank % plane

    def slots_of(message, fold, folded, used):
        degree = fold_block(message) * block + fold
        upper = jnp.where(folded, degree - lowest, degrees - 1 - degree - lowest)
        upper = jnp.where(used & (upper >= 0), upper, -1)
        lower = jnp.where(used & folded & (degree <= lowest), degrees - degree, -1)
        return upper, lower

    upper, lower = slots_of(*plan.message_rows())
    sent = jnp.where(upper >= 0, upper, lower)
    received = exchange(pack(plan, control[0], pair_order, sent[:, None]))

    tables = make_tables(plan, legendre[0], slots_of(*plan.transform_rows()))

    info = jnp.stack([is_high, fold_block(me - group * is_high) * block])
    received, tables = lax.optimization_barrier((received, tables))
    filtered = exchange(filter_rows(plan, info, received, near_blocks, far_blocks))

    extra_block = lowest // block
    extra_message = fold_block(extra_block)
    extra_row = plan.extra_row(extra_message, lowest - extra_block * block)
    where = jnp.stack([extra_message, extra_row])
    starts = jnp.cumsum(band_rows) - band_rows
    outgoing = to_bands(plan, where, starts, band_rows, filtered, tables, depth, level_cols)
    outgoing = outgoing.reshape(-1, depth, level_cols)
    return lax.all_to_all(outgoing, axes, split_axis=0, concat_axis=0, tiled=True)


def solution(mesh):
    return jax.shard_map(
        per_device,
        mesh=mesh,
        in_specs=(
            P(("wave", "lev"), None, None),
            P(("wave", "lev"), None, None),
            P(("wave", "lev"), None, None),
            P(("wave", "lev")),
            P(),
        ),
        out_specs=P(None, "wave", "lev"),
        check_vma=False,
    )
```

```python
import functools

import jax
import jax.numpy as jnp
import numpy as np
from jax import lax
from jax.experimental import pallas as pl
from jax.experimental.pallas import tpu as pltpu
from jax.sharding import PartitionSpec as P

BF = jnp.bfloat16
F32 = jnp.float32
SUB = 16
DIGIT = 16


def ceil_to(value, step):
    return (value + step - 1) // step * step


class Plan:
    def __init__(self, devices, degrees):
        self.devices = devices
        self.group = devices // 2
        self.degrees = degrees
        self.block = degrees // devices
        self.chunks = []
        row, fold = 0, 0
        for count in self.fold_counts(self.block):
            self.chunks.append((row, fold, count))
            row += ceil_to(2 * count, SUB)
            fold += count
        self.rows = row
        whole = [(at, n) for at, (_, _, n) in enumerate(self.chunks) if n % SUB == 0]
        mixed = [(at, n) for at, (_, _, n) in enumerate(self.chunks) if n % SUB]
        lower = [(at, 0, n) for at, n in whole] + [(at, 0, ceil_to(2 * n, SUB)) for at, n in mixed]
        self.segments = lower + [(at, n, n) for at, n in whole]
        self.widths = [
            self.group * sum(n for _, _, n in self.segments),
            self.group * sum(n for _, _, n in lower),
        ]

    @staticmethod
    def fold_counts(block):
        return (block - 8, 8) if block % SUB == 8 and block > 8 else (block,)

    def chunk_rows(self, at):
        _, first, count = self.chunks[at]
        height = ceil_to(2 * count, SUB)
        fold = np.zeros(height, np.int32)
        fold[:2 * count] = first + np.tile(np.arange(count), 2)
        row = np.arange(height)
        return fold, row < count, row < 2 * count

    def message_rows(self):
        tables = [self.chunk_rows(at) for at in range(len(self.chunks))]
        one = [np.concatenate(column) for column in zip(*tables)]
        return [np.repeat(np.arange(self.group, dtype=np.int32), self.rows)] + [
            np.tile(column, self.group) for column in one
        ]

    def transform_rows(self):
        parts = []
        for at, first, count in self.segments:
            columns = [column[first:first + count] for column in self.chunk_rows(at)]
            parts.append(
                [np.repeat(np.arange(self.group, dtype=np.int32), count)]
                + [np.tile(column, self.group) for column in columns]
            )
        return [np.concatenate(column) for column in zip(*parts)]

    def extra_row(self, message, fold):
        base, result = 0, jnp.int32(0)
        for at, first, count in self.segments:
            if first == 0:
                start = self.chunks[at][1]
                here = (fold >= start) & (fold < start + self.chunks[at][2])
                result = jnp.where(here, base + message * count + fold - start, result)
            base += self.group * count
        return result


def pack_kernel(plan, levels, info_ref, slot_ref, control_ref, out_ref):
    slots = control_ref.shape[0]
    messages = out_ref.shape[0]
    even = slots - 1
    rows = messages * plan.rows
    slot = slot_ref[...]
    pick = (slot == lax.broadcasted_iota(jnp.int32, (rows, even), 1)).astype(F32).astype(BF)
    got = jnp.dot(pick, control_ref[:even, :], preferred_element_type=F32)
    last = control_ref[even:slots, :].astype(F32)
    got = jnp.where(slot == even, last, got).astype(BF)
    extra_slot = plan.degrees - info_ref[0]
    lane = lax.broadcasted_iota(jnp.int32, (SUB, even), 1)
    first = lax.broadcasted_iota(jnp.int32, (SUB, even), 0) == 0
    choose = jnp.where(first & (lane == extra_slot), 1.0, 0.0).astype(BF)
    extra = jnp.dot(choose, control_ref[:even, :], preferred_element_type=F32)
    extra = jnp.where(extra_slot == even, last, extra)
    place = lax.broadcasted_iota(jnp.int32, (SUB, levels), 0)
    tail = jnp.zeros((SUB, levels), F32)
    for c in range(4):
        tail = jnp.where(place == c, extra[0:1, c * levels:(c + 1) * levels], tail)
    high_digit = (info_ref[0] // DIGIT).astype(F32)
    low_digit = (info_ref[0] % DIGIT).astype(F32)
    tail = jnp.where(place == 4, high_digit, jnp.where(place == 5, low_digit, tail)).astype(BF)
    for k in range(messages):
        for c in range(4):
            out_ref[k, c * plan.rows:(c + 1) * plan.rows, :] = got[
                k * plan.rows:(k + 1) * plan.rows, c * levels:(c + 1) * levels
            ]
        out_ref[k, 4 * plan.rows:, :] = tail


def pack(plan, control, lowest, slots_of_rows):
    slots, columns = control.shape
    levels = columns // 4
    height = 4 * plan.rows + SUB
    per_step = max(1, min(plan.group, 320 // plan.rows))
    return pl.pallas_call(
        functools.partial(pack_kernel, plan, levels),
        grid=(plan.group // per_step,),
        out_shape=jax.ShapeDtypeStruct((plan.group, height, levels), BF),
        in_specs=[
            pl.BlockSpec(memory_space=pltpu.SMEM),
            pl.BlockSpec((per_step * plan.rows, 1), lambda k: (k, 0)),
            pl.BlockSpec((slots, columns), lambda k: (0, 0)),
        ],
        out_specs=pl.BlockSpec((per_step, height, levels), lambda k: (k, 0, 0)),
        compiler_params=pltpu.CompilerParams(vmem_limit_bytes=16 * 1024 * 1024),
        cost_estimate=pl.CostEstimate(flops=1, bytes_accessed=1, transcendentals=0),
        name="pack_rows",
    )(lowest, slots_of_rows, control)


def table_kernel(plan, upper_ref, lower_ref, legendre_ref, *refs):
    outs, picks = refs[:2], refs[2:]
    slots = legendre_ref.shape[0]
    even = slots - 1

    @pl.when(pl.program_id(0) == 0)
    def _():
        for index_ref, pick_ref in zip((upper_ref, lower_ref), picks):
            slot = lax.broadcasted_iota(jnp.int32, pick_ref.shape, 0)
            pick_ref[...] = jnp.where(slot == index_ref[...], 1.0, 0.0).astype(BF)

    def times(rows, picked):
        return lax.dot_general(rows, picked, (((0,), (0,)), ((), ())), preferred_element_type=F32)

    for out_ref, pick_ref in zip(outs, picks):
        got = times(legendre_ref[:even, :], pick_ref[:even, :])
        last = jnp.concatenate(
            [legendre_ref[even:slots, :].astype(F32), jnp.zeros((SUB - 1, legendre_ref.shape[1]), F32)], axis=0
        ).astype(BF)
        out_ref[...] = (got + times(last, pick_ref[even:even + SUB, :])).astype(BF)


def make_tables(plan, legendre, slots_of_rows):
    slots, latitudes = legendre.shape
    tile = 256
    index = [rows[None, :width] for rows, width in zip(slots_of_rows, plan.widths)]
    return pl.pallas_call(
        functools.partial(table_kernel, plan),
        grid=(latitudes // tile,),
        out_shape=[jax.ShapeDtypeStruct((latitudes, width), BF) for width in plan.widths],
        in_specs=[pl.BlockSpec((1, width), lambda t: (0, 0)) for width in plan.widths]
        + [pl.BlockSpec((slots, tile), lambda t: (0, t))],
        out_specs=[pl.BlockSpec((tile, width), lambda t: (t, 0)) for width in plan.widths],
        scratch_shapes=[pltpu.VMEM((slots - 1 + SUB, width), BF) for width in plan.widths],
        compiler_params=pltpu.CompilerParams(vmem_limit_bytes=20 * 1024 * 1024),
        cost_estimate=pl.CostEstimate(
            flops=20 * latitudes * slots * sum(plan.widths), bytes_accessed=2 * legendre.size, transcendentals=0
        ),
        name="make_tables",
    )(*index, legendre)


def swap_matrix():
    i = lax.broadcasted_iota(jnp.int32, (SUB * SUB, SUB * SUB), 0)
    j = lax.broadcasted_iota(jnp.int32, (SUB * SUB, SUB * SUB), 1)
    return jnp.where((i // SUB == j % SUB) & (i % SUB == j // SUB), 1.0, 0.0).astype(BF)


def filter_kernel(plan, levels, info_ref, rows_ref, *refs):
    *blocks, out_ref, held_ref, x_ref, y_ref, z_ref, in_sems, out_sems = refs
    pieces = len(blocks) // 2
    each = plan.block // pieces
    first_fold = info_ref[1].astype(F32)
    swap = swap_matrix()

    arrivals = []
    for at, block in enumerate(blocks):
        place = info_ref[0] if at < pieces else 1 - info_ref[0]
        folds = pl.ds(at % pieces * each, each)
        arrivals.append(pltpu.make_async_copy(block, held_ref.at[place, folds], in_sems.at[at]))
        arrivals[at].start()

    def low_matrix(fold):
        return held_ref[0, fold]

    def high_matrix(fold):
        return held_ref[1, fold // each * each + each - 1 - fold % each]

    def times(rows, matrix):
        return lax.dot_general(rows, matrix, (((1,), (1,)), ((), ())), preferred_element_type=F32)

    def turn(rows):
        return jnp.dot(swap, rows, preferred_element_type=F32)

    groups = plan.group // SUB
    held = plan.rows * SUB
    for g in range(groups):
        sources = slice(g * SUB, (g + 1) * SUB)
        for r in range(0, plan.rows, SUB):
            parts = []
            for c in range(4):
                start = c * plan.rows + r
                parts.append(rows_ref[sources, start:start + SUB, :].reshape(SUB * SUB, levels))
            x_ref[g * held + r * SUB:g * held + (r + SUB) * SUB, :] = turn(jnp.concatenate(parts, axis=1)).astype(BF)

    for arrival in arrivals:
        arrival.wait()

    departures = []

    def send(rows):
        at = len(departures)
        departures.append(pltpu.make_async_copy(z_ref.at[:, rows, :], out_ref.at[:, rows, :], out_sems.at[at]))
        departures[at].start()

    tails = []
    for g in range(groups):
        sources = slice(g * SUB, (g + 1) * SUB)
        tail = turn(rows_ref[sources, 4 * plan.rows:4 * plan.rows + SUB, :].reshape(SUB * SUB, levels))
        low = tail[4 * SUB:5 * SUB] * DIGIT + tail[5 * SUB:6 * SUB]
        tails.append([tail[:4 * SUB].astype(BF), jnp.concatenate([low] * 4, axis=0), jnp.zeros((4 * SUB, levels), F32)])

    for row0, fold0, count in plan.chunks:
        height = ceil_to(2 * count, SUB)
        for g in range(groups):
            sources = slice(g * SUB, (g + 1) * SUB)
            extra, low, kept = tails[g]
            for i in range(count):
                def stack(row):
                    at = g * held + row * SUB
                    return jnp.concatenate(
                        [x_ref[at:at + SUB, c * levels:(c + 1) * levels] for c in range(4)], axis=0
                    )

                folded, high = stack(row0 + i), stack(row0 + count + i)
                from_low = times(folded, low_matrix(fold0 + i))
                from_high = times(jnp.concatenate([folded, high, extra], axis=0), high_matrix(fold0 + i))
                fold = first_fold + (fold0 + i)
                mixed = jnp.where(low <= fold, from_low, from_high[:4 * SUB])
                kept = jnp.where(low == fold, from_high[8 * SUB:], kept)
                for row, value in ((row0 + i, mixed), (row0 + count + i, from_high[4 * SUB:8 * SUB])):
                    value = value.astype(BF)
                    for c in range(4):
                        y_ref[row * SUB:(row + 1) * SUB, c * levels:(c + 1) * levels] = value[c * SUB:(c + 1) * SUB]
            tails[g][2] = kept
            if height > 2 * count:
                y_ref[(row0 + 2 * count) * SUB:(row0 + height) * SUB, :] = jnp.zeros(
                    ((height - 2 * count) * SUB, 4 * levels), BF
                )
            for r in range(row0, row0 + height, SUB):
                back = turn(y_ref[r * SUB:(r + SUB) * SUB, :]).astype(BF)
                for c in range(4):
                    start = c * plan.rows + r
                    z_ref[sources, start:start + SUB, :] = back[:, c * levels:(c + 1) * levels].reshape(
                        SUB, SUB, levels
                    )
        for c in range(4):
            send(pl.ds(c * plan.rows + row0, height))
    for g in range(groups):
        sources = slice(g * SUB, (g + 1) * SUB)
        filled = jnp.concatenate([tails[g][2], jnp.zeros((12 * SUB, levels), F32)], axis=0).astype(BF)
        z_ref[sources, 4 * plan.rows:4 * plan.rows + SUB, :] = turn(filled).astype(BF).reshape(SUB, SUB, levels)
    send(pl.ds(4 * plan.rows, SUB))
    for departure in departures:
        departure.wait()


def filter_rows(plan, info, received, near_blocks, far_blocks):
    levels = received.shape[2]
    blocks = [*near_blocks, *far_blocks]
    smem, vmem = pl.BlockSpec(memory_space=pltpu.SMEM), pl.BlockSpec(memory_space=pltpu.VMEM)
    anywhere = pl.BlockSpec(memory_space=pl.ANY)
    return pl.pallas_call(
        functools.partial(filter_kernel, plan, levels),
        out_shape=jax.ShapeDtypeStruct(received.shape, BF),
        in_specs=[smem, vmem] + [anywhere] * len(blocks),
        out_specs=anywhere,
        scratch_shapes=[
            pltpu.VMEM((2, plan.block, levels, levels), BF),
            pltpu.VMEM((plan.group * plan.rows, 4 * levels), BF),
            pltpu.VMEM((plan.rows * SUB, 4 * levels), BF),
            pltpu.VMEM(received.shape, BF),
            pltpu.SemaphoreType.DMA((len(blocks),)),
            pltpu.SemaphoreType.DMA((4 * len(plan.chunks) + 1,)),
        ],
        compiler_params=pltpu.CompilerParams(vmem_limit_bytes=20 * 1024 * 1024),
        cost_estimate=pl.CostEstimate(
            flops=2 * plan.group * 16 * plan.block * levels * levels * 4,
            bytes_accessed=2 * 2 * received.size + 4 * plan.block * levels * levels,
            transcendentals=0,
        ),
        name="filter_rows",
    )(info, received, *blocks)


def grid_kernel(plan, levels, latitudes, depth, level_cols, tile, info_ref, starts_ref, bands_ref, part_ref, *refs):
    tables, out_ref, held_tables = refs[:2], refs[2], refs[3:5]
    upper_ref, lower_ref, *grids, cut_ref, sems, out_sems = refs[5:]
    waves = bands_ref.shape[0]
    groups = 4 * levels // level_cols
    tiles = [slice(start, stop) for start, stop in zip(tile, tile[1:])]

    def copy(half, at):
        rows = tiles[at]
        return pltpu.make_async_copy(tables[half].at[rows], held_tables[half].at[rows], sems.at[half, at])

    for half in (1, 0):
        for at in range(len(tiles)):
            copy(half, at).start()

    base = 0
    for at, first, rows in plan.segments:
        for k in range(plan.group):
            for c in range(4):
                start = c * plan.rows + plan.chunks[at][0] + first
                cols = slice(c * levels, (c + 1) * levels)
                value = part_ref[k, start:start + rows, :]
                upper_ref[base + k * rows:base + (k + 1) * rows, cols] = value
                if base < plan.widths[1]:
                    lower_ref[base + k * rows:base + (k + 1) * rows, cols] = value
        base += plan.group * rows

    extra = part_ref[info_ref[0], 4 * plan.rows:4 * plan.rows + SUB, :]
    base = info_ref[1] // SUB * SUB
    place = pl.ds(pl.multiple_of(base, SUB), SUB)
    here = lax.broadcasted_iota(jnp.int32, (SUB, levels), 0) == info_ref[1] - base
    for c in range(4):
        cols = slice(c * levels, (c + 1) * levels)
        held = upper_ref[place, cols].astype(F32)
        lower_ref[place, cols] = jnp.where(here, extra[c:c + 1, :].astype(F32), held).astype(BF)

    def transform(half, at):
        copy(half, at).wait()
        rows = tiles[at]
        grids[half][rows, :] = jnp.dot(
            held_tables[half][rows, :], (upper_ref, lower_ref)[half][...], preferred_element_type=F32
        )

    def departure(half, w):
        messages = pl.ds(w * groups, groups)
        return pltpu.make_async_copy(cut_ref.at[messages, half], out_ref.at[messages, half], out_sems.at[half, w])

    def cut(half, w):
        place = lax.broadcasted_iota(jnp.int32, (8, 4 * levels), 0)
        start = starts_ref[w]
        base = start // 8 * 8
        offset = start - base

        def slab(at):
            held = grids[half][pl.ds(pl.multiple_of(base + at, 8), 8), :]
            return pltpu.roll(held, (8 - offset) % 8, axis=0)

        after = slab(0)
        done = []
        for r in range(0, depth, 8):
            now, after = after, slab(r + 8)
            got = jnp.where(place < 8 - offset, now, after)
            done.append(jnp.where(place < bands_ref[w] - r, got, 0.0))
            if len(done) == 2 or r + 8 == depth:
                rows = jnp.concatenate(done, axis=0).astype(BF)
                first = r + 8 - rows.shape[0]
                for g in range(groups):
                    cut_ref[w * groups + g, half, first:r + 8, :] = rows[:, g * level_cols:(g + 1) * level_cols]
                done = []
        departure(half, w).start()

    for at in range(len(tiles)):
        transform(1, at)
    for at in range(len(tiles)):
        transform(0, at)
        for w in range(at * waves // len(tiles), (at + 1) * waves // len(tiles)):
            cut(1, w)
    for w in range(waves):
        cut(0, w)
    for half in range(2):
        for w in range(waves):
            departure(half, w).wait()


def to_bands(plan, info, starts, bands, part, tables, depth, level_cols):
    latitudes = tables[0].shape[0]
    levels = part.shape[2]
    columns = 4 * levels
    tile = [0] + list(range(latitudes // 5, latitudes + 1, 2 * latitudes // 5))
    smem, vmem = pl.BlockSpec(memory_space=pltpu.SMEM), pl.BlockSpec(memory_space=pltpu.VMEM)
    messages = bands.shape[0] * columns // level_cols
    grid = pltpu.VMEM((ceil_to(latitudes + depth, 8) + 8, columns), F32)
    held = 2 * (latitudes + columns) * sum(plan.widths) + 8 * (latitudes + depth) * columns
    held += 4 * messages * depth * ceil_to(level_cols, 128) + 2 * part.size
    limit = max(52 * 1024 * 1024, held + 4 * 1024 * 1024)
    return pl.pallas_call(
        functools.partial(grid_kernel, plan, levels, latitudes, depth, level_cols, tile),
        out_shape=jax.ShapeDtypeStruct((messages, 2, depth, level_cols), BF),
        in_specs=[smem, smem, smem, vmem] + [pl.BlockSpec(memory_space=pl.ANY)] * 2,
        out_specs=pl.BlockSpec(memory_space=pl.ANY),
        scratch_shapes=[
            pltpu.VMEM(tables[0].shape, BF),
            pltpu.VMEM(tables[1].shape, BF),
            pltpu.VMEM((plan.widths[0], columns), BF),
            pltpu.VMEM((plan.widths[1], columns), BF),
            grid,
            grid,
            pltpu.VMEM((messages, 2, depth, level_cols), BF),
            pltpu.SemaphoreType.DMA((2, len(tile) - 1)),
            pltpu.SemaphoreType.DMA((2, bands.shape[0])),
        ],
        compiler_params=pltpu.CompilerParams(vmem_limit_bytes=limit),
        cost_estimate=pl.CostEstimate(
            flops=2 * latitudes * sum(plan.widths) * columns,
            bytes_accessed=2 * latitudes * sum(plan.widths) + 4 * messages * depth * level_cols,
            transcendentals=0,
        ),
        name="grid_bands",
    )(info, starts, bands, part, *tables)


def per_device(control, covariance, legendre, pair_order, band_rows):
    axes = ("wave", "lev")
    waves, lev_count = lax.axis_size("wave"), lax.axis_size("lev")
    _, slots, columns = control.shape
    degrees, levels = slots - 1, columns // 4
    latitudes = legendre.shape[2]
    depth = 5 * latitudes // (4 * waves)
    level_cols = columns // lev_count
    plan = Plan(waves * lev_count, degrees)
    group, block = plan.group, plan.block
    me = lax.axis_index("wave") * lev_count + lax.axis_index("lev")
    is_high = (me >= group).astype(jnp.int32)
    lowest = pair_order[0]
    halves = [list(range(group)), list(range(group, 2 * group))]

    def exchange(rows):
        return lax.all_to_all(rows, axes, split_axis=0, concat_axis=0, tiled=True, axis_index_groups=halves)

    plane = group // 2
    whole = range(2 * group)
    far = [(d, (3 - d // plane) * plane + d % plane) for d in whole]
    near = [(d, d // plane * plane + plane - 1 - d % plane) for d in whole]
    pieces = 2 if block % 2 == 0 else 1
    each = block // pieces
    own = []
    for fold in range(0, block, each):
        start = jnp.where(is_high == 1, block - fold - each, fold)
        own.append(lax.dynamic_slice_in_dim(covariance, start, each, 0).astype(BF))
        own[-1], covariance = lax.optimization_barrier((own[-1], covariance))
    *own, control = lax.optimization_barrier((*own, control))
    far_blocks = [lax.ppermute(part, axes, far) for part in own]
    near_blocks = [lax.ppermute(part, axes, near) for part in own]

    def fold_block(rank):
        rank = jnp.where(is_high == 1, group - 1 - rank, rank)
        return rank // plane * plane + plane - 1 - rank % plane

    def slots_of(message, fold, folded, used):
        degree = fold_block(message) * block + fold
        upper = jnp.where(folded, degree - lowest, degrees - 1 - degree - lowest)
        upper = jnp.where(used & (upper >= 0), upper, -1)
        lower = jnp.where(used & folded & (degree <= lowest), degrees - degree, -1)
        return upper, lower

    upper, lower = slots_of(*plan.message_rows())
    sent = jnp.where(upper >= 0, upper, lower)
    received = exchange(pack(plan, control[0], pair_order, sent[:, None]))

    tables = make_tables(plan, legendre[0], slots_of(*plan.transform_rows()))

    info = jnp.stack([is_high, fold_block(me - group * is_high) * block])
    received, tables = lax.optimization_barrier((received, tables))
    filtered = exchange(filter_rows(plan, info, received, near_blocks, far_blocks))

    extra_block = lowest // block
    extra_message = fold_block(extra_block)
    extra_row = plan.extra_row(extra_message, lowest - extra_block * block)
    where = jnp.stack([extra_message, extra_row])
    starts = jnp.cumsum(band_rows) - band_rows
    outgoing = to_bands(plan, where, starts, band_rows, filtered, tables, depth, level_cols)
    outgoing = outgoing.reshape(-1, depth, level_cols)
    return lax.all_to_all(outgoing, axes, split_axis=0, concat_axis=0, tiled=True)


def solution(mesh):
    return jax.shard_map(
        per_device,
        mesh=mesh,
        in_specs=(
            P(("wave", "lev"), None, None),
            P(("wave", "lev"), None, None),
            P(("wave", "lev"), None, None),
            P(("wave", "lev")),
            P(),
        ),
        out_specs=P(None, "wave", "lev"),
        check_vma=False,
    )
```

```python
import functools

import jax
import jax.numpy as jnp
import numpy as np
from jax import lax
from jax.experimental import pallas as pl
from jax.experimental.pallas import tpu as pltpu
from jax.sharding import PartitionSpec as P

BF = jnp.bfloat16
F32 = jnp.float32
SUB = 16
DIGIT = 16


def ceil_to(value, step):
    return (value + step - 1) // step * step


class Plan:
    def __init__(self, devices, degrees):
        self.devices = devices
        self.group = devices // 2
        self.degrees = degrees
        self.block = degrees // devices
        self.chunks = []
        row, fold = 0, 0
        for count in self.fold_counts(self.block):
            self.chunks.append((row, fold, count))
            row += ceil_to(2 * count, SUB)
            fold += count
        self.rows = row
        whole = [(at, n) for at, (_, _, n) in enumerate(self.chunks) if n % SUB == 0]
        mixed = [(at, n) for at, (_, _, n) in enumerate(self.chunks) if n % SUB]
        lower = [(at, 0, n) for at, n in whole] + [(at, 0, ceil_to(2 * n, SUB)) for at, n in mixed]
        self.segments = lower + [(at, n, n) for at, n in whole]
        self.widths = [
            self.group * sum(n for _, _, n in self.segments),
            self.group * sum(n for _, _, n in lower),
        ]

    @staticmethod
    def fold_counts(block):
        return (block - 8, 8) if block % SUB == 8 and block > 8 else (block,)

    def chunk_rows(self, at):
        _, first, count = self.chunks[at]
        height = ceil_to(2 * count, SUB)
        fold = np.zeros(height, np.int32)
        fold[:2 * count] = first + np.tile(np.arange(count), 2)
        row = np.arange(height)
        return fold, row < count, row < 2 * count

    def message_rows(self):
        tables = [self.chunk_rows(at) for at in range(len(self.chunks))]
        one = [np.concatenate(column) for column in zip(*tables)]
        return [np.repeat(np.arange(self.group, dtype=np.int32), self.rows)] + [
            np.tile(column, self.group) for column in one
        ]

    def transform_rows(self):
        parts = []
        for at, first, count in self.segments:
            columns = [column[first:first + count] for column in self.chunk_rows(at)]
            parts.append(
                [np.repeat(np.arange(self.group, dtype=np.int32), count)]
                + [np.tile(column, self.group) for column in columns]
            )
        return [np.concatenate(column) for column in zip(*parts)]

    def extra_row(self, message, fold):
        base, result = 0, jnp.int32(0)
        for at, first, count in self.segments:
            if first == 0:
                start = self.chunks[at][1]
                here = (fold >= start) & (fold < start + self.chunks[at][2])
                result = jnp.where(here, base + message * count + fold - start, result)
            base += self.group * count
        return result


def cast_kernel(info_ref, blocks_ref, *refs):
    *outs, held_ref, cast_ref, in_sems, out_sems = refs
    total, each = blocks_ref.shape[0], outs[0].shape[0]
    part = each // 2 if each % 2 == 0 else each
    arrivals, departures = [], []
    for fold in range(0, total, part):
        piece, inside = fold // each, fold % each
        start = jnp.where(info_ref[0] == 1, total - (piece + 1) * each, piece * each) + inside
        at, here = len(arrivals), pl.ds(fold, part)
        arrivals.append(pltpu.make_async_copy(blocks_ref.at[pl.ds(start, part)], held_ref.at[here], in_sems.at[at]))
        arrivals[at].start()
        there = outs[piece].at[pl.ds(inside, part)]
        departures.append(pltpu.make_async_copy(cast_ref.at[here], there, out_sems.at[at]))
    for at, fold in enumerate(range(0, total, part)):
        arrivals[at].wait()
        cast_ref[fold:fold + part] = held_ref[fold:fold + part].astype(BF)
        departures[at].start()
    for departure in departures:
        departure.wait()


def cast_blocks(blocks, info, pieces):
    each = blocks.shape[0] // pieces
    steps = pieces * (2 if each % 2 == 0 else 1)
    anywhere = pl.BlockSpec(memory_space=pl.ANY)
    return pl.pallas_call(
        cast_kernel,
        out_shape=[jax.ShapeDtypeStruct((each, *blocks.shape[1:]), BF)] * pieces,
        in_specs=[pl.BlockSpec(memory_space=pltpu.SMEM), anywhere],
        out_specs=[anywhere] * pieces,
        scratch_shapes=[
            pltpu.VMEM(blocks.shape, F32),
            pltpu.VMEM(blocks.shape, BF),
            pltpu.SemaphoreType.DMA((steps,)),
            pltpu.SemaphoreType.DMA((steps,)),
        ],
        compiler_params=pltpu.CompilerParams(vmem_limit_bytes=56 * 1024 * 1024),
        cost_estimate=pl.CostEstimate(flops=1, bytes_accessed=6 * blocks.size, transcendentals=0),
        name="cast_blocks",
    )(info, blocks)


def pack_kernel(plan, levels, info_ref, slot_ref, control_ref, out_ref):
    slots = control_ref.shape[0]
    messages = out_ref.shape[0]
    even = slots - 1
    rows = messages * plan.rows
    slot = slot_ref[...]
    pick = (slot == lax.broadcasted_iota(jnp.int32, (rows, even), 1)).astype(F32).astype(BF)
    got = jnp.dot(pick, control_ref[:even, :], preferred_element_type=F32)
    last = control_ref[even:slots, :].astype(F32)
    got = jnp.where(slot == even, last, got).astype(BF)
    extra_slot = plan.degrees - info_ref[0]
    lane = lax.broadcasted_iota(jnp.int32, (SUB, even), 1)
    first = lax.broadcasted_iota(jnp.int32, (SUB, even), 0) == 0
    choose = jnp.where(first & (lane == extra_slot), 1.0, 0.0).astype(BF)
    extra = jnp.dot(choose, control_ref[:even, :], preferred_element_type=F32)
    extra = jnp.where(extra_slot == even, last, extra)
    place = lax.broadcasted_iota(jnp.int32, (SUB, levels), 0)
    tail = jnp.zeros((SUB, levels), F32)
    for c in range(4):
        tail = jnp.where(place == c, extra[0:1, c * levels:(c + 1) * levels], tail)
    high_digit = (info_ref[0] // DIGIT).astype(F32)
    low_digit = (info_ref[0] % DIGIT).astype(F32)
    tail = jnp.where(place == 4, high_digit, jnp.where(place == 5, low_digit, tail)).astype(BF)
    for k in range(messages):
        for c in range(4):
            out_ref[k, c * plan.rows:(c + 1) * plan.rows, :] = got[
                k * plan.rows:(k + 1) * plan.rows, c * levels:(c + 1) * levels
            ]
        out_ref[k, 4 * plan.rows:, :] = tail


def pack(plan, control, lowest, slots_of_rows):
    slots, columns = control.shape
    levels = columns // 4
    height = 4 * plan.rows + SUB
    per_step = max(1, min(plan.group, 320 // plan.rows))
    return pl.pallas_call(
        functools.partial(pack_kernel, plan, levels),
        grid=(plan.group // per_step,),
        out_shape=jax.ShapeDtypeStruct((plan.group, height, levels), BF),
        in_specs=[
            pl.BlockSpec(memory_space=pltpu.SMEM),
            pl.BlockSpec((per_step * plan.rows, 1), lambda k: (k, 0)),
            pl.BlockSpec((slots, columns), lambda k: (0, 0)),
        ],
        out_specs=pl.BlockSpec((per_step, height, levels), lambda k: (k, 0, 0)),
        compiler_params=pltpu.CompilerParams(vmem_limit_bytes=16 * 1024 * 1024),
        cost_estimate=pl.CostEstimate(flops=1, bytes_accessed=1, transcendentals=0),
        name="pack_rows",
    )(lowest, slots_of_rows, control)


def table_kernel(plan, upper_ref, lower_ref, legendre_ref, *refs):
    outs, picks = refs[:2], refs[2:]
    slots = legendre_ref.shape[0]
    even = slots - 1

    @pl.when(pl.program_id(0) == 0)
    def _():
        for index_ref, pick_ref in zip((upper_ref, lower_ref), picks):
            slot = lax.broadcasted_iota(jnp.int32, pick_ref.shape, 0)
            pick_ref[...] = jnp.where(slot == index_ref[...], 1.0, 0.0).astype(BF)

    def times(rows, picked):
        return lax.dot_general(rows, picked, (((0,), (0,)), ((), ())), preferred_element_type=F32)

    for out_ref, pick_ref in zip(outs, picks):
        got = times(legendre_ref[:even, :], pick_ref[:even, :])
        last = jnp.concatenate(
            [legendre_ref[even:slots, :].astype(F32), jnp.zeros((SUB - 1, legendre_ref.shape[1]), F32)], axis=0
        ).astype(BF)
        out_ref[...] = (got + times(last, pick_ref[even:even + SUB, :])).astype(BF)


def make_tables(plan, legendre, slots_of_rows):
    slots, latitudes = legendre.shape
    tile = 256
    index = [rows[None, :width] for rows, width in zip(slots_of_rows, plan.widths)]
    return pl.pallas_call(
        functools.partial(table_kernel, plan),
        grid=(latitudes // tile,),
        out_shape=[jax.ShapeDtypeStruct((latitudes, width), BF) for width in plan.widths],
        in_specs=[pl.BlockSpec((1, width), lambda t: (0, 0)) for width in plan.widths]
        + [pl.BlockSpec((slots, tile), lambda t: (0, t))],
        out_specs=[pl.BlockSpec((tile, width), lambda t: (t, 0)) for width in plan.widths],
        scratch_shapes=[pltpu.VMEM((slots - 1 + SUB, width), BF) for width in plan.widths],
        compiler_params=pltpu.CompilerParams(vmem_limit_bytes=20 * 1024 * 1024),
        cost_estimate=pl.CostEstimate(
            flops=20 * latitudes * slots * sum(plan.widths), bytes_accessed=2 * legendre.size, transcendentals=0
        ),
        name="make_tables",
    )(*index, legendre)


def swap_matrix():
    i = lax.broadcasted_iota(jnp.int32, (SUB * SUB, SUB * SUB), 0)
    j = lax.broadcasted_iota(jnp.int32, (SUB * SUB, SUB * SUB), 1)
    return jnp.where((i // SUB == j % SUB) & (i % SUB == j // SUB), 1.0, 0.0).astype(BF)


def filter_kernel(plan, levels, info_ref, rows_ref, *refs):
    *blocks, out_ref, held_ref, x_ref, y_ref, z_ref, in_sems, out_sems = refs
    pieces = len(blocks) // 2
    each = plan.block // pieces
    first_fold = info_ref[1].astype(F32)
    swap = swap_matrix()

    arrivals = []
    for at, block in enumerate(blocks):
        place = info_ref[0] if at < pieces else 1 - info_ref[0]
        folds = pl.ds(at % pieces * each, each)
        arrivals.append(pltpu.make_async_copy(block, held_ref.at[place, folds], in_sems.at[at]))
        arrivals[at].start()

    def low_matrix(fold):
        return held_ref[0, fold]

    def high_matrix(fold):
        return held_ref[1, fold // each * each + each - 1 - fold % each]

    def times(rows, matrix):
        return lax.dot_general(rows, matrix, (((1,), (1,)), ((), ())), preferred_element_type=F32)

    def turn(rows):
        return jnp.dot(swap, rows, preferred_element_type=F32)

    groups = plan.group // SUB
    held = plan.rows * SUB
    for g in range(groups):
        sources = slice(g * SUB, (g + 1) * SUB)
        for r in range(0, plan.rows, SUB):
            parts = []
            for c in range(4):
                start = c * plan.rows + r
                parts.append(rows_ref[sources, start:start + SUB, :].reshape(SUB * SUB, levels))
            x_ref[g * held + r * SUB:g * held + (r + SUB) * SUB, :] = turn(jnp.concatenate(parts, axis=1)).astype(BF)

    for arrival in arrivals:
        arrival.wait()

    departures = []

    def send(rows):
        at = len(departures)
        departures.append(pltpu.make_async_copy(z_ref.at[:, rows, :], out_ref.at[:, rows, :], out_sems.at[at]))
        departures[at].start()

    tails = []
    for g in range(groups):
        sources = slice(g * SUB, (g + 1) * SUB)
        tail = turn(rows_ref[sources, 4 * plan.rows:4 * plan.rows + SUB, :].reshape(SUB * SUB, levels))
        low = tail[4 * SUB:5 * SUB] * DIGIT + tail[5 * SUB:6 * SUB]
        tails.append([tail[:4 * SUB].astype(BF), jnp.concatenate([low] * 4, axis=0), jnp.zeros((4 * SUB, levels), F32)])

    for row0, fold0, count in plan.chunks:
        height = ceil_to(2 * count, SUB)
        for g in range(groups):
            sources = slice(g * SUB, (g + 1) * SUB)
            extra, low, kept = tails[g]
            for i in range(count):
                def stack(row):
                    at = g * held + row * SUB
                    return jnp.concatenate(
                        [x_ref[at:at + SUB, c * levels:(c + 1) * levels] for c in range(4)], axis=0
                    )

                folded, high = stack(row0 + i), stack(row0 + count + i)
                from_low = times(folded, low_matrix(fold0 + i))
                from_high = times(jnp.concatenate([folded, high, extra], axis=0), high_matrix(fold0 + i))
                fold = first_fold + (fold0 + i)
                mixed = jnp.where(low <= fold, from_low, from_high[:4 * SUB])
                kept = jnp.where(low == fold, from_high[8 * SUB:], kept)
                for row, value in ((row0 + i, mixed), (row0 + count + i, from_high[4 * SUB:8 * SUB])):
                    value = value.astype(BF)
                    for c in range(4):
                        y_ref[row * SUB:(row + 1) * SUB, c * levels:(c + 1) * levels] = value[c * SUB:(c + 1) * SUB]
            tails[g][2] = kept
            if height > 2 * count:
                y_ref[(row0 + 2 * count) * SUB:(row0 + height) * SUB, :] = jnp.zeros(
                    ((height - 2 * count) * SUB, 4 * levels), BF
                )
            for r in range(row0, row0 + height, SUB):
                back = turn(y_ref[r * SUB:(r + SUB) * SUB, :]).astype(BF)
                for c in range(4):
                    start = c * plan.rows + r
                    z_ref[sources, start:start + SUB, :] = back[:, c * levels:(c + 1) * levels].reshape(
                        SUB, SUB, levels
                    )
        for c in range(4):
            send(pl.ds(c * plan.rows + row0, height))
    for g in range(groups):
        sources = slice(g * SUB, (g + 1) * SUB)
        filled = jnp.concatenate([tails[g][2], jnp.zeros((12 * SUB, levels), F32)], axis=0).astype(BF)
        z_ref[sources, 4 * plan.rows:4 * plan.rows + SUB, :] = turn(filled).astype(BF).reshape(SUB, SUB, levels)
    send(pl.ds(4 * plan.rows, SUB))
    for departure in departures:
        departure.wait()


def filter_rows(plan, info, received, near_blocks, far_blocks):
    levels = received.shape[2]
    blocks = [*near_blocks, *far_blocks]
    smem, vmem = pl.BlockSpec(memory_space=pltpu.SMEM), pl.BlockSpec(memory_space=pltpu.VMEM)
    anywhere = pl.BlockSpec(memory_space=pl.ANY)
    return pl.pallas_call(
        functools.partial(filter_kernel, plan, levels),
        out_shape=jax.ShapeDtypeStruct(received.shape, BF),
        in_specs=[smem, vmem] + [anywhere] * len(blocks),
        out_specs=anywhere,
        scratch_shapes=[
            pltpu.VMEM((2, plan.block, levels, levels), BF),
            pltpu.VMEM((plan.group * plan.rows, 4 * levels), BF),
            pltpu.VMEM((plan.rows * SUB, 4 * levels), BF),
            pltpu.VMEM(received.shape, BF),
            pltpu.SemaphoreType.DMA((len(blocks),)),
            pltpu.SemaphoreType.DMA((4 * len(plan.chunks) + 1,)),
        ],
        compiler_params=pltpu.CompilerParams(vmem_limit_bytes=20 * 1024 * 1024),
        cost_estimate=pl.CostEstimate(
            flops=2 * plan.group * 16 * plan.block * levels * levels * 4,
            bytes_accessed=2 * 2 * received.size + 4 * plan.block * levels * levels,
            transcendentals=0,
        ),
        name="filter_rows",
    )(info, received, *blocks)


def grid_kernel(plan, levels, latitudes, depth, level_cols, tile, info_ref, starts_ref, bands_ref, part_ref, *refs):
    tables, out_ref, held_tables = refs[:2], refs[2], refs[3:5]
    upper_ref, lower_ref, *grids, cut_ref, sems, out_sems = refs[5:]
    waves = bands_ref.shape[0]
    groups = 4 * levels // level_cols
    tiles = [slice(start, stop) for start, stop in zip(tile, tile[1:])]

    def copy(half, at):
        rows = tiles[at]
        return pltpu.make_async_copy(tables[half].at[rows], held_tables[half].at[rows], sems.at[half, at])

    for half in (1, 0):
        for at in range(len(tiles)):
            copy(half, at).start()

    base = 0
    for at, first, rows in plan.segments:
        for k in range(plan.group):
            for c in range(4):
                start = c * plan.rows + plan.chunks[at][0] + first
                cols = slice(c * levels, (c + 1) * levels)
                value = part_ref[k, start:start + rows, :]
                upper_ref[base + k * rows:base + (k + 1) * rows, cols] = value
                if base < plan.widths[1]:
                    lower_ref[base + k * rows:base + (k + 1) * rows, cols] = value
        base += plan.group * rows

    extra = part_ref[info_ref[0], 4 * plan.rows:4 * plan.rows + SUB, :]
    base = info_ref[1] // SUB * SUB
    place = pl.ds(pl.multiple_of(base, SUB), SUB)
    here = lax.broadcasted_iota(jnp.int32, (SUB, levels), 0) == info_ref[1] - base
    for c in range(4):
        cols = slice(c * levels, (c + 1) * levels)
        held = upper_ref[place, cols].astype(F32)
        lower_ref[place, cols] = jnp.where(here, extra[c:c + 1, :].astype(F32), held).astype(BF)

    def transform(half, at):
        copy(half, at).wait()
        rows = tiles[at]
        grids[half][rows, :] = jnp.dot(
            held_tables[half][rows, :], (upper_ref, lower_ref)[half][...], preferred_element_type=F32
        )

    def departure(half, w):
        messages = pl.ds(w * groups, groups)
        return pltpu.make_async_copy(cut_ref.at[messages, half], out_ref.at[messages, half], out_sems.at[half, w])

    def cut(half, w):
        place = lax.broadcasted_iota(jnp.int32, (8, 4 * levels), 0)
        start = starts_ref[w]
        base = start // 8 * 8
        offset = start - base

        def slab(at):
            held = grids[half][pl.ds(pl.multiple_of(base + at, 8), 8), :]
            return pltpu.roll(held, (8 - offset) % 8, axis=0)

        after = slab(0)
        done = []
        for r in range(0, depth, 8):
            now, after = after, slab(r + 8)
            got = jnp.where(place < 8 - offset, now, after)
            done.append(jnp.where(place < bands_ref[w] - r, got, 0.0))
            if len(done) == 2 or r + 8 == depth:
                rows = jnp.concatenate(done, axis=0).astype(BF)
                first = r + 8 - rows.shape[0]
                for g in range(groups):
                    cut_ref[w * groups + g, half, first:r + 8, :] = rows[:, g * level_cols:(g + 1) * level_cols]
                done = []
        departure(half, w).start()

    for at in range(len(tiles)):
        transform(1, at)
    for at in range(len(tiles)):
        transform(0, at)
        for w in range(at * waves // len(tiles), (at + 1) * waves // len(tiles)):
            cut(1, w)
    for w in range(waves):
        cut(0, w)
    for half in range(2):
        for w in range(waves):
            departure(half, w).wait()


def to_bands(plan, info, starts, bands, part, tables, depth, level_cols):
    latitudes = tables[0].shape[0]
    levels = part.shape[2]
    columns = 4 * levels
    tile = [0] + list(range(latitudes // 5, latitudes + 1, 2 * latitudes // 5))
    smem, vmem = pl.BlockSpec(memory_space=pltpu.SMEM), pl.BlockSpec(memory_space=pltpu.VMEM)
    messages = bands.shape[0] * columns // level_cols
    grid = pltpu.VMEM((ceil_to(latitudes + depth, 8) + 8, columns), F32)
    held = 2 * (latitudes + columns) * sum(plan.widths) + 8 * (latitudes + depth) * columns
    held += 4 * messages * depth * ceil_to(level_cols, 128) + 2 * part.size
    limit = max(52 * 1024 * 1024, held + 4 * 1024 * 1024)
    return pl.pallas_call(
        functools.partial(grid_kernel, plan, levels, latitudes, depth, level_cols, tile),
        out_shape=jax.ShapeDtypeStruct((messages, 2, depth, level_cols), BF),
        in_specs=[smem, smem, smem, vmem] + [pl.BlockSpec(memory_space=pl.ANY)] * 2,
        out_specs=pl.BlockSpec(memory_space=pl.ANY),
        scratch_shapes=[
            pltpu.VMEM(tables[0].shape, BF),
            pltpu.VMEM(tables[1].shape, BF),
            pltpu.VMEM((plan.widths[0], columns), BF),
            pltpu.VMEM((plan.widths[1], columns), BF),
            grid,
            grid,
            pltpu.VMEM((messages, 2, depth, level_cols), BF),
            pltpu.SemaphoreType.DMA((2, len(tile) - 1)),
            pltpu.SemaphoreType.DMA((2, bands.shape[0])),
        ],
        compiler_params=pltpu.CompilerParams(vmem_limit_bytes=limit),
        cost_estimate=pl.CostEstimate(
            flops=2 * latitudes * sum(plan.widths) * columns,
            bytes_accessed=2 * latitudes * sum(plan.widths) + 4 * messages * depth * level_cols,
            transcendentals=0,
        ),
        name="grid_bands",
    )(info, starts, bands, part, *tables)


def per_device(control, covariance, legendre, pair_order, band_rows):
    axes = ("wave", "lev")
    waves, lev_count = lax.axis_size("wave"), lax.axis_size("lev")
    _, slots, columns = control.shape
    degrees, levels = slots - 1, columns // 4
    latitudes = legendre.shape[2]
    depth = 5 * latitudes // (4 * waves)
    level_cols = columns // lev_count
    plan = Plan(waves * lev_count, degrees)
    group, block = plan.group, plan.block
    me = lax.axis_index("wave") * lev_count + lax.axis_index("lev")
    is_high = (me >= group).astype(jnp.int32)
    lowest = pair_order[0]
    halves = [list(range(group)), list(range(group, 2 * group))]

    def exchange(rows):
        return lax.all_to_all(rows, axes, split_axis=0, concat_axis=0, tiled=True, axis_index_groups=halves)

    plane = group // 2
    whole = range(2 * group)
    far = [(d, (3 - d // plane) * plane + d % plane) for d in whole]
    near = [(d, d // plane * plane + plane - 1 - d % plane) for d in whole]
    pieces = 2 if block % 2 == 0 else 1
    own = cast_blocks(covariance, is_high[None], pieces)
    *own, control = lax.optimization_barrier((*own, control))
    far_blocks = [lax.ppermute(part, axes, far) for part in own]
    near_blocks = [lax.ppermute(part, axes, near) for part in own]

    def fold_block(rank):
        rank = jnp.where(is_high == 1, group - 1 - rank, rank)
        return rank // plane * plane + plane - 1 - rank % plane

    def slots_of(message, fold, folded, used):
        degree = fold_block(message) * block + fold
        upper = jnp.where(folded, degree - lowest, degrees - 1 - degree - lowest)
        upper = jnp.where(used & (upper >= 0), upper, -1)
        lower = jnp.where(used & folded & (degree <= lowest), degrees - degree, -1)
        return upper, lower

    upper, lower = slots_of(*plan.message_rows())
    sent = jnp.where(upper >= 0, upper, lower)
    received = exchange(pack(plan, control[0], pair_order, sent[:, None]))

    tables = make_tables(plan, legendre[0], slots_of(*plan.transform_rows()))

    info = jnp.stack([is_high, fold_block(me - group * is_high) * block])
    received, tables = lax.optimization_barrier((received, tables))
    filtered = exchange(filter_rows(plan, info, received, near_blocks, far_blocks))

    extra_block = lowest // block
    extra_message = fold_block(extra_block)
    extra_row = plan.extra_row(extra_message, lowest - extra_block * block)
    where = jnp.stack([extra_message, extra_row])
    starts = jnp.cumsum(band_rows) - band_rows
    outgoing = to_bands(plan, where, starts, band_rows, filtered, tables, depth, level_cols)
    outgoing = outgoing.reshape(-1, depth, level_cols)
    return lax.all_to_all(outgoing, axes, split_axis=0, concat_axis=0, tiled=True)


def solution(mesh):
    return jax.shard_map(
        per_device,
        mesh=mesh,
        in_specs=(
            P(("wave", "lev"), None, None),
            P(("wave", "lev"), None, None),
            P(("wave", "lev"), None, None),
            P(("wave", "lev")),
            P(),
        ),
        out_specs=P(None, "wave", "lev"),
        check_vma=False,
    )
```

```python
import functools

import jax
import jax.numpy as jnp
import numpy as np
from jax import lax
from jax.experimental import pallas as pl
from jax.experimental.pallas import tpu as pltpu
from jax.sharding import PartitionSpec as P

BF = jnp.bfloat16
F32 = jnp.float32
SUB = 16
DIGIT = 16


def ceil_to(value, step):
    return (value + step - 1) // step * step


class Plan:
    def __init__(self, devices, degrees):
        self.devices = devices
        self.group = devices // 2
        self.degrees = degrees
        self.block = degrees // devices
        self.chunks = []
        row, fold = 0, 0
        for count in self.fold_counts(self.block):
            self.chunks.append((row, fold, count))
            row += ceil_to(2 * count, SUB)
            fold += count
        self.rows = row
        whole = [(at, n) for at, (_, _, n) in enumerate(self.chunks) if n % SUB == 0]
        mixed = [(at, n) for at, (_, _, n) in enumerate(self.chunks) if n % SUB]
        lower = [(at, 0, n) for at, n in whole] + [(at, 0, ceil_to(2 * n, SUB)) for at, n in mixed]
        self.segments = lower + [(at, n, n) for at, n in whole]
        self.widths = [
            self.group * sum(n for _, _, n in self.segments),
            self.group * sum(n for _, _, n in lower),
        ]

    @staticmethod
    def fold_counts(block):
        return (block - 8, 8) if block % SUB == 8 and block > 8 else (block,)

    def chunk_rows(self, at):
        _, first, count = self.chunks[at]
        height = ceil_to(2 * count, SUB)
        fold = np.zeros(height, np.int32)
        fold[:2 * count] = first + np.tile(np.arange(count), 2)
        row = np.arange(height)
        return fold, row < count, row < 2 * count

    def message_rows(self):
        tables = [self.chunk_rows(at) for at in range(len(self.chunks))]
        one = [np.concatenate(column) for column in zip(*tables)]
        return [np.repeat(np.arange(self.group, dtype=np.int32), self.rows)] + [
            np.tile(column, self.group) for column in one
        ]

    def transform_rows(self):
        parts = []
        for at, first, count in self.segments:
            columns = [column[first:first + count] for column in self.chunk_rows(at)]
            parts.append(
                [np.repeat(np.arange(self.group, dtype=np.int32), count)]
                + [np.tile(column, self.group) for column in columns]
            )
        return [np.concatenate(column) for column in zip(*parts)]

    def extra_row(self, message, fold):
        base, result = 0, jnp.int32(0)
        for at, first, count in self.segments:
            if first == 0:
                start = self.chunks[at][1]
                here = (fold >= start) & (fold < start + self.chunks[at][2])
                result = jnp.where(here, base + message * count + fold - start, result)
            base += self.group * count
        return result


def cast_kernel(plan, chunk, steps, info_ref, blocks_ref, out_ref, held_ref, cast_ref, in_sems, out_sems):
    _, fold, count = chunk
    start = jnp.where(info_ref[0] == 1, plan.block - fold - count, fold)
    each = count // steps
    arrivals, departures = [], []
    for at in range(steps):
        here = pl.ds(at * each, each)
        arrivals.append(
            pltpu.make_async_copy(blocks_ref.at[pl.ds(start + at * each, each)], held_ref.at[here], in_sems.at[at])
        )
        arrivals[at].start()
        departures.append(pltpu.make_async_copy(cast_ref.at[here], out_ref.at[here], out_sems.at[at]))
    for at in range(steps):
        arrivals[at].wait()
        cast_ref[at * each:(at + 1) * each] = held_ref[at * each:(at + 1) * each].astype(BF)
        departures[at].start()
    for departure in departures:
        departure.wait()


def cast_blocks(plan, at, blocks, info):
    count = plan.chunks[at][2]
    steps = 4 if count % 32 == 0 else 1
    shape = (count, *blocks.shape[1:])
    anywhere = pl.BlockSpec(memory_space=pl.ANY)
    return pl.pallas_call(
        functools.partial(cast_kernel, plan, plan.chunks[at], steps),
        out_shape=jax.ShapeDtypeStruct(shape, BF),
        in_specs=[pl.BlockSpec(memory_space=pltpu.SMEM), anywhere],
        out_specs=anywhere,
        scratch_shapes=[
            pltpu.VMEM(shape, F32),
            pltpu.VMEM(shape, BF),
            pltpu.SemaphoreType.DMA((steps,)),
            pltpu.SemaphoreType.DMA((steps,)),
        ],
        compiler_params=pltpu.CompilerParams(vmem_limit_bytes=56 * 1024 * 1024),
        cost_estimate=pl.CostEstimate(flops=1, bytes_accessed=6 * count, transcendentals=0),
        name="cast_blocks",
    )(info, blocks)


def pack_kernel(plan, levels, info_ref, slot_ref, control_ref, out_ref):
    slots = control_ref.shape[0]
    messages = out_ref.shape[0]
    even = slots - 1
    rows = messages * plan.rows
    slot = slot_ref[...]
    pick = (slot == lax.broadcasted_iota(jnp.int32, (rows, even), 1)).astype(F32).astype(BF)
    got = jnp.dot(pick, control_ref[:even, :], preferred_element_type=F32)
    last = control_ref[even:slots, :].astype(F32)
    got = jnp.where(slot == even, last, got).astype(BF)
    extra_slot = plan.degrees - info_ref[0]
    lane = lax.broadcasted_iota(jnp.int32, (SUB, even), 1)
    first = lax.broadcasted_iota(jnp.int32, (SUB, even), 0) == 0
    choose = jnp.where(first & (lane == extra_slot), 1.0, 0.0).astype(BF)
    extra = jnp.dot(choose, control_ref[:even, :], preferred_element_type=F32)
    extra = jnp.where(extra_slot == even, last, extra)
    place = lax.broadcasted_iota(jnp.int32, (SUB, levels), 0)
    tail = jnp.zeros((SUB, levels), F32)
    for c in range(4):
        tail = jnp.where(place == c, extra[0:1, c * levels:(c + 1) * levels], tail)
    high_digit = (info_ref[0] // DIGIT).astype(F32)
    low_digit = (info_ref[0] % DIGIT).astype(F32)
    tail = jnp.where(place == 4, high_digit, jnp.where(place == 5, low_digit, tail)).astype(BF)
    for k in range(messages):
        for c in range(4):
            out_ref[k, c * plan.rows:(c + 1) * plan.rows, :] = got[
                k * plan.rows:(k + 1) * plan.rows, c * levels:(c + 1) * levels
            ]
        out_ref[k, 4 * plan.rows:, :] = tail


def pack(plan, control, lowest, slots_of_rows):
    slots, columns = control.shape
    levels = columns // 4
    height = 4 * plan.rows + SUB
    per_step = max(1, min(plan.group, 320 // plan.rows))
    return pl.pallas_call(
        functools.partial(pack_kernel, plan, levels),
        grid=(plan.group // per_step,),
        out_shape=jax.ShapeDtypeStruct((plan.group, height, levels), BF),
        in_specs=[
            pl.BlockSpec(memory_space=pltpu.SMEM),
            pl.BlockSpec((per_step * plan.rows, 1), lambda k: (k, 0)),
            pl.BlockSpec((slots, columns), lambda k: (0, 0)),
        ],
        out_specs=pl.BlockSpec((per_step, height, levels), lambda k: (k, 0, 0)),
        compiler_params=pltpu.CompilerParams(vmem_limit_bytes=16 * 1024 * 1024),
        cost_estimate=pl.CostEstimate(flops=1, bytes_accessed=1, transcendentals=0),
        name="pack_rows",
    )(lowest, slots_of_rows, control)


def table_kernel(plan, upper_ref, lower_ref, legendre_ref, *refs):
    outs, picks = refs[:2], refs[2:]
    slots = legendre_ref.shape[0]
    even = slots - 1

    @pl.when(pl.program_id(0) == 0)
    def _():
        for index_ref, pick_ref in zip((upper_ref, lower_ref), picks):
            slot = lax.broadcasted_iota(jnp.int32, pick_ref.shape, 0)
            pick_ref[...] = jnp.where(slot == index_ref[...], 1.0, 0.0).astype(BF)

    def times(rows, picked):
        return lax.dot_general(rows, picked, (((0,), (0,)), ((), ())), preferred_element_type=F32)

    for out_ref, pick_ref in zip(outs, picks):
        got = times(legendre_ref[:even, :], pick_ref[:even, :])
        last = jnp.concatenate(
            [legendre_ref[even:slots, :].astype(F32), jnp.zeros((SUB - 1, legendre_ref.shape[1]), F32)], axis=0
        ).astype(BF)
        out_ref[...] = (got + times(last, pick_ref[even:even + SUB, :])).astype(BF)


def make_tables(plan, legendre, slots_of_rows):
    slots, latitudes = legendre.shape
    tile = 256
    index = [rows[None, :width] for rows, width in zip(slots_of_rows, plan.widths)]
    return pl.pallas_call(
        functools.partial(table_kernel, plan),
        grid=(latitudes // tile,),
        out_shape=[jax.ShapeDtypeStruct((latitudes, width), BF) for width in plan.widths],
        in_specs=[pl.BlockSpec((1, width), lambda t: (0, 0)) for width in plan.widths]
        + [pl.BlockSpec((slots, tile), lambda t: (0, t))],
        out_specs=[pl.BlockSpec((tile, width), lambda t: (t, 0)) for width in plan.widths],
        scratch_shapes=[pltpu.VMEM((slots - 1 + SUB, width), BF) for width in plan.widths],
        compiler_params=pltpu.CompilerParams(vmem_limit_bytes=20 * 1024 * 1024),
        cost_estimate=pl.CostEstimate(
            flops=20 * latitudes * slots * sum(plan.widths), bytes_accessed=2 * legendre.size, transcendentals=0
        ),
        name="make_tables",
    )(*index, legendre)


def swap_matrix():
    i = lax.broadcasted_iota(jnp.int32, (SUB * SUB, SUB * SUB), 0)
    j = lax.broadcasted_iota(jnp.int32, (SUB * SUB, SUB * SUB), 1)
    return jnp.where((i // SUB == j % SUB) & (i % SUB == j // SUB), 1.0, 0.0).astype(BF)


def filter_kernel(plan, at, levels, info_ref, rows_ref, near_ref, far_ref, *refs):
    first, last = at == 0, at == len(plan.chunks) - 1
    before_ref = None if first else refs[0]
    out_ref, *after, held_ref, x_ref, y_ref, z_ref, in_sems, out_sems = refs[0 if first else 2:]
    row0, fold0, count = plan.chunks[at]
    height = ceil_to(2 * count, SUB)
    groups = plan.group // SUB
    first_fold = (info_ref[1] + fold0).astype(F32)
    swap = swap_matrix()

    near = pltpu.make_async_copy(near_ref, held_ref.at[info_ref[0]], in_sems.at[0])
    far = pltpu.make_async_copy(far_ref, held_ref.at[1 - info_ref[0]], in_sems.at[1])
    near.start()
    far.start()

    def turn(rows):
        return jnp.dot(swap, rows, preferred_element_type=F32)

    held = height * SUB
    tails = []
    for g in range(groups):
        sources = slice(g * SUB, (g + 1) * SUB)
        for r in range(0, height, SUB):
            parts = []
            for c in range(4):
                start = c * plan.rows + row0 + r
                parts.append(rows_ref[sources, start:start + SUB, :].reshape(SUB * SUB, levels))
            x_ref[g * held + r * SUB:g * held + (r + SUB) * SUB, :] = turn(jnp.concatenate(parts, axis=1)).astype(BF)
        tail = turn(rows_ref[sources, 4 * plan.rows:4 * plan.rows + SUB, :].reshape(SUB * SUB, levels))
        low = tail[4 * SUB:5 * SUB] * DIGIT + tail[5 * SUB:6 * SUB]
        if first:
            kept = jnp.zeros((4 * SUB, levels), F32)
        else:
            kept = before_ref[4 * SUB * g:4 * SUB * (g + 1), :]
        tails.append((tail[:4 * SUB].astype(BF), jnp.concatenate([low] * 4, axis=0), kept))
    near.wait()
    far.wait()

    for g in range(groups):
        sources = slice(g * SUB, (g + 1) * SUB)
        extra, low, kept = tails[g]
        for i in range(count):
            def stack(row):
                start = g * held + row * SUB
                return [x_ref[start:start + SUB, c * levels:(c + 1) * levels] for c in range(4)]

            rows = jnp.concatenate([*stack(i), *stack(count + i), extra], axis=0)
            matrices = jnp.concatenate([held_ref[0, i], held_ref[1, count - 1 - i]], axis=0)
            both = lax.dot_general(rows, matrices, (((1,), (1,)), ((), ())), preferred_element_type=F32)
            from_low, from_high = both[:4 * SUB, :levels], both[:, levels:]
            fold = first_fold + i
            mixed = jnp.where(low <= fold, from_low, from_high[:4 * SUB])
            kept = jnp.where(low == fold, from_high[8 * SUB:], kept)
            for row, value in ((i, mixed), (count + i, from_high[4 * SUB:8 * SUB])):
                value = value.astype(BF)
                for c in range(4):
                    y_ref[row * SUB:(row + 1) * SUB, c * levels:(c + 1) * levels] = value[c * SUB:(c + 1) * SUB]
        if height > 2 * count:
            y_ref[2 * count * SUB:height * SUB, :] = jnp.zeros(((height - 2 * count) * SUB, 4 * levels), BF)
        for r in range(0, height, SUB):
            back = turn(y_ref[r * SUB:(r + SUB) * SUB, :]).astype(BF)
            for c in range(4):
                z_ref[sources, c * height + r:c * height + r + SUB, :] = back[:, c * levels:(c + 1) * levels].reshape(
                    SUB, SUB, levels
                )
        if last:
            filled = jnp.concatenate([kept, jnp.zeros((12 * SUB, levels), F32)], axis=0).astype(BF)
            z_ref[sources, 4 * height:4 * height + SUB, :] = turn(filled).astype(BF).reshape(SUB, SUB, levels)
        else:
            after[0][4 * SUB * g:4 * SUB * (g + 1), :] = kept

    moves = [(c * height, c * plan.rows + row0, height) for c in range(4)]
    if last:
        moves.append((4 * height, 4 * plan.rows, SUB))
    departures = [
        pltpu.make_async_copy(z_ref.at[:, pl.ds(here, n), :], out_ref.at[:, pl.ds(there, n), :], out_sems.at[c])
        for c, (here, there, n) in enumerate(moves)
    ]
    for departure in departures:
        departure.start()
    for departure in departures:
        departure.wait()


def filter_rows(plan, at, info, received, near, far, before):
    levels = received.shape[2]
    count = plan.chunks[at][2]
    height = ceil_to(2 * count, SUB)
    last = at == len(plan.chunks) - 1
    smem, vmem = pl.BlockSpec(memory_space=pltpu.SMEM), pl.BlockSpec(memory_space=pltpu.VMEM)
    anywhere = pl.BlockSpec(memory_space=pl.ANY)
    out_shape = [jax.ShapeDtypeStruct(received.shape, BF)]
    if not last:
        out_shape.append(jax.ShapeDtypeStruct((4 * plan.group, levels), F32))
    return pl.pallas_call(
        functools.partial(filter_kernel, plan, at, levels),
        out_shape=out_shape,
        in_specs=[smem, vmem, anywhere, anywhere] + ([vmem, anywhere] if before else []),
        out_specs=[anywhere] + [vmem] * (len(out_shape) - 1),
        input_output_aliases={5: 0} if before else {},
        scratch_shapes=[
            pltpu.VMEM((2, count, levels, levels), BF),
            pltpu.VMEM((plan.group * height, 4 * levels), BF),
            pltpu.VMEM((height * SUB, 4 * levels), BF),
            pltpu.VMEM((plan.group, 4 * height + SUB, levels), BF),
            pltpu.SemaphoreType.DMA((2,)),
            pltpu.SemaphoreType.DMA((5,)),
        ],
        compiler_params=pltpu.CompilerParams(vmem_limit_bytes=20 * 1024 * 1024),
        cost_estimate=pl.CostEstimate(
            flops=2 * plan.group * 16 * count * levels * levels * 4,
            bytes_accessed=2 * 2 * received.size + 4 * count * levels * levels,
            transcendentals=0,
        ),
        name="filter_rows",
    )(info, received, near, far, *before)


def grid_kernel(plan, levels, latitudes, depth, level_cols, tile, info_ref, starts_ref, bands_ref, part_ref, *refs):
    tables, out_ref, held_tables = refs[:2], refs[2], refs[3:5]
    upper_ref, lower_ref, *grids, cut_ref, sems, out_sems = refs[5:]
    waves = bands_ref.shape[0]
    groups = 4 * levels // level_cols
    tiles = [slice(start, stop) for start, stop in zip(tile, tile[1:])]

    def copy(half, at):
        rows = tiles[at]
        return pltpu.make_async_copy(tables[half].at[rows], held_tables[half].at[rows], sems.at[half, at])

    for half in (1, 0):
        for at in range(len(tiles)):
            copy(half, at).start()

    base = 0
    for at, first, rows in plan.segments:
        for k in range(plan.group):
            for c in range(4):
                start = c * plan.rows + plan.chunks[at][0] + first
                cols = slice(c * levels, (c + 1) * levels)
                value = part_ref[k, start:start + rows, :]
                upper_ref[base + k * rows:base + (k + 1) * rows, cols] = value
                if base < plan.widths[1]:
                    lower_ref[base + k * rows:base + (k + 1) * rows, cols] = value
        base += plan.group * rows

    extra = part_ref[info_ref[0], 4 * plan.rows:4 * plan.rows + SUB, :]
    base = info_ref[1] // SUB * SUB
    place = pl.ds(pl.multiple_of(base, SUB), SUB)
    here = lax.broadcasted_iota(jnp.int32, (SUB, levels), 0) == info_ref[1] - base
    for c in range(4):
        cols = slice(c * levels, (c + 1) * levels)
        held = upper_ref[place, cols].astype(F32)
        lower_ref[place, cols] = jnp.where(here, extra[c:c + 1, :].astype(F32), held).astype(BF)

    def transform(half, at):
        copy(half, at).wait()
        rows = tiles[at]
        grids[half][rows, :] = jnp.dot(
            held_tables[half][rows, :], (upper_ref, lower_ref)[half][...], preferred_element_type=F32
        )

    def departure(half, w):
        messages = pl.ds(w * groups, groups)
        return pltpu.make_async_copy(cut_ref.at[messages, half], out_ref.at[messages, half], out_sems.at[half, w])

    def cut(half, w):
        place = lax.broadcasted_iota(jnp.int32, (8, 4 * levels), 0)
        start = starts_ref[w]
        base = start // 8 * 8
        offset = start - base

        def slab(at):
            held = grids[half][pl.ds(pl.multiple_of(base + at, 8), 8), :]
            return pltpu.roll(held, (8 - offset) % 8, axis=0)

        after = slab(0)
        done = []
        for r in range(0, depth, 8):
            now, after = after, slab(r + 8)
            got = jnp.where(place < 8 - offset, now, after)
            done.append(jnp.where(place < bands_ref[w] - r, got, 0.0))
            if len(done) == 2 or r + 8 == depth:
                rows = jnp.concatenate(done, axis=0).astype(BF)
                first = r + 8 - rows.shape[0]
                for g in range(groups):
                    cut_ref[w * groups + g, half, first:r + 8, :] = rows[:, g * level_cols:(g + 1) * level_cols]
                done = []
        departure(half, w).start()

    for at in range(len(tiles)):
        transform(1, at)
    for at in range(len(tiles)):
        transform(0, at)
        for w in range(at * waves // len(tiles), (at + 1) * waves // len(tiles)):
            cut(1, w)
    for w in range(waves):
        cut(0, w)
    for half in range(2):
        for w in range(waves):
            departure(half, w).wait()


def to_bands(plan, info, starts, bands, part, tables, depth, level_cols):
    latitudes = tables[0].shape[0]
    levels = part.shape[2]
    columns = 4 * levels
    tile = [0] + list(range(latitudes // 5, latitudes + 1, 2 * latitudes // 5))
    smem, vmem = pl.BlockSpec(memory_space=pltpu.SMEM), pl.BlockSpec(memory_space=pltpu.VMEM)
    messages = bands.shape[0] * columns // level_cols
    grid = pltpu.VMEM((ceil_to(latitudes + depth, 8) + 8, columns), F32)
    held = 2 * (latitudes + columns) * sum(plan.widths) + 8 * (latitudes + depth) * columns
    held += 4 * messages * depth * ceil_to(level_cols, 128) + 2 * part.size
    limit = max(52 * 1024 * 1024, held + 4 * 1024 * 1024)
    return pl.pallas_call(
        functools.partial(grid_kernel, plan, levels, latitudes, depth, level_cols, tile),
        out_shape=jax.ShapeDtypeStruct((messages, 2, depth, level_cols), BF),
        in_specs=[smem, smem, smem, vmem] + [pl.BlockSpec(memory_space=pl.ANY)] * 2,
        out_specs=pl.BlockSpec(memory_space=pl.ANY),
        scratch_shapes=[
            pltpu.VMEM(tables[0].shape, BF),
            pltpu.VMEM(tables[1].shape, BF),
            pltpu.VMEM((plan.widths[0], columns), BF),
            pltpu.VMEM((plan.widths[1], columns), BF),
            grid,
            grid,
            pltpu.VMEM((messages, 2, depth, level_cols), BF),
            pltpu.SemaphoreType.DMA((2, len(tile) - 1)),
            pltpu.SemaphoreType.DMA((2, bands.shape[0])),
        ],
        compiler_params=pltpu.CompilerParams(vmem_limit_bytes=limit),
        cost_estimate=pl.CostEstimate(
            flops=2 * latitudes * sum(plan.widths) * columns,
            bytes_accessed=2 * latitudes * sum(plan.widths) + 4 * messages * depth * level_cols,
            transcendentals=0,
        ),
        name="grid_bands",
    )(info, starts, bands, part, *tables)


def per_device(control, covariance, legendre, pair_order, band_rows):
    axes = ("wave", "lev")
    waves, lev_count = lax.axis_size("wave"), lax.axis_size("lev")
    _, slots, columns = control.shape
    degrees, levels = slots - 1, columns // 4
    latitudes = legendre.shape[2]
    depth = 5 * latitudes // (4 * waves)
    level_cols = columns // lev_count
    plan = Plan(waves * lev_count, degrees)
    group, block = plan.group, plan.block
    me = lax.axis_index("wave") * lev_count + lax.axis_index("lev")
    is_high = (me >= group).astype(jnp.int32)
    lowest = pair_order[0]
    halves = [list(range(group)), list(range(group, 2 * group))]

    def exchange(rows):
        return lax.all_to_all(rows, axes, split_axis=0, concat_axis=0, tiled=True, axis_index_groups=halves)

    plane = group // 2
    whole = range(2 * group)
    far = [(d, (3 - d // plane) * plane + d % plane) for d in whole]
    near = [(d, d // plane * plane + plane - 1 - d % plane) for d in whole]
    far_blocks, near_blocks = [], []

    def swap_chunk(own):
        far_blocks.append(lax.ppermute(own, axes, far))
        near_blocks.append(lax.ppermute(own, axes, near))

    own = cast_blocks(plan, 0, covariance, is_high[None])
    own, control = lax.optimization_barrier((own, control))
    swap_chunk(own)

    def fold_block(rank):
        rank = jnp.where(is_high == 1, group - 1 - rank, rank)
        return rank // plane * plane + plane - 1 - rank % plane

    def slots_of(message, fold, folded, used):
        degree = fold_block(message) * block + fold
        upper = jnp.where(folded, degree - lowest, degrees - 1 - degree - lowest)
        upper = jnp.where(used & (upper >= 0), upper, -1)
        lower = jnp.where(used & folded & (degree <= lowest), degrees - degree, -1)
        return upper, lower

    upper, lower = slots_of(*plan.message_rows())
    sent = jnp.where(upper >= 0, upper, lower)
    packed = pack(plan, control[0], pair_order, sent[:, None])
    packed, legendre = lax.optimization_barrier((packed, legendre))
    received = exchange(packed)

    tables = make_tables(plan, legendre[0], slots_of(*plan.transform_rows()))
    for at in range(1, len(plan.chunks)):
        covariance, tables = lax.optimization_barrier((covariance, tables))
        swap_chunk(cast_blocks(plan, at, covariance, is_high[None]))

    info = jnp.stack([is_high, fold_block(me - group * is_high) * block])
    received, tables = lax.optimization_barrier((received, tables))
    before = ()
    for at, (near_block, far_block) in enumerate(zip(near_blocks, far_blocks)):
        result, *extras = filter_rows(plan, at, info, received, near_block, far_block, before)
        before = (*extras, result)
    filtered = exchange(result)

    extra_block = lowest // block
    extra_message = fold_block(extra_block)
    extra_row = plan.extra_row(extra_message, lowest - extra_block * block)
    where = jnp.stack([extra_message, extra_row])
    starts = jnp.cumsum(band_rows) - band_rows
    outgoing = to_bands(plan, where, starts, band_rows, filtered, tables, depth, level_cols)
    outgoing = outgoing.reshape(-1, depth, level_cols)
    return lax.all_to_all(outgoing, axes, split_axis=0, concat_axis=0, tiled=True)


def solution(mesh):
    return jax.shard_map(
        per_device,
        mesh=mesh,
        in_specs=(
            P(("wave", "lev"), None, None),
            P(("wave", "lev"), None, None),
            P(("wave", "lev"), None, None),
            P(("wave", "lev")),
            P(),
        ),
        out_specs=P(None, "wave", "lev"),
        check_vma=False,
    )
```

```python
import functools

import jax
import jax.numpy as jnp
import numpy as np
from jax import lax
from jax.experimental import pallas as pl
from jax.experimental.pallas import tpu as pltpu
from jax.sharding import PartitionSpec as P

BF = jnp.bfloat16
F32 = jnp.float32
SUB = 16
DIGIT = 16


def ceil_to(value, step):
    return (value + step - 1) // step * step


class Plan:
    def __init__(self, devices, degrees):
        self.devices = devices
        self.group = devices // 2
        self.degrees = degrees
        self.block = degrees // devices
        self.chunks = []
        row, fold = 0, 0
        for count in self.fold_counts(self.block):
            self.chunks.append((row, fold, count))
            row += ceil_to(2 * count, SUB)
            fold += count
        self.rows = row
        whole = [(at, n) for at, (_, _, n) in enumerate(self.chunks) if n % SUB == 0]
        mixed = [(at, n) for at, (_, _, n) in enumerate(self.chunks) if n % SUB]
        lower = [(at, 0, n) for at, n in whole] + [(at, 0, ceil_to(2 * n, SUB)) for at, n in mixed]
        self.segments = lower + [(at, n, n) for at, n in whole]
        self.widths = [
            self.group * sum(n for _, _, n in self.segments),
            self.group * sum(n for _, _, n in lower),
        ]

    @staticmethod
    def fold_counts(block):
        return (block - 8, 8) if block % SUB == 8 and block > 8 else (block,)

    def chunk_rows(self, at):
        _, first, count = self.chunks[at]
        height = ceil_to(2 * count, SUB)
        fold = np.zeros(height, np.int32)
        fold[:2 * count] = first + np.tile(np.arange(count), 2)
        row = np.arange(height)
        return fold, row < count, row < 2 * count

    def message_rows(self):
        tables = [self.chunk_rows(at) for at in range(len(self.chunks))]
        one = [np.concatenate(column) for column in zip(*tables)]
        return [np.repeat(np.arange(self.group, dtype=np.int32), self.rows)] + [
            np.tile(column, self.group) for column in one
        ]

    def transform_rows(self):
        parts = []
        for at, first, count in self.segments:
            columns = [column[first:first + count] for column in self.chunk_rows(at)]
            parts.append(
                [np.repeat(np.arange(self.group, dtype=np.int32), count)]
                + [np.tile(column, self.group) for column in columns]
            )
        return [np.concatenate(column) for column in zip(*parts)]

    def extra_row(self, message, fold):
        base, result = 0, jnp.int32(0)
        for at, first, count in self.segments:
            if first == 0:
                start = self.chunks[at][1]
                here = (fold >= start) & (fold < start + self.chunks[at][2])
                result = jnp.where(here, base + message * count + fold - start, result)
            base += self.group * count
        return result


def cast_kernel(plan, chunk, steps, info_ref, blocks_ref, out_ref, held_ref, cast_ref, in_sems, out_sems):
    _, fold, count = chunk
    start = jnp.where(info_ref[0] == 1, plan.block - fold - count, fold)
    each = count // steps
    arrivals, departures = [], []
    for at in range(steps):
        here = pl.ds(at * each, each)
        arrivals.append(
            pltpu.make_async_copy(blocks_ref.at[pl.ds(start + at * each, each)], held_ref.at[here], in_sems.at[at])
        )
        arrivals[at].start()
        departures.append(pltpu.make_async_copy(cast_ref.at[here], out_ref.at[here], out_sems.at[at]))
    for at in range(steps):
        arrivals[at].wait()
        cast_ref[at * each:(at + 1) * each] = held_ref[at * each:(at + 1) * each].astype(BF)
        departures[at].start()
    for departure in departures:
        departure.wait()


def cast_blocks(plan, at, blocks, info):
    count = plan.chunks[at][2]
    steps = 4 if count % 32 == 0 else 1
    shape = (count, *blocks.shape[1:])
    anywhere = pl.BlockSpec(memory_space=pl.ANY)
    return pl.pallas_call(
        functools.partial(cast_kernel, plan, plan.chunks[at], steps),
        out_shape=jax.ShapeDtypeStruct(shape, BF),
        in_specs=[pl.BlockSpec(memory_space=pltpu.SMEM), anywhere],
        out_specs=anywhere,
        scratch_shapes=[
            pltpu.VMEM(shape, F32),
            pltpu.VMEM(shape, BF),
            pltpu.SemaphoreType.DMA((steps,)),
            pltpu.SemaphoreType.DMA((steps,)),
        ],
        compiler_params=pltpu.CompilerParams(vmem_limit_bytes=56 * 1024 * 1024),
        cost_estimate=pl.CostEstimate(flops=1, bytes_accessed=6 * count, transcendentals=0),
        name="cast_blocks",
    )(info, blocks)


def pack_kernel(plan, levels, info_ref, slot_ref, control_ref, out_ref):
    slots = control_ref.shape[0]
    messages = out_ref.shape[0]
    even = slots - 1
    rows = messages * plan.rows
    slot = slot_ref[...]
    pick = (slot == lax.broadcasted_iota(jnp.int32, (rows, even), 1)).astype(F32).astype(BF)
    got = jnp.dot(pick, control_ref[:even, :], preferred_element_type=F32)
    last = control_ref[even:slots, :].astype(F32)
    got = jnp.where(slot == even, last, got).astype(BF)
    extra_slot = plan.degrees - info_ref[0]
    lane = lax.broadcasted_iota(jnp.int32, (SUB, even), 1)
    first = lax.broadcasted_iota(jnp.int32, (SUB, even), 0) == 0
    choose = jnp.where(first & (lane == extra_slot), 1.0, 0.0).astype(BF)
    extra = jnp.dot(choose, control_ref[:even, :], preferred_element_type=F32)
    extra = jnp.where(extra_slot == even, last, extra)
    place = lax.broadcasted_iota(jnp.int32, (SUB, levels), 0)
    tail = jnp.zeros((SUB, levels), F32)
    for c in range(4):
        tail = jnp.where(place == c, extra[0:1, c * levels:(c + 1) * levels], tail)
    high_digit = (info_ref[0] // DIGIT).astype(F32)
    low_digit = (info_ref[0] % DIGIT).astype(F32)
    tail = jnp.where(place == 4, high_digit, jnp.where(place == 5, low_digit, tail)).astype(BF)
    for k in range(messages):
        for c in range(4):
            out_ref[k, c * plan.rows:(c + 1) * plan.rows, :] = got[
                k * plan.rows:(k + 1) * plan.rows, c * levels:(c + 1) * levels
            ]
        out_ref[k, 4 * plan.rows:, :] = tail


def pack(plan, control, lowest, slots_of_rows):
    slots, columns = control.shape
    levels = columns // 4
    height = 4 * plan.rows + SUB
    per_step = max(1, min(plan.group, 320 // plan.rows))
    return pl.pallas_call(
        functools.partial(pack_kernel, plan, levels),
        grid=(plan.group // per_step,),
        out_shape=jax.ShapeDtypeStruct((plan.group, height, levels), BF),
        in_specs=[
            pl.BlockSpec(memory_space=pltpu.SMEM),
            pl.BlockSpec((per_step * plan.rows, 1), lambda k: (k, 0)),
            pl.BlockSpec((slots, columns), lambda k: (0, 0)),
        ],
        out_specs=pl.BlockSpec((per_step, height, levels), lambda k: (k, 0, 0)),
        compiler_params=pltpu.CompilerParams(vmem_limit_bytes=16 * 1024 * 1024),
        cost_estimate=pl.CostEstimate(flops=1, bytes_accessed=1, transcendentals=0),
        name="pack_rows",
    )(lowest, slots_of_rows, control)


def table_kernel(plan, upper_ref, lower_ref, legendre_ref, *refs):
    outs, picks = refs[:2], refs[2:]
    slots = legendre_ref.shape[0]
    even = slots - 1

    @pl.when(pl.program_id(0) == 0)
    def _():
        for index_ref, pick_ref in zip((upper_ref, lower_ref), picks):
            slot = lax.broadcasted_iota(jnp.int32, pick_ref.shape, 0)
            pick_ref[...] = jnp.where(slot == index_ref[...], 1.0, 0.0).astype(BF)

    def times(rows, picked):
        return lax.dot_general(rows, picked, (((0,), (0,)), ((), ())), preferred_element_type=F32)

    for out_ref, pick_ref in zip(outs, picks):
        got = times(legendre_ref[:even, :], pick_ref[:even, :])
        last = jnp.concatenate(
            [legendre_ref[even:slots, :].astype(F32), jnp.zeros((SUB - 1, legendre_ref.shape[1]), F32)], axis=0
        ).astype(BF)
        out_ref[...] = (got + times(last, pick_ref[even:even + SUB, :])).astype(BF)


def make_tables(plan, legendre, slots_of_rows):
    slots, latitudes = legendre.shape
    tile = 256
    index = [rows[None, :width] for rows, width in zip(slots_of_rows, plan.widths)]
    return pl.pallas_call(
        functools.partial(table_kernel, plan),
        grid=(latitudes // tile,),
        out_shape=[jax.ShapeDtypeStruct((latitudes, width), BF) for width in plan.widths],
        in_specs=[pl.BlockSpec((1, width), lambda t: (0, 0)) for width in plan.widths]
        + [pl.BlockSpec((slots, tile), lambda t: (0, t))],
        out_specs=[pl.BlockSpec((tile, width), lambda t: (t, 0)) for width in plan.widths],
        scratch_shapes=[pltpu.VMEM((slots - 1 + SUB, width), BF) for width in plan.widths],
        compiler_params=pltpu.CompilerParams(vmem_limit_bytes=20 * 1024 * 1024),
        cost_estimate=pl.CostEstimate(
            flops=20 * latitudes * slots * sum(plan.widths), bytes_accessed=2 * legendre.size, transcendentals=0
        ),
        name="make_tables",
    )(*index, legendre)


def swap_matrix():
    i = lax.broadcasted_iota(jnp.int32, (SUB * SUB, SUB * SUB), 0)
    j = lax.broadcasted_iota(jnp.int32, (SUB * SUB, SUB * SUB), 1)
    return jnp.where((i // SUB == j % SUB) & (i % SUB == j // SUB), 1.0, 0.0).astype(BF)


def filter_kernel(plan, at, levels, info_ref, rows_ref, near_ref, far_ref, *refs):
    first, last = at == 0, at == len(plan.chunks) - 1
    before_ref = None if first else refs[0]
    out_ref, *after, held_ref, x_ref, y_ref, z_ref, in_sems, out_sems = refs[0 if first else 2:]
    row0, fold0, count = plan.chunks[at]
    height = ceil_to(2 * count, SUB)
    groups = plan.group // SUB
    first_fold = (info_ref[1] + fold0).astype(F32)
    swap = swap_matrix()

    near = pltpu.make_async_copy(near_ref, held_ref.at[info_ref[0]], in_sems.at[0])
    far = pltpu.make_async_copy(far_ref, held_ref.at[1 - info_ref[0]], in_sems.at[1])
    near.start()
    far.start()

    def turn(rows):
        return jnp.dot(swap, rows, preferred_element_type=F32)

    held = height * SUB
    tails = []
    for g in range(groups):
        sources = slice(g * SUB, (g + 1) * SUB)
        for r in range(0, height, SUB):
            parts = []
            for c in range(4):
                start = c * plan.rows + row0 + r
                parts.append(rows_ref[sources, start:start + SUB, :].reshape(SUB * SUB, levels))
            x_ref[g * held + r * SUB:g * held + (r + SUB) * SUB, :] = turn(jnp.concatenate(parts, axis=1)).astype(BF)
        tail = turn(rows_ref[sources, 4 * plan.rows:4 * plan.rows + SUB, :].reshape(SUB * SUB, levels))
        low = tail[4 * SUB:5 * SUB] * DIGIT + tail[5 * SUB:6 * SUB]
        if first:
            kept = jnp.zeros((4 * SUB, levels), F32)
        else:
            kept = before_ref[4 * SUB * g:4 * SUB * (g + 1), :]
        tails.append((tail[:4 * SUB].astype(BF), jnp.concatenate([low] * 4, axis=0), kept))
    near.wait()
    far.wait()

    for g in range(groups):
        sources = slice(g * SUB, (g + 1) * SUB)
        extra, low, kept = tails[g]
        for i in range(count):
            def stack(row):
                start = g * held + row * SUB
                return [x_ref[start:start + SUB, c * levels:(c + 1) * levels] for c in range(4)]

            rows = jnp.concatenate([*stack(i), *stack(count + i), extra], axis=0)
            matrices = jnp.concatenate([held_ref[0, i], held_ref[1, count - 1 - i]], axis=0)
            both = lax.dot_general(rows, matrices, (((1,), (1,)), ((), ())), preferred_element_type=F32)
            from_low, from_high = both[:4 * SUB, :levels], both[:, levels:]
            fold = first_fold + i
            mixed = jnp.where(low <= fold, from_low, from_high[:4 * SUB])
            kept = jnp.where(low == fold, from_high[8 * SUB:], kept)
            for row, value in ((i, mixed), (count + i, from_high[4 * SUB:8 * SUB])):
                value = value.astype(BF)
                for c in range(4):
                    y_ref[row * SUB:(row + 1) * SUB, c * levels:(c + 1) * levels] = value[c * SUB:(c + 1) * SUB]
        if height > 2 * count:
            y_ref[2 * count * SUB:height * SUB, :] = jnp.zeros(((height - 2 * count) * SUB, 4 * levels), BF)
        for r in range(0, height, SUB):
            back = turn(y_ref[r * SUB:(r + SUB) * SUB, :]).astype(BF)
            for c in range(4):
                z_ref[sources, c * height + r:c * height + r + SUB, :] = back[:, c * levels:(c + 1) * levels].reshape(
                    SUB, SUB, levels
                )
        if last:
            filled = jnp.concatenate([kept, jnp.zeros((12 * SUB, levels), F32)], axis=0).astype(BF)
            z_ref[sources, 4 * height:4 * height + SUB, :] = turn(filled).astype(BF).reshape(SUB, SUB, levels)
        else:
            after[0][4 * SUB * g:4 * SUB * (g + 1), :] = kept

    moves = [(c * height, c * plan.rows + row0, height) for c in range(4)]
    if last:
        moves.append((4 * height, 4 * plan.rows, SUB))
    departures = [
        pltpu.make_async_copy(z_ref.at[:, pl.ds(here, n), :], out_ref.at[:, pl.ds(there, n), :], out_sems.at[c])
        for c, (here, there, n) in enumerate(moves)
    ]
    for departure in departures:
        departure.start()
    for departure in departures:
        departure.wait()


def filter_rows(plan, at, info, received, near, far, before):
    levels = received.shape[2]
    count = plan.chunks[at][2]
    height = ceil_to(2 * count, SUB)
    last = at == len(plan.chunks) - 1
    smem, vmem = pl.BlockSpec(memory_space=pltpu.SMEM), pl.BlockSpec(memory_space=pltpu.VMEM)
    anywhere = pl.BlockSpec(memory_space=pl.ANY)
    out_shape = [jax.ShapeDtypeStruct(received.shape, BF)]
    if not last:
        out_shape.append(jax.ShapeDtypeStruct((4 * plan.group, levels), F32))
    return pl.pallas_call(
        functools.partial(filter_kernel, plan, at, levels),
        out_shape=out_shape,
        in_specs=[smem, vmem, anywhere, anywhere] + ([vmem, anywhere] if before else []),
        out_specs=[anywhere] + [vmem] * (len(out_shape) - 1),
        input_output_aliases={5: 0} if before else {},
        scratch_shapes=[
            pltpu.VMEM((2, count, levels, levels), BF),
            pltpu.VMEM((plan.group * height, 4 * levels), BF),
            pltpu.VMEM((height * SUB, 4 * levels), BF),
            pltpu.VMEM((plan.group, 4 * height + SUB, levels), BF),
            pltpu.SemaphoreType.DMA((2,)),
            pltpu.SemaphoreType.DMA((5,)),
        ],
        compiler_params=pltpu.CompilerParams(vmem_limit_bytes=20 * 1024 * 1024),
        cost_estimate=pl.CostEstimate(
            flops=2 * plan.group * 16 * count * levels * levels * 4,
            bytes_accessed=2 * 2 * received.size + 4 * count * levels * levels,
            transcendentals=0,
        ),
        name="filter_rows",
    )(info, received, near, far, *before)


def grid_kernel(plan, levels, latitudes, depth, level_cols, tile, info_ref, starts_ref, bands_ref, part_ref, *refs):
    tables, out_ref, held_tables = refs[:2], refs[2], refs[3:5]
    upper_ref, lower_ref, *grids, cut_ref, sems, out_sems = refs[5:]
    waves = bands_ref.shape[0]
    groups = 4 * levels // level_cols
    tiles = [[slice(start, stop) for start, stop in zip(edges, edges[1:])] for edges in tile]

    def copy(half, at):
        rows = tiles[half][at]
        return pltpu.make_async_copy(tables[half].at[rows], held_tables[half].at[rows], sems.at[half, at])

    for half in (1, 0):
        for at in range(len(tiles[half])):
            copy(half, at).start()

    base = 0
    for at, first, rows in plan.segments:
        for k in range(plan.group):
            for c in range(4):
                start = c * plan.rows + plan.chunks[at][0] + first
                cols = slice(c * levels, (c + 1) * levels)
                value = part_ref[k, start:start + rows, :]
                upper_ref[base + k * rows:base + (k + 1) * rows, cols] = value
                if base < plan.widths[1]:
                    lower_ref[base + k * rows:base + (k + 1) * rows, cols] = value
        base += plan.group * rows

    extra = part_ref[info_ref[0], 4 * plan.rows:4 * plan.rows + SUB, :]
    base = info_ref[1] // SUB * SUB
    place = pl.ds(pl.multiple_of(base, SUB), SUB)
    here = lax.broadcasted_iota(jnp.int32, (SUB, levels), 0) == info_ref[1] - base
    for c in range(4):
        cols = slice(c * levels, (c + 1) * levels)
        held = upper_ref[place, cols].astype(F32)
        lower_ref[place, cols] = jnp.where(here, extra[c:c + 1, :].astype(F32), held).astype(BF)

    def transform(half, at):
        copy(half, at).wait()
        rows = tiles[half][at]
        grids[half][rows, :] = jnp.dot(
            held_tables[half][rows, :], (upper_ref, lower_ref)[half][...], preferred_element_type=F32
        )

    def departure(half, w):
        messages = pl.ds(w * groups, groups)
        return pltpu.make_async_copy(cut_ref.at[messages, half], out_ref.at[messages, half], out_sems.at[half, w])

    def cut(half, w):
        place = lax.broadcasted_iota(jnp.int32, (8, 4 * levels), 0)
        start = starts_ref[w]
        base = start // 8 * 8
        offset = start - base

        def slab(at):
            held = grids[half][pl.ds(pl.multiple_of(base + at, 8), 8), :]
            return pltpu.roll(held, (8 - offset) % 8, axis=0)

        after = slab(0)
        done = []
        for r in range(0, depth, 8):
            now, after = after, slab(r + 8)
            got = jnp.where(place < 8 - offset, now, after)
            done.append(jnp.where(place < bands_ref[w] - r, got, 0.0))
            if len(done) == 2 or r + 8 == depth:
                rows = jnp.concatenate(done, axis=0).astype(BF)
                first = r + 8 - rows.shape[0]
                for g in range(groups):
                    cut_ref[w * groups + g, half, first:r + 8, :] = rows[:, g * level_cols:(g + 1) * level_cols]
                done = []
        departure(half, w).start()

    for at in range(len(tiles[1])):
        transform(1, at)
    todo = [[w for w in range(waves)] for _ in range(2)]
    made = 0
    for at, rows in enumerate(tiles[0]):
        transform(0, at)
        for w in list(todo[1]):
            if at > 0 or w < waves // 2:
                cut(1, w)
                todo[1].remove(w)
        for w in list(todo[0]):
            if depth * (w + 1) <= made:
                cut(0, w)
                todo[0].remove(w)
        made = rows.stop
    for w in todo[0]:
        cut(0, w)
    for half in range(2):
        for w in range(waves):
            departure(half, w).wait()


def to_bands(plan, info, starts, bands, part, tables, depth, level_cols):
    latitudes = tables[0].shape[0]
    levels = part.shape[2]
    columns = 4 * levels
    fifth = latitudes // 5
    tile = [[0, 2 * fifth, 4 * fifth, latitudes], [0, fifth, 3 * fifth, latitudes]]
    smem, vmem = pl.BlockSpec(memory_space=pltpu.SMEM), pl.BlockSpec(memory_space=pltpu.VMEM)
    messages = bands.shape[0] * columns // level_cols
    grid = pltpu.VMEM((ceil_to(latitudes + depth, 8) + 8, columns), F32)
    held = 2 * (latitudes + columns) * sum(plan.widths) + 8 * (latitudes + depth) * columns
    held += 4 * messages * depth * ceil_to(level_cols, 128) + 2 * part.size
    limit = max(52 * 1024 * 1024, held + 4 * 1024 * 1024)
    return pl.pallas_call(
        functools.partial(grid_kernel, plan, levels, latitudes, depth, level_cols, tile),
        out_shape=jax.ShapeDtypeStruct((messages, 2, depth, level_cols), BF),
        in_specs=[smem, smem, smem, vmem] + [pl.BlockSpec(memory_space=pl.ANY)] * 2,
        out_specs=pl.BlockSpec(memory_space=pl.ANY),
        scratch_shapes=[
            pltpu.VMEM(tables[0].shape, BF),
            pltpu.VMEM(tables[1].shape, BF),
            pltpu.VMEM((plan.widths[0], columns), BF),
            pltpu.VMEM((plan.widths[1], columns), BF),
            grid,
            grid,
            pltpu.VMEM((messages, 2, depth, level_cols), BF),
            pltpu.SemaphoreType.DMA((2, 3)),
            pltpu.SemaphoreType.DMA((2, bands.shape[0])),
        ],
        compiler_params=pltpu.CompilerParams(vmem_limit_bytes=limit),
        cost_estimate=pl.CostEstimate(
            flops=2 * latitudes * sum(plan.widths) * columns,
            bytes_accessed=2 * latitudes * sum(plan.widths) + 4 * messages * depth * level_cols,
            transcendentals=0,
        ),
        name="grid_bands",
    )(info, starts, bands, part, *tables)


def per_device(control, covariance, legendre, pair_order, band_rows):
    axes = ("wave", "lev")
    waves, lev_count = lax.axis_size("wave"), lax.axis_size("lev")
    _, slots, columns = control.shape
    degrees, levels = slots - 1, columns // 4
    latitudes = legendre.shape[2]
    depth = 5 * latitudes // (4 * waves)
    level_cols = columns // lev_count
    plan = Plan(waves * lev_count, degrees)
    group, block = plan.group, plan.block
    me = lax.axis_index("wave") * lev_count + lax.axis_index("lev")
    is_high = (me >= group).astype(jnp.int32)
    lowest = pair_order[0]
    halves = [list(range(group)), list(range(group, 2 * group))]

    def exchange(rows):
        return lax.all_to_all(rows, axes, split_axis=0, concat_axis=0, tiled=True, axis_index_groups=halves)

    plane = group // 2
    whole = range(2 * group)
    far = [(d, (3 - d // plane) * plane + d % plane) for d in whole]
    near = [(d, d // plane * plane + plane - 1 - d % plane) for d in whole]
    far_blocks, near_blocks = [], []

    def swap_chunk(own):
        far_blocks.append(lax.ppermute(own, axes, far))
        near_blocks.append(lax.ppermute(own, axes, near))

    own = cast_blocks(plan, 0, covariance, is_high[None])
    own, control = lax.optimization_barrier((own, control))
    swap_chunk(own)

    def fold_block(rank):
        rank = jnp.where(is_high == 1, group - 1 - rank, rank)
        return rank // plane * plane + plane - 1 - rank % plane

    def slots_of(message, fold, folded, used):
        degree = fold_block(message) * block + fold
        upper = jnp.where(folded, degree - lowest, degrees - 1 - degree - lowest)
        upper = jnp.where(used & (upper >= 0), upper, -1)
        lower = jnp.where(used & folded & (degree <= lowest), degrees - degree, -1)
        return upper, lower

    upper, lower = slots_of(*plan.message_rows())
    sent = jnp.where(upper >= 0, upper, lower)
    packed = pack(plan, control[0], pair_order, sent[:, None])
    packed, legendre = lax.optimization_barrier((packed, legendre))
    received = exchange(packed)

    tables = make_tables(plan, legendre[0], slots_of(*plan.transform_rows()))
    for at in range(1, len(plan.chunks)):
        covariance, tables = lax.optimization_barrier((covariance, tables))
        swap_chunk(cast_blocks(plan, at, covariance, is_high[None]))

    info = jnp.stack([is_high, fold_block(me - group * is_high) * block])
    received, tables = lax.optimization_barrier((received, tables))
    before = ()
    for at, (near_block, far_block) in enumerate(zip(near_blocks, far_blocks)):
        result, *extras = filter_rows(plan, at, info, received, near_block, far_block, before)
        before = (*extras, result)
    filtered = exchange(result)

    extra_block = lowest // block
    extra_message = fold_block(extra_block)
    extra_row = plan.extra_row(extra_message, lowest - extra_block * block)
    where = jnp.stack([extra_message, extra_row])
    starts = jnp.cumsum(band_rows) - band_rows
    outgoing = to_bands(plan, where, starts, band_rows, filtered, tables, depth, level_cols)
    outgoing = outgoing.reshape(-1, depth, level_cols)
    return lax.all_to_all(outgoing, axes, split_axis=0, concat_axis=0, tiled=True)


def solution(mesh):
    return jax.shard_map(
        per_device,
        mesh=mesh,
        in_specs=(
            P(("wave", "lev"), None, None),
            P(("wave", "lev"), None, None),
            P(("wave", "lev"), None, None),
            P(("wave", "lev")),
            P(),
        ),
        out_specs=P(None, "wave", "lev"),
        check_vma=False,
    )
```

```python
import functools

import jax
import jax.numpy as jnp
import numpy as np
from jax import lax
from jax.experimental import pallas as pl
from jax.experimental.pallas import tpu as pltpu
from jax.sharding import PartitionSpec as P

BF = jnp.bfloat16
F32 = jnp.float32
SUB = 16
DIGIT = 16


def ceil_to(value, step):
    return (value + step - 1) // step * step


class Plan:
    def __init__(self, devices, degrees):
        self.devices = devices
        self.group = devices // 2
        self.degrees = degrees
        self.block = degrees // devices
        self.chunks = []
        row, fold = 0, 0
        for count in self.fold_counts(self.block):
            self.chunks.append((row, fold, count))
            row += ceil_to(2 * count, SUB)
            fold += count
        self.rows = row
        whole = [(at, n) for at, (_, _, n) in enumerate(self.chunks) if n % SUB == 0]
        mixed = [(at, n) for at, (_, _, n) in enumerate(self.chunks) if n % SUB]
        lower = [(at, 0, n) for at, n in whole] + [(at, 0, ceil_to(2 * n, SUB)) for at, n in mixed]
        self.segments = lower + [(at, n, n) for at, n in whole]
        self.widths = [
            self.group * sum(n for _, _, n in self.segments),
            self.group * sum(n for _, _, n in lower),
        ]

    @staticmethod
    def fold_counts(block):
        return (block - 8, 8) if block % SUB == 8 and block > 8 else (block,)

    def chunk_rows(self, at):
        _, first, count = self.chunks[at]
        height = ceil_to(2 * count, SUB)
        fold = np.zeros(height, np.int32)
        fold[:2 * count] = first + np.tile(np.arange(count), 2)
        row = np.arange(height)
        return fold, row < count, row < 2 * count

    def message_rows(self):
        tables = [self.chunk_rows(at) for at in range(len(self.chunks))]
        one = [np.concatenate(column) for column in zip(*tables)]
        return [np.repeat(np.arange(self.group, dtype=np.int32), self.rows)] + [
            np.tile(column, self.group) for column in one
        ]

    def transform_rows(self):
        parts = []
        for at, first, count in self.segments:
            columns = [column[first:first + count] for column in self.chunk_rows(at)]
            parts.append(
                [np.repeat(np.arange(self.group, dtype=np.int32), count)]
                + [np.tile(column, self.group) for column in columns]
            )
        return [np.concatenate(column) for column in zip(*parts)]

    def extra_row(self, message, fold):
        base, result = 0, jnp.int32(0)
        for at, first, count in self.segments:
            if first == 0:
                start = self.chunks[at][1]
                here = (fold >= start) & (fold < start + self.chunks[at][2])
                result = jnp.where(here, base + message * count + fold - start, result)
            base += self.group * count
        return result


def cast_kernel(plan, chunk, steps, info_ref, blocks_ref, out_ref, held_ref, cast_ref, in_sems, out_sems):
    _, fold, count = chunk
    start = jnp.where(info_ref[0] == 1, plan.block - fold - count, fold)
    each = count // steps
    arrivals, departures = [], []
    for at in range(steps):
        here = pl.ds(at * each, each)
        arrivals.append(
            pltpu.make_async_copy(blocks_ref.at[pl.ds(start + at * each, each)], held_ref.at[here], in_sems.at[at])
        )
        arrivals[at].start()
        departures.append(pltpu.make_async_copy(cast_ref.at[here], out_ref.at[here], out_sems.at[at]))
    for at in range(steps):
        arrivals[at].wait()
        cast_ref[at * each:(at + 1) * each] = held_ref[at * each:(at + 1) * each].astype(BF)
        departures[at].start()
    for departure in departures:
        departure.wait()


def cast_blocks(plan, at, blocks, info):
    count = plan.chunks[at][2]
    steps = 4 if count % 32 == 0 else 1
    shape = (count, *blocks.shape[1:])
    anywhere = pl.BlockSpec(memory_space=pl.ANY)
    return pl.pallas_call(
        functools.partial(cast_kernel, plan, plan.chunks[at], steps),
        out_shape=jax.ShapeDtypeStruct(shape, BF),
        in_specs=[pl.BlockSpec(memory_space=pltpu.SMEM), anywhere],
        out_specs=anywhere,
        scratch_shapes=[
            pltpu.VMEM(shape, F32),
            pltpu.VMEM(shape, BF),
            pltpu.SemaphoreType.DMA((steps,)),
            pltpu.SemaphoreType.DMA((steps,)),
        ],
        compiler_params=pltpu.CompilerParams(vmem_limit_bytes=56 * 1024 * 1024),
        cost_estimate=pl.CostEstimate(flops=1, bytes_accessed=6 * count, transcendentals=0),
        name="cast_blocks",
    )(info, blocks)


def pack_kernel(plan, levels, info_ref, slot_ref, control_ref, out_ref):
    slots = control_ref.shape[0]
    messages = out_ref.shape[0]
    even = slots - 1
    rows = messages * plan.rows
    slot = slot_ref[...]
    pick = (slot == lax.broadcasted_iota(jnp.int32, (rows, even), 1)).astype(F32).astype(BF)
    got = jnp.dot(pick, control_ref[:even, :], preferred_element_type=F32)
    last = control_ref[even:slots, :].astype(F32)
    got = jnp.where(slot == even, last, got).astype(BF)
    extra_slot = plan.degrees - info_ref[0]
    lane = lax.broadcasted_iota(jnp.int32, (SUB, even), 1)
    first = lax.broadcasted_iota(jnp.int32, (SUB, even), 0) == 0
    choose = jnp.where(first & (lane == extra_slot), 1.0, 0.0).astype(BF)
    extra = jnp.dot(choose, control_ref[:even, :], preferred_element_type=F32)
    extra = jnp.where(extra_slot == even, last, extra)
    place = lax.broadcasted_iota(jnp.int32, (SUB, levels), 0)
    tail = jnp.zeros((SUB, levels), F32)
    for c in range(4):
        tail = jnp.where(place == c, extra[0:1, c * levels:(c + 1) * levels], tail)
    high_digit = (info_ref[0] // DIGIT).astype(F32)
    low_digit = (info_ref[0] % DIGIT).astype(F32)
    tail = jnp.where(place == 4, high_digit, jnp.where(place == 5, low_digit, tail)).astype(BF)
    for k in range(messages):
        for c in range(4):
            out_ref[k, c * plan.rows:(c + 1) * plan.rows, :] = got[
                k * plan.rows:(k + 1) * plan.rows, c * levels:(c + 1) * levels
            ]
        out_ref[k, 4 * plan.rows:, :] = tail


def pack(plan, control, lowest, slots_of_rows):
    slots, columns = control.shape
    levels = columns // 4
    height = 4 * plan.rows + SUB
    per_step = max(1, min(plan.group, 320 // plan.rows))
    return pl.pallas_call(
        functools.partial(pack_kernel, plan, levels),
        grid=(plan.group // per_step,),
        out_shape=jax.ShapeDtypeStruct((plan.group, height, levels), BF),
        in_specs=[
            pl.BlockSpec(memory_space=pltpu.SMEM),
            pl.BlockSpec((per_step * plan.rows, 1), lambda k: (k, 0)),
            pl.BlockSpec((slots, columns), lambda k: (0, 0)),
        ],
        out_specs=pl.BlockSpec((per_step, height, levels), lambda k: (k, 0, 0)),
        compiler_params=pltpu.CompilerParams(vmem_limit_bytes=16 * 1024 * 1024),
        cost_estimate=pl.CostEstimate(flops=1, bytes_accessed=1, transcendentals=0),
        name="pack_rows",
    )(lowest, slots_of_rows, control)


def table_kernel(plan, upper_ref, lower_ref, legendre_ref, *refs):
    outs, picks = refs[:2], refs[2:]
    slots = legendre_ref.shape[0]
    even = slots - 1

    @pl.when(pl.program_id(0) == 0)
    def _():
        for index_ref, pick_ref in zip((upper_ref, lower_ref), picks):
            slot = lax.broadcasted_iota(jnp.int32, pick_ref.shape, 0)
            pick_ref[...] = jnp.where(slot == index_ref[...], 1.0, 0.0).astype(BF)

    def times(rows, picked):
        return lax.dot_general(rows, picked, (((0,), (0,)), ((), ())), preferred_element_type=F32)

    for out_ref, pick_ref in zip(outs, picks):
        got = times(legendre_ref[:even, :], pick_ref[:even, :])
        last = jnp.concatenate(
            [legendre_ref[even:slots, :].astype(F32), jnp.zeros((SUB - 1, legendre_ref.shape[1]), F32)], axis=0
        ).astype(BF)
        out_ref[...] = (got + times(last, pick_ref[even:even + SUB, :])).astype(BF)


def make_tables(plan, legendre, slots_of_rows):
    slots, latitudes = legendre.shape
    tile = 256
    index = [rows[None, :width] for rows, width in zip(slots_of_rows, plan.widths)]
    return pl.pallas_call(
        functools.partial(table_kernel, plan),
        grid=(latitudes // tile,),
        out_shape=[jax.ShapeDtypeStruct((latitudes, width), BF) for width in plan.widths],
        in_specs=[pl.BlockSpec((1, width), lambda t: (0, 0)) for width in plan.widths]
        + [pl.BlockSpec((slots, tile), lambda t: (0, t))],
        out_specs=[pl.BlockSpec((tile, width), lambda t: (t, 0)) for width in plan.widths],
        scratch_shapes=[pltpu.VMEM((slots - 1 + SUB, width), BF) for width in plan.widths],
        compiler_params=pltpu.CompilerParams(vmem_limit_bytes=20 * 1024 * 1024),
        cost_estimate=pl.CostEstimate(
            flops=20 * latitudes * slots * sum(plan.widths), bytes_accessed=2 * legendre.size, transcendentals=0
        ),
        name="make_tables",
    )(*index, legendre)


def swap_matrix():
    i = lax.broadcasted_iota(jnp.int32, (SUB * SUB, SUB * SUB), 0)
    j = lax.broadcasted_iota(jnp.int32, (SUB * SUB, SUB * SUB), 1)
    return jnp.where((i // SUB == j % SUB) & (i % SUB == j // SUB), 1.0, 0.0).astype(BF)


def filter_kernel(plan, at, levels, info_ref, rows_ref, near_ref, far_ref, *refs):
    first, last = at == 0, at == len(plan.chunks) - 1
    before_ref = None if first else refs[0]
    out_ref, *after, held_ref, x_ref, y_ref, z_ref, in_sems, out_sems = refs[0 if first else 2:]
    row0, fold0, count = plan.chunks[at]
    height = ceil_to(2 * count, SUB)
    groups = plan.group // SUB
    first_fold = (info_ref[1] + fold0).astype(F32)
    swap = swap_matrix()

    near = pltpu.make_async_copy(near_ref, held_ref.at[info_ref[0]], in_sems.at[0])
    far = pltpu.make_async_copy(far_ref, held_ref.at[1 - info_ref[0]], in_sems.at[1])
    near.start()
    far.start()

    def turn(rows):
        return jnp.dot(swap, rows, preferred_element_type=F32)

    held = height * SUB
    tails = []
    for g in range(groups):
        sources = slice(g * SUB, (g + 1) * SUB)
        for r in range(0, height, SUB):
            parts = []
            for c in range(4):
                start = c * plan.rows + row0 + r
                parts.append(rows_ref[sources, start:start + SUB, :].reshape(SUB * SUB, levels))
            x_ref[g * held + r * SUB:g * held + (r + SUB) * SUB, :] = turn(jnp.concatenate(parts, axis=1)).astype(BF)
        tail = turn(rows_ref[sources, 4 * plan.rows:4 * plan.rows + SUB, :].reshape(SUB * SUB, levels))
        low = tail[4 * SUB:5 * SUB] * DIGIT + tail[5 * SUB:6 * SUB]
        if first:
            kept = jnp.zeros((4 * SUB, levels), F32)
        else:
            kept = before_ref[4 * SUB * g:4 * SUB * (g + 1), :]
        tails.append((tail[:4 * SUB].astype(BF), jnp.concatenate([low] * 4, axis=0), kept))
    near.wait()
    far.wait()

    for g in range(groups):
        sources = slice(g * SUB, (g + 1) * SUB)
        extra, low, kept = tails[g]
        for i in range(count):
            def stack(row):
                start = g * held + row * SUB
                return [x_ref[start:start + SUB, c * levels:(c + 1) * levels] for c in range(4)]

            rows = jnp.concatenate([*stack(i), *stack(count + i), extra], axis=0)
            matrices = jnp.concatenate([held_ref[0, i], held_ref[1, count - 1 - i]], axis=0)
            both = lax.dot_general(rows, matrices, (((1,), (1,)), ((), ())), preferred_element_type=F32)
            from_low, from_high = both[:4 * SUB, :levels], both[:, levels:]
            fold = first_fold + i
            mixed = jnp.where(low <= fold, from_low, from_high[:4 * SUB])
            kept = jnp.where(low == fold, from_high[8 * SUB:], kept)
            for row, value in ((i, mixed), (count + i, from_high[4 * SUB:8 * SUB])):
                value = value.astype(BF)
                for c in range(4):
                    y_ref[row * SUB:(row + 1) * SUB, c * levels:(c + 1) * levels] = value[c * SUB:(c + 1) * SUB]
        if height > 2 * count:
            y_ref[2 * count * SUB:height * SUB, :] = jnp.zeros(((height - 2 * count) * SUB, 4 * levels), BF)
        for r in range(0, height, SUB):
            back = turn(y_ref[r * SUB:(r + SUB) * SUB, :]).astype(BF)
            for c in range(4):
                z_ref[sources, c * height + r:c * height + r + SUB, :] = back[:, c * levels:(c + 1) * levels].reshape(
                    SUB, SUB, levels
                )
        if last:
            filled = jnp.concatenate([kept, jnp.zeros((12 * SUB, levels), F32)], axis=0).astype(BF)
            z_ref[sources, 4 * height:4 * height + SUB, :] = turn(filled).astype(BF).reshape(SUB, SUB, levels)
        else:
            after[0][4 * SUB * g:4 * SUB * (g + 1), :] = kept

    moves = [(c * height, c * plan.rows + row0, height) for c in range(4)]
    if last:
        moves.append((4 * height, 4 * plan.rows, SUB))
    departures = [
        pltpu.make_async_copy(z_ref.at[:, pl.ds(here, n), :], out_ref.at[:, pl.ds(there, n), :], out_sems.at[c])
        for c, (here, there, n) in enumerate(moves)
    ]
    for departure in departures:
        departure.start()
    for departure in departures:
        departure.wait()


def filter_rows(plan, at, info, received, near, far, before):
    levels = received.shape[2]
    count = plan.chunks[at][2]
    height = ceil_to(2 * count, SUB)
    last = at == len(plan.chunks) - 1
    smem, vmem = pl.BlockSpec(memory_space=pltpu.SMEM), pl.BlockSpec(memory_space=pltpu.VMEM)
    anywhere = pl.BlockSpec(memory_space=pl.ANY)
    out_shape = [jax.ShapeDtypeStruct(received.shape, BF)]
    if not last:
        out_shape.append(jax.ShapeDtypeStruct((4 * plan.group, levels), F32))
    return pl.pallas_call(
        functools.partial(filter_kernel, plan, at, levels),
        out_shape=out_shape,
        in_specs=[smem, vmem, anywhere, anywhere] + ([vmem, anywhere] if before else []),
        out_specs=[anywhere] + [vmem] * (len(out_shape) - 1),
        input_output_aliases={5: 0} if before else {},
        scratch_shapes=[
            pltpu.VMEM((2, count, levels, levels), BF),
            pltpu.VMEM((plan.group * height, 4 * levels), BF),
            pltpu.VMEM((height * SUB, 4 * levels), BF),
            pltpu.VMEM((plan.group, 4 * height + SUB, levels), BF),
            pltpu.SemaphoreType.DMA((2,)),
            pltpu.SemaphoreType.DMA((5,)),
        ],
        compiler_params=pltpu.CompilerParams(vmem_limit_bytes=20 * 1024 * 1024),
        cost_estimate=pl.CostEstimate(
            flops=2 * plan.group * 16 * count * levels * levels * 4,
            bytes_accessed=2 * 2 * received.size + 4 * count * levels * levels,
            transcendentals=0,
        ),
        name="filter_rows",
    )(info, received, near, far, *before)


def grid_kernel(plan, levels, latitudes, depth, level_cols, tile, info_ref, starts_ref, bands_ref, part_ref, *refs):
    tables, out_ref, held_tables = refs[:2], refs[2], refs[3:5]
    upper_ref, lower_ref, *grids, cut_ref, sems, out_sems = refs[5:]
    waves = bands_ref.shape[0]
    groups = 4 * levels // level_cols
    tiles = [[slice(start, stop) for start, stop in zip(edges, edges[1:])] for edges in tile]

    def copy(half, at):
        rows = tiles[half][at]
        return pltpu.make_async_copy(tables[half].at[rows], held_tables[half].at[rows], sems.at[half, at])

    for half in (1, 0):
        for at in range(len(tiles[half])):
            copy(half, at).start()

    base = 0
    for at, first, rows in plan.segments:
        for k in range(plan.group):
            for c in range(4):
                start = c * plan.rows + plan.chunks[at][0] + first
                cols = slice(c * levels, (c + 1) * levels)
                value = part_ref[k, start:start + rows, :]
                upper_ref[base + k * rows:base + (k + 1) * rows, cols] = value
                if base < plan.widths[1]:
                    lower_ref[base + k * rows:base + (k + 1) * rows, cols] = value
        base += plan.group * rows

    extra = part_ref[info_ref[0], 4 * plan.rows:4 * plan.rows + SUB, :]
    base = info_ref[1] // SUB * SUB
    place = pl.ds(pl.multiple_of(base, SUB), SUB)
    here = lax.broadcasted_iota(jnp.int32, (SUB, levels), 0) == info_ref[1] - base
    for c in range(4):
        cols = slice(c * levels, (c + 1) * levels)
        held = upper_ref[place, cols].astype(F32)
        lower_ref[place, cols] = jnp.where(here, extra[c:c + 1, :].astype(F32), held).astype(BF)

    def transform(half, at):
        copy(half, at).wait()
        rows = tiles[half][at]
        grids[half][rows, :] = jnp.dot(
            held_tables[half][rows, :], (upper_ref, lower_ref)[half][...], preferred_element_type=F32
        )

    def departure(half, w):
        messages = pl.ds(w * groups, groups)
        return pltpu.make_async_copy(cut_ref.at[messages, half], out_ref.at[messages, half], out_sems.at[half, w])

    def cut(half, w):
        place = lax.broadcasted_iota(jnp.int32, (8, 4 * levels), 0)
        start = starts_ref[w]
        base = start // 8 * 8
        offset = start - base

        def slab(at):
            held = grids[half][pl.ds(pl.multiple_of(base + at, 8), 8), :]
            return pltpu.roll(held, (8 - offset) % 8, axis=0)

        after = slab(0)
        done = []
        for r in range(0, depth, 8):
            now, after = after, slab(r + 8)
            got = jnp.where(place < 8 - offset, now, after)
            done.append(jnp.where(place < bands_ref[w] - r, got, 0.0))
            if len(done) == 2 or r + 8 == depth:
                rows = jnp.concatenate(done, axis=0).astype(BF)
                first = r + 8 - rows.shape[0]
                for g in range(groups):
                    cut_ref[w * groups + g, half, first:r + 8, :] = rows[:, g * level_cols:(g + 1) * level_cols]
                done = []
        departure(half, w).start()

    for at in range(len(tiles[1])):
        transform(1, at)
    todo = [[w for w in range(waves)] for _ in range(2)]
    made = 0
    for at, rows in enumerate(tiles[0]):
        transform(0, at)
        for w in list(todo[1]):
            if at > 0 or w < waves // 2:
                cut(1, w)
                todo[1].remove(w)
        for w in list(todo[0]):
            if depth * (w + 1) <= made:
                cut(0, w)
                todo[0].remove(w)
        made = rows.stop
    for w in todo[0]:
        cut(0, w)
    for half in range(2):
        for w in range(waves):
            departure(half, w).wait()


def to_bands(plan, info, starts, bands, part, tables, depth, level_cols):
    latitudes = tables[0].shape[0]
    levels = part.shape[2]
    columns = 4 * levels
    fifth = latitudes // 5
    tile = [[0, latitudes // 2, latitudes], [0, fifth, latitudes]]
    smem, vmem = pl.BlockSpec(memory_space=pltpu.SMEM), pl.BlockSpec(memory_space=pltpu.VMEM)
    messages = bands.shape[0] * columns // level_cols
    grid = pltpu.VMEM((ceil_to(latitudes + depth, 8) + 8, columns), F32)
    held = 2 * (latitudes + columns) * sum(plan.widths) + 8 * (latitudes + depth) * columns
    held += 4 * messages * depth * ceil_to(level_cols, 128) + 2 * part.size
    limit = max(52 * 1024 * 1024, min(held + 8 * 1024 * 1024, 60 * 1024 * 1024))
    return pl.pallas_call(
        functools.partial(grid_kernel, plan, levels, latitudes, depth, level_cols, tile),
        out_shape=jax.ShapeDtypeStruct((messages, 2, depth, level_cols), BF),
        in_specs=[smem, smem, smem, vmem] + [pl.BlockSpec(memory_space=pl.ANY)] * 2,
        out_specs=pl.BlockSpec(memory_space=pl.ANY),
        scratch_shapes=[
            pltpu.VMEM(tables[0].shape, BF),
            pltpu.VMEM(tables[1].shape, BF),
            pltpu.VMEM((plan.widths[0], columns), BF),
            pltpu.VMEM((plan.widths[1], columns), BF),
            grid,
            grid,
            pltpu.VMEM((messages, 2, depth, level_cols), BF),
            pltpu.SemaphoreType.DMA((2, 2)),
            pltpu.SemaphoreType.DMA((2, bands.shape[0])),
        ],
        compiler_params=pltpu.CompilerParams(vmem_limit_bytes=limit),
        cost_estimate=pl.CostEstimate(
            flops=2 * latitudes * sum(plan.widths) * columns,
            bytes_accessed=2 * latitudes * sum(plan.widths) + 4 * messages * depth * level_cols,
            transcendentals=0,
        ),
        name="grid_bands",
    )(info, starts, bands, part, *tables)


def per_device(control, covariance, legendre, pair_order, band_rows):
    axes = ("wave", "lev")
    waves, lev_count = lax.axis_size("wave"), lax.axis_size("lev")
    _, slots, columns = control.shape
    degrees, levels = slots - 1, columns // 4
    latitudes = legendre.shape[2]
    depth = 5 * latitudes // (4 * waves)
    level_cols = columns // lev_count
    plan = Plan(waves * lev_count, degrees)
    group, block = plan.group, plan.block
    me = lax.axis_index("wave") * lev_count + lax.axis_index("lev")
    is_high = (me >= group).astype(jnp.int32)
    lowest = pair_order[0]
    halves = [list(range(group)), list(range(group, 2 * group))]

    def exchange(rows):
        return lax.all_to_all(rows, axes, split_axis=0, concat_axis=0, tiled=True, axis_index_groups=halves)

    plane = group // 2
    whole = range(2 * group)
    far = [(d, (3 - d // plane) * plane + d % plane) for d in whole]
    near = [(d, d // plane * plane + plane - 1 - d % plane) for d in whole]
    far_blocks, near_blocks = [], []

    def swap_chunk(own):
        far_blocks.append(lax.ppermute(own, axes, far))
        near_blocks.append(lax.ppermute(own, axes, near))

    own = cast_blocks(plan, 0, covariance, is_high[None])
    own, control = lax.optimization_barrier((own, control))
    swap_chunk(own)

    def fold_block(rank):
        rank = jnp.where(is_high == 1, group - 1 - rank, rank)
        return rank // plane * plane + plane - 1 - rank % plane

    def slots_of(message, fold, folded, used):
        degree = fold_block(message) * block + fold
        upper = jnp.where(folded, degree - lowest, degrees - 1 - degree - lowest)
        upper = jnp.where(used & (upper >= 0), upper, -1)
        lower = jnp.where(used & folded & (degree <= lowest), degrees - degree, -1)
        return upper, lower

    upper, lower = slots_of(*plan.message_rows())
    sent = jnp.where(upper >= 0, upper, lower)
    packed = pack(plan, control[0], pair_order, sent[:, None])
    packed, legendre = lax.optimization_barrier((packed, legendre))
    received = exchange(packed)

    tables = make_tables(plan, legendre[0], slots_of(*plan.transform_rows()))
    for at in range(1, len(plan.chunks)):
        covariance, tables = lax.optimization_barrier((covariance, tables))
        swap_chunk(cast_blocks(plan, at, covariance, is_high[None]))

    info = jnp.stack([is_high, fold_block(me - group * is_high) * block])
    received, tables = lax.optimization_barrier((received, tables))
    before = ()
    for at, (near_block, far_block) in enumerate(zip(near_blocks, far_blocks)):
        result, *extras = filter_rows(plan, at, info, received, near_block, far_block, before)
        before = (*extras, result)
    filtered = exchange(result)

    extra_block = lowest // block
    extra_message = fold_block(extra_block)
    extra_row = plan.extra_row(extra_message, lowest - extra_block * block)
    where = jnp.stack([extra_message, extra_row])
    starts = jnp.cumsum(band_rows) - band_rows
    outgoing = to_bands(plan, where, starts, band_rows, filtered, tables, depth, level_cols)
    outgoing = outgoing.reshape(-1, depth, level_cols)
    return lax.all_to_all(outgoing, axes, split_axis=0, concat_axis=0, tiled=True)


def solution(mesh):
    return jax.shard_map(
        per_device,
        mesh=mesh,
        in_specs=(
            P(("wave", "lev"), None, None),
            P(("wave", "lev"), None, None),
            P(("wave", "lev"), None, None),
            P(("wave", "lev")),
            P(),
        ),
        out_specs=P(None, "wave", "lev"),
        check_vma=False,
    )
```

```python
import functools

import jax
import jax.numpy as jnp
import numpy as np
from jax import lax
from jax.experimental import pallas as pl
from jax.experimental.pallas import tpu as pltpu
from jax.sharding import PartitionSpec as P

BF = jnp.bfloat16
F32 = jnp.float32
SUB = 16
DIGIT = 16


def ceil_to(value, step):
    return (value + step - 1) // step * step


class Plan:
    def __init__(self, devices, degrees):
        self.devices = devices
        self.group = devices // 2
        self.degrees = degrees
        self.block = degrees // devices
        self.chunks = []
        row, fold = 0, 0
        for count in self.fold_counts(self.block):
            self.chunks.append((row, fold, count))
            row += ceil_to(2 * count, SUB)
            fold += count
        self.rows = row
        whole = [(at, n) for at, (_, _, n) in enumerate(self.chunks) if n % SUB == 0]
        mixed = [(at, n) for at, (_, _, n) in enumerate(self.chunks) if n % SUB]
        lower = [(at, 0, n) for at, n in whole] + [(at, 0, ceil_to(2 * n, SUB)) for at, n in mixed]
        self.segments = lower + [(at, n, n) for at, n in whole]
        self.widths = [
            self.group * sum(n for _, _, n in self.segments),
            self.group * sum(n for _, _, n in lower),
        ]

    @staticmethod
    def fold_counts(block):
        return (block - 8, 8) if block % SUB == 8 and block > 8 else (block,)

    def chunk_rows(self, at):
        _, first, count = self.chunks[at]
        height = ceil_to(2 * count, SUB)
        fold = np.zeros(height, np.int32)
        fold[:2 * count] = first + np.tile(np.arange(count), 2)
        row = np.arange(height)
        return fold, row < count, row < 2 * count

    def message_rows(self):
        tables = [self.chunk_rows(at) for at in range(len(self.chunks))]
        one = [np.concatenate(column) for column in zip(*tables)]
        return [np.repeat(np.arange(self.group, dtype=np.int32), self.rows)] + [
            np.tile(column, self.group) for column in one
        ]

    def transform_rows(self):
        parts = []
        for at, first, count in self.segments:
            columns = [column[first:first + count] for column in self.chunk_rows(at)]
            parts.append(
                [np.repeat(np.arange(self.group, dtype=np.int32), count)]
                + [np.tile(column, self.group) for column in columns]
            )
        return [np.concatenate(column) for column in zip(*parts)]

    def extra_row(self, message, fold):
        base, result = 0, jnp.int32(0)
        for at, first, count in self.segments:
            if first == 0:
                start = self.chunks[at][1]
                here = (fold >= start) & (fold < start + self.chunks[at][2])
                result = jnp.where(here, base + message * count + fold - start, result)
            base += self.group * count
        return result


def cast_kernel(plan, chunk, steps, info_ref, blocks_ref, out_ref, held_ref, cast_ref, in_sems, out_sems):
    _, fold, count = chunk
    start = jnp.where(info_ref[0] == 1, plan.block - fold - count, fold)
    each = count // steps
    arrivals, departures = [], []
    for at in range(steps):
        here = pl.ds(at * each, each)
        arrivals.append(
            pltpu.make_async_copy(blocks_ref.at[pl.ds(start + at * each, each)], held_ref.at[here], in_sems.at[at])
        )
        arrivals[at].start()
        departures.append(pltpu.make_async_copy(cast_ref.at[here], out_ref.at[here], out_sems.at[at]))
    for at in range(steps):
        arrivals[at].wait()
        cast_ref[at * each:(at + 1) * each] = held_ref[at * each:(at + 1) * each].astype(BF)
        departures[at].start()
    for departure in departures:
        departure.wait()


def cast_blocks(plan, at, blocks, info):
    count = plan.chunks[at][2]
    steps = 4 if count % 32 == 0 else 1
    shape = (count, *blocks.shape[1:])
    anywhere = pl.BlockSpec(memory_space=pl.ANY)
    return pl.pallas_call(
        functools.partial(cast_kernel, plan, plan.chunks[at], steps),
        out_shape=jax.ShapeDtypeStruct(shape, BF),
        in_specs=[pl.BlockSpec(memory_space=pltpu.SMEM), anywhere],
        out_specs=anywhere,
        scratch_shapes=[
            pltpu.VMEM(shape, F32),
            pltpu.VMEM(shape, BF),
            pltpu.SemaphoreType.DMA((steps,)),
            pltpu.SemaphoreType.DMA((steps,)),
        ],
        compiler_params=pltpu.CompilerParams(vmem_limit_bytes=56 * 1024 * 1024),
        cost_estimate=pl.CostEstimate(flops=1, bytes_accessed=6 * count, transcendentals=0),
        name="cast_blocks",
    )(info, blocks)


def pack_kernel(plan, levels, info_ref, slot_ref, control_ref, out_ref):
    slots = control_ref.shape[0]
    messages = out_ref.shape[0]
    even = slots - 1
    rows = messages * plan.rows
    slot = slot_ref[...]
    pick = (slot == lax.broadcasted_iota(jnp.int32, (rows, even), 1)).astype(F32).astype(BF)
    got = jnp.dot(pick, control_ref[:even, :], preferred_element_type=F32)
    last = control_ref[even:slots, :].astype(F32)
    got = jnp.where(slot == even, last, got).astype(BF)
    extra_slot = plan.degrees - info_ref[0]
    lane = lax.broadcasted_iota(jnp.int32, (SUB, even), 1)
    first = lax.broadcasted_iota(jnp.int32, (SUB, even), 0) == 0
    choose = jnp.where(first & (lane == extra_slot), 1.0, 0.0).astype(BF)
    extra = jnp.dot(choose, control_ref[:even, :], preferred_element_type=F32)
    extra = jnp.where(extra_slot == even, last, extra)
    place = lax.broadcasted_iota(jnp.int32, (SUB, levels), 0)
    tail = jnp.zeros((SUB, levels), F32)
    for c in range(4):
        tail = jnp.where(place == c, extra[0:1, c * levels:(c + 1) * levels], tail)
    high_digit = (info_ref[0] // DIGIT).astype(F32)
    low_digit = (info_ref[0] % DIGIT).astype(F32)
    tail = jnp.where(place == 4, high_digit, jnp.where(place == 5, low_digit, tail)).astype(BF)
    for k in range(messages):
        for c in range(4):
            out_ref[k, c * plan.rows:(c + 1) * plan.rows, :] = got[
                k * plan.rows:(k + 1) * plan.rows, c * levels:(c + 1) * levels
            ]
        out_ref[k, 4 * plan.rows:, :] = tail


def pack(plan, control, lowest, slots_of_rows):
    slots, columns = control.shape
    levels = columns // 4
    height = 4 * plan.rows + SUB
    per_step = max(1, min(plan.group, 320 // plan.rows))
    return pl.pallas_call(
        functools.partial(pack_kernel, plan, levels),
        grid=(plan.group // per_step,),
        out_shape=jax.ShapeDtypeStruct((plan.group, height, levels), BF),
        in_specs=[
            pl.BlockSpec(memory_space=pltpu.SMEM),
            pl.BlockSpec((per_step * plan.rows, 1), lambda k: (k, 0)),
            pl.BlockSpec((slots, columns), lambda k: (0, 0)),
        ],
        out_specs=pl.BlockSpec((per_step, height, levels), lambda k: (k, 0, 0)),
        compiler_params=pltpu.CompilerParams(vmem_limit_bytes=16 * 1024 * 1024),
        cost_estimate=pl.CostEstimate(flops=1, bytes_accessed=1, transcendentals=0),
        name="pack_rows",
    )(lowest, slots_of_rows, control)


def table_kernel(plan, upper_ref, lower_ref, legendre_ref, *refs):
    outs, picks = refs[:2], refs[2:]
    slots = legendre_ref.shape[0]
    even = slots - 1

    @pl.when(pl.program_id(0) == 0)
    def _():
        for index_ref, pick_ref in zip((upper_ref, lower_ref), picks):
            slot = lax.broadcasted_iota(jnp.int32, pick_ref.shape, 0)
            pick_ref[...] = jnp.where(slot == index_ref[...], 1.0, 0.0).astype(BF)

    def times(rows, picked):
        return lax.dot_general(rows, picked, (((0,), (0,)), ((), ())), preferred_element_type=F32)

    for out_ref, pick_ref in zip(outs, picks):
        got = times(legendre_ref[:even, :], pick_ref[:even, :])
        last = jnp.concatenate(
            [legendre_ref[even:slots, :].astype(F32), jnp.zeros((SUB - 1, legendre_ref.shape[1]), F32)], axis=0
        ).astype(BF)
        out_ref[...] = (got + times(last, pick_ref[even:even + SUB, :])).astype(BF)


def make_tables(plan, legendre, slots_of_rows):
    slots, latitudes = legendre.shape
    tile = 256
    index = [rows[None, :width] for rows, width in zip(slots_of_rows, plan.widths)]
    return pl.pallas_call(
        functools.partial(table_kernel, plan),
        grid=(latitudes // tile,),
        out_shape=[jax.ShapeDtypeStruct((latitudes, width), BF) for width in plan.widths],
        in_specs=[pl.BlockSpec((1, width), lambda t: (0, 0)) for width in plan.widths]
        + [pl.BlockSpec((slots, tile), lambda t: (0, t))],
        out_specs=[pl.BlockSpec((tile, width), lambda t: (t, 0)) for width in plan.widths],
        scratch_shapes=[pltpu.VMEM((slots - 1 + SUB, width), BF) for width in plan.widths],
        compiler_params=pltpu.CompilerParams(vmem_limit_bytes=20 * 1024 * 1024),
        cost_estimate=pl.CostEstimate(
            flops=20 * latitudes * slots * sum(plan.widths), bytes_accessed=2 * legendre.size, transcendentals=0
        ),
        name="make_tables",
    )(*index, legendre)


def swap_matrix():
    i = lax.broadcasted_iota(jnp.int32, (SUB * SUB, SUB * SUB), 0)
    j = lax.broadcasted_iota(jnp.int32, (SUB * SUB, SUB * SUB), 1)
    return jnp.where((i // SUB == j % SUB) & (i % SUB == j // SUB), 1.0, 0.0).astype(BF)


def filter_kernel(plan, at, levels, info_ref, rows_ref, near_ref, far_ref, *refs):
    first, last = at == 0, at == len(plan.chunks) - 1
    before_ref = None if first else refs[0]
    out_ref, *after, held_ref, x_ref, y_ref, z_ref, in_sems, out_sems = refs[0 if first else 2:]
    row0, fold0, count = plan.chunks[at]
    height = ceil_to(2 * count, SUB)
    groups = plan.group // SUB
    first_fold = (info_ref[1] + fold0).astype(F32)
    swap = swap_matrix()

    arrivals = []
    if first:
        for side, (ref, place) in enumerate(((near_ref, info_ref[0]), (far_ref, 1 - info_ref[0]))):
            arrivals.append(pltpu.make_async_copy(ref, held_ref.at[place], in_sems.at[side]))
            arrivals[side].start()

    def matrices(i):
        at = count - 1 - i
        if first:
            return [held_ref[0, i], held_ref[1, at]]
        is_high = info_ref[0] == 1
        return [jnp.where(is_high, far_ref[i], near_ref[i]), jnp.where(is_high, near_ref[at], far_ref[at])]

    def turn(rows):
        return jnp.dot(swap, rows, preferred_element_type=F32)

    held = height * SUB
    tails = []
    for g in range(groups):
        sources = slice(g * SUB, (g + 1) * SUB)
        for r in range(0, height, SUB):
            parts = []
            for c in range(4):
                start = c * plan.rows + row0 + r
                parts.append(rows_ref[sources, start:start + SUB, :].reshape(SUB * SUB, levels))
            x_ref[g * held + r * SUB:g * held + (r + SUB) * SUB, :] = turn(jnp.concatenate(parts, axis=1)).astype(BF)
        tail = turn(rows_ref[sources, 4 * plan.rows:4 * plan.rows + SUB, :].reshape(SUB * SUB, levels))
        low = tail[4 * SUB:5 * SUB] * DIGIT + tail[5 * SUB:6 * SUB]
        if first:
            kept = jnp.zeros((4 * SUB, levels), F32)
        else:
            kept = before_ref[4 * SUB * g:4 * SUB * (g + 1), :]
        tails.append((tail[:4 * SUB].astype(BF), jnp.concatenate([low] * 4, axis=0), kept))
    for arrival in arrivals:
        arrival.wait()

    for g in range(groups):
        sources = slice(g * SUB, (g + 1) * SUB)
        extra, low, kept = tails[g]
        for i in range(count):
            def stack(row):
                start = g * held + row * SUB
                return [x_ref[start:start + SUB, c * levels:(c + 1) * levels] for c in range(4)]

            rows = jnp.concatenate([*stack(i), *stack(count + i), extra], axis=0)
            both = lax.dot_general(
                rows, jnp.concatenate(matrices(i), axis=0), (((1,), (1,)), ((), ())), preferred_element_type=F32
            )
            from_low, from_high = both[:4 * SUB, :levels], both[:, levels:]
            fold = first_fold + i
            mixed = jnp.where(low <= fold, from_low, from_high[:4 * SUB])
            kept = jnp.where(low == fold, from_high[8 * SUB:], kept)
            for row, value in ((i, mixed), (count + i, from_high[4 * SUB:8 * SUB])):
                value = value.astype(BF)
                for c in range(4):
                    y_ref[row * SUB:(row + 1) * SUB, c * levels:(c + 1) * levels] = value[c * SUB:(c + 1) * SUB]
        if height > 2 * count:
            y_ref[2 * count * SUB:height * SUB, :] = jnp.zeros(((height - 2 * count) * SUB, 4 * levels), BF)
        for r in range(0, height, SUB):
            back = turn(y_ref[r * SUB:(r + SUB) * SUB, :]).astype(BF)
            for c in range(4):
                z_ref[sources, c * height + r:c * height + r + SUB, :] = back[:, c * levels:(c + 1) * levels].reshape(
                    SUB, SUB, levels
                )
        if last:
            filled = jnp.concatenate([kept, jnp.zeros((12 * SUB, levels), F32)], axis=0).astype(BF)
            z_ref[sources, 4 * height:4 * height + SUB, :] = turn(filled).astype(BF).reshape(SUB, SUB, levels)
        else:
            after[0][4 * SUB * g:4 * SUB * (g + 1), :] = kept

    moves = [(c * height, c * plan.rows + row0, height) for c in range(4)]
    if last:
        moves.append((4 * height, 4 * plan.rows, SUB))
    departures = [
        pltpu.make_async_copy(z_ref.at[:, pl.ds(here, n), :], out_ref.at[:, pl.ds(there, n), :], out_sems.at[c])
        for c, (here, there, n) in enumerate(moves)
    ]
    for departure in departures:
        departure.start()
    for departure in departures:
        departure.wait()


def filter_rows(plan, at, info, received, near, far, before):
    levels = received.shape[2]
    count = plan.chunks[at][2]
    height = ceil_to(2 * count, SUB)
    last = at == len(plan.chunks) - 1
    smem, vmem = pl.BlockSpec(memory_space=pltpu.SMEM), pl.BlockSpec(memory_space=pltpu.VMEM)
    anywhere = pl.BlockSpec(memory_space=pl.ANY)
    out_shape = [jax.ShapeDtypeStruct(received.shape, BF)]
    if not last:
        out_shape.append(jax.ShapeDtypeStruct((4 * plan.group, levels), F32))
    return pl.pallas_call(
        functools.partial(filter_kernel, plan, at, levels),
        out_shape=out_shape,
        in_specs=[smem, vmem] + ([vmem, vmem, vmem, anywhere] if before else [anywhere, anywhere]),
        out_specs=[anywhere] + [vmem] * (len(out_shape) - 1),
        input_output_aliases={5: 0} if before else {},
        scratch_shapes=[
            pltpu.VMEM((2, count, levels, levels), BF),
            pltpu.VMEM((plan.group * height, 4 * levels), BF),
            pltpu.VMEM((height * SUB, 4 * levels), BF),
            pltpu.VMEM((plan.group, 4 * height + SUB, levels), BF),
            pltpu.SemaphoreType.DMA((2,)),
            pltpu.SemaphoreType.DMA((5,)),
        ],
        compiler_params=pltpu.CompilerParams(vmem_limit_bytes=20 * 1024 * 1024),
        cost_estimate=pl.CostEstimate(
            flops=2 * plan.group * 16 * count * levels * levels * 4,
            bytes_accessed=2 * 2 * received.size + 4 * count * levels * levels,
            transcendentals=0,
        ),
        name="filter_rows",
    )(info, received, near, far, *before)


def grid_kernel(plan, levels, latitudes, depth, level_cols, tile, info_ref, starts_ref, bands_ref, part_ref, *refs):
    tables, out_ref, held_tables = refs[:2], refs[2], refs[3:5]
    upper_ref, lower_ref, *grids, cut_ref, sems, out_sems = refs[5:]
    waves = bands_ref.shape[0]
    groups = 4 * levels // level_cols
    tiles = [slice(start, stop) for start, stop in zip(tile, tile[1:])]

    def copy(half, at):
        rows = tiles[at]
        return pltpu.make_async_copy(tables[half].at[rows], held_tables[half].at[rows], sems.at[half, at])

    for half in (1, 0):
        for at in range(len(tiles)):
            copy(half, at).start()

    base = 0
    for at, first, rows in plan.segments:
        for k in range(plan.group):
            for c in range(4):
                start = c * plan.rows + plan.chunks[at][0] + first
                cols = slice(c * levels, (c + 1) * levels)
                value = part_ref[k, start:start + rows, :]
                upper_ref[base + k * rows:base + (k + 1) * rows, cols] = value
                if base < plan.widths[1]:
                    lower_ref[base + k * rows:base + (k + 1) * rows, cols] = value
        base += plan.group * rows

    extra = part_ref[info_ref[0], 4 * plan.rows:4 * plan.rows + SUB, :]
    base = info_ref[1] // SUB * SUB
    place = pl.ds(pl.multiple_of(base, SUB), SUB)
    here = lax.broadcasted_iota(jnp.int32, (SUB, levels), 0) == info_ref[1] - base
    for c in range(4):
        cols = slice(c * levels, (c + 1) * levels)
        held = upper_ref[place, cols].astype(F32)
        lower_ref[place, cols] = jnp.where(here, extra[c:c + 1, :].astype(F32), held).astype(BF)

    def transform(half, at):
        copy(half, at).wait()
        rows = tiles[at]
        grids[half][rows, :] = jnp.dot(
            held_tables[half][rows, :], (upper_ref, lower_ref)[half][...], preferred_element_type=F32
        )

    def departure(half, w):
        messages = pl.ds(w * groups, groups)
        return pltpu.make_async_copy(cut_ref.at[messages, half], out_ref.at[messages, half], out_sems.at[half, w])

    def cut(half, w):
        place = lax.broadcasted_iota(jnp.int32, (8, levels), 0)
        start = starts_ref[w]
        base = start // 8 * 8
        offset = start - base
        front = place < 8 - offset

        def slab(at):
            rows = pl.ds(pl.multiple_of(base + at, 8), 8)
            held = [grids[half][rows, c * levels:(c + 1) * levels] for c in range(4)]
            return [pltpu.roll(part, (8 - offset) % 8, axis=0) for part in held]

        after = slab(0)
        done = []
        for r in range(0, depth, 8):
            now, after = after, slab(r + 8)
            inside = place < bands_ref[w] - r
            done.append([jnp.where(inside, jnp.where(front, *pair), 0.0) for pair in zip(now, after)])
            if len(done) == 2 or r + 8 == depth:
                first = r + 8 - 8 * len(done)
                for c, parts in enumerate(zip(*done)):
                    rows = jnp.concatenate(parts, axis=0).astype(BF)
                    for at in range(0, levels, level_cols):
                        message = w * groups + (c * levels + at) // level_cols
                        cut_ref[message, half, first:r + 8, :] = rows[:, at:at + level_cols]
                done = []
        departure(half, w).start()

    for at in range(len(tiles)):
        transform(1, at)
    for at in range(len(tiles)):
        transform(0, at)
        for w in range(at * waves // len(tiles), (at + 1) * waves // len(tiles)):
            cut(1, w)
    for w in range(waves):
        cut(0, w)
    for half in range(2):
        for w in range(waves):
            departure(half, w).wait()


def to_bands(plan, info, starts, bands, part, tables, depth, level_cols):
    latitudes = tables[0].shape[0]
    levels = part.shape[2]
    columns = 4 * levels
    tile = [0] + list(range(latitudes // 5, latitudes + 1, 2 * latitudes // 5))
    smem, vmem = pl.BlockSpec(memory_space=pltpu.SMEM), pl.BlockSpec(memory_space=pltpu.VMEM)
    messages = bands.shape[0] * columns // level_cols
    grid = pltpu.VMEM((ceil_to(latitudes + depth, 8) + 8, columns), F32)
    held = 2 * (latitudes + columns) * sum(plan.widths) + 8 * (latitudes + depth) * columns
    held += 4 * messages * depth * ceil_to(level_cols, 128) + 2 * part.size
    limit = max(52 * 1024 * 1024, held + 4 * 1024 * 1024)
    return pl.pallas_call(
        functools.partial(grid_kernel, plan, levels, latitudes, depth, level_cols, tile),
        out_shape=jax.ShapeDtypeStruct((messages, 2, depth, level_cols), BF),
        in_specs=[smem, smem, smem, vmem] + [pl.BlockSpec(memory_space=pl.ANY)] * 2,
        out_specs=pl.BlockSpec(memory_space=pl.ANY),
        scratch_shapes=[
            pltpu.VMEM(tables[0].shape, BF),
            pltpu.VMEM(tables[1].shape, BF),
            pltpu.VMEM((plan.widths[0], columns), BF),
            pltpu.VMEM((plan.widths[1], columns), BF),
            grid,
            grid,
            pltpu.VMEM((messages, 2, depth, level_cols), BF),
            pltpu.SemaphoreType.DMA((2, len(tile) - 1)),
            pltpu.SemaphoreType.DMA((2, bands.shape[0])),
        ],
        compiler_params=pltpu.CompilerParams(vmem_limit_bytes=limit),
        cost_estimate=pl.CostEstimate(
            flops=2 * latitudes * sum(plan.widths) * columns,
            bytes_accessed=2 * latitudes * sum(plan.widths) + 4 * messages * depth * level_cols,
            transcendentals=0,
        ),
        name="grid_bands",
    )(info, starts, bands, part, *tables)


def per_device(control, covariance, legendre, pair_order, band_rows):
    axes = ("wave", "lev")
    waves, lev_count = lax.axis_size("wave"), lax.axis_size("lev")
    _, slots, columns = control.shape
    degrees, levels = slots - 1, columns // 4
    latitudes = legendre.shape[2]
    depth = 5 * latitudes // (4 * waves)
    level_cols = columns // lev_count
    plan = Plan(waves * lev_count, degrees)
    group, block = plan.group, plan.block
    me = lax.axis_index("wave") * lev_count + lax.axis_index("lev")
    is_high = (me >= group).astype(jnp.int32)
    lowest = pair_order[0]
    halves = [list(range(group)), list(range(group, 2 * group))]

    def exchange(rows):
        return lax.all_to_all(rows, axes, split_axis=0, concat_axis=0, tiled=True, axis_index_groups=halves)

    plane = group // 2
    whole = range(2 * group)
    far = [(d, (3 - d // plane) * plane + d % plane) for d in whole]
    near = [(d, d // plane * plane + plane - 1 - d % plane) for d in whole]
    far_blocks, near_blocks = [], []

    def swap_chunk(own):
        far_blocks.append(lax.ppermute(own, axes, far))
        near_blocks.append(lax.ppermute(own, axes, near))

    own = cast_blocks(plan, 0, covariance, is_high[None])
    own, control = lax.optimization_barrier((own, control))
    swap_chunk(own)

    def fold_block(rank):
        rank = jnp.where(is_high == 1, group - 1 - rank, rank)
        return rank // plane * plane + plane - 1 - rank % plane

    def slots_of(message, fold, folded, used):
        degree = fold_block(message) * block + fold
        upper = jnp.where(folded, degree - lowest, degrees - 1 - degree - lowest)
        upper = jnp.where(used & (upper >= 0), upper, -1)
        lower = jnp.where(used & folded & (degree <= lowest), degrees - degree, -1)
        return upper, lower

    upper, lower = slots_of(*plan.message_rows())
    sent = jnp.where(upper >= 0, upper, lower)
    packed = pack(plan, control[0], pair_order, sent[:, None])
    packed, legendre = lax.optimization_barrier((packed, legendre))
    received = exchange(packed)

    tables = make_tables(plan, legendre[0], slots_of(*plan.transform_rows()))
    for at in range(1, len(plan.chunks)):
        covariance, tables = lax.optimization_barrier((covariance, tables))
        swap_chunk(cast_blocks(plan, at, covariance, is_high[None]))

    info = jnp.stack([is_high, fold_block(me - group * is_high) * block])
    received, tables = lax.optimization_barrier((received, tables))
    before = ()
    for at, (near_block, far_block) in enumerate(zip(near_blocks, far_blocks)):
        result, *extras = filter_rows(plan, at, info, received, near_block, far_block, before)
        before = (*extras, result)
    filtered = exchange(result)

    extra_block = lowest // block
    extra_message = fold_block(extra_block)
    extra_row = plan.extra_row(extra_message, lowest - extra_block * block)
    where = jnp.stack([extra_message, extra_row])
    starts = jnp.cumsum(band_rows) - band_rows
    outgoing = to_bands(plan, where, starts, band_rows, filtered, tables, depth, level_cols)
    outgoing = outgoing.reshape(-1, depth, level_cols)
    return lax.all_to_all(outgoing, axes, split_axis=0, concat_axis=0, tiled=True)


def solution(mesh):
    return jax.shard_map(
        per_device,
        mesh=mesh,
        in_specs=(
            P(("wave", "lev"), None, None),
            P(("wave", "lev"), None, None),
            P(("wave", "lev"), None, None),
            P(("wave", "lev")),
            P(),
        ),
        out_specs=P(None, "wave", "lev"),
        check_vma=False,
    )
```
